32 devices in a mesh: row: 8 (over z, core), col: 4 (over y, x).
Axes of the slice: x: 2, y: 2, z: 4, core: 2. Of those that a mesh axis runs over, the one named last changes fastest.
Arguments:
- eigvec: float32 [16384, 8192], P('row', 'col'), may hold values from -6 to 6
- slots: float32 [4, 16384, 256], P('col', 'row'), may hold values from -0.046875 to 0.046875
- roots: int32 [3], replicated, may hold values from 0 to 3, as said below
- tfac: float32 [3, 256, 256], replicated, as said below
Outputs:
- transformed: float32 [16384, 8192], P('row', 'col')
The draws below stay inside these ranges and needn't reach their ends.
Inputs may be any that keep to these rules, and one draw needn't show every extreme that they name: The panels lie in consecutive grid columns, roots[k] = (roots[0] + k) mod 4; roots[0] is one of the last two grid columns, so the panels always wrap past the last grid column. tfac[k] is upper triangular with a diagonal between 1 and 2.
All inputs are finite; a program needn't handle non-finite values.
Results may differ from the reference program's by a relative error of at most 0.00013.
Values sent between devices are 32-bit elements; how exact they have to be, the bound alone decides.
No kernel may reach another device: no remote copies, remote signals or barrier semaphores. Data moves between devices by JAX's collectives and lax.ppermute only.
A program may use at most 128 MiB of HBM per device.

```python
import jax
import jax.numpy as jnp
from jax import lax

NB = 256
NE = 8192
PANELS = 3
ROWS = 16384
GRID_COLS = 4


def draw_roots(key, part):
    start = jax.random.randint(key, (), GRID_COLS - 2, GRID_COLS)
    return ((start + jnp.arange(PANELS)) % GRID_COLS).astype(jnp.int32)


def draw_tfac(key, part):
    key_diag, key_off = jax.random.split(jax.random.fold_in(key, 17))
    diag = jax.random.uniform(key_diag, (PANELS, NB), jnp.float32, 1.0, 2.0)
    off = jax.random.normal(key_off, (PANELS, NB, NB), jnp.float32) * (0.6 / jnp.sqrt(NB * 1.0))
    upper = jnp.triu(off, 1)
    return upper + diag[:, :, None] * jnp.eye(NB, dtype=jnp.float32)[None]


def steps_of(own_key, shape, cuts, least, top_value):
    gain, own = 1.0, jax.random.fold_in(own_key, 6)
    for dim, blocks in cuts:
        steps = jnp.exp(jax.random.uniform(jax.random.fold_in(own, dim), (blocks,), jnp.float32, least / len(cuts), top_value / len(cuts)))
        gain = gain * jnp.repeat(steps, shape[dim] // blocks).reshape([-1 if axis == dim else 1 for axis in range(len(shape))])
    return gain


def bell_draw(key, shape, deviation, bound, shards=(), held_as=jnp.bfloat16):
    drawn = jax.random.normal(key, shape, jnp.float32) * deviation
    if len(shards) > 0:
        drawn = steps_of(key, shape, shards, -0.22, 0.18) * drawn
    return jnp.clip(drawn, min=-bound, max=bound).astype(held_as)


def setup_inputs(seed: int = 0) -> dict:
    seeds = jax.random.split(jax.random.key(seed), 5)
    return {
        "eigvec": bell_draw(seeds[0], (ROWS, NE), 1.0, 6.0, ((0, 8), (1, 4)), jnp.float32),
        "slots": bell_draw(seeds[1], (GRID_COLS, ROWS, NB), ROWS ** -0.5, 0.046875, ((0, 4), (1, 8)), jnp.float32),
        "roots": draw_roots(jax.random.fold_in(seeds[4], 71), 0),
        "tfac": draw_tfac(jax.random.fold_in(seeds[4], 71), 0),
    }


def reference(eigvec, slots, roots, tfac):
    current = eigvec
    for index in range(PANELS):
        panel = slots[roots[index]]
        inner = jnp.dot(panel.T, current, precision=lax.Precision.HIGHEST, preferred_element_type=jnp.float32)
        scaled = jnp.dot(tfac[index], inner, precision=lax.Precision.HIGHEST, preferred_element_type=jnp.float32)
        current = current - jnp.dot(panel, scaled, precision=lax.Precision.HIGHEST, preferred_element_type=jnp.float32)
    return current
```

```python
import functools

import jax
import jax.numpy as jnp
from jax import lax
from jax.experimental import pallas as pl
from jax.experimental.pallas import tpu as pltpu
from jax.sharding import PartitionSpec as P

PANELS = 3
BLOCK = 512
VMEM = 40 * 1024 * 1024
F32 = jnp.float32
BF16 = jnp.bfloat16


def split(value):
    high = value.astype(BF16)
    return high, (value - high.astype(F32)).astype(BF16)


def dot(left, right):
    return jnp.dot(left, right, preferred_element_type=F32)


def dot_three(left, right):
    left_high, left_low = split(left)
    right_high, right_low = split(right)
    return dot(left_high, right_high) + (dot(left_high, right_low) + dot(left_low, right_high))


def params():
    return pltpu.CompilerParams(vmem_limit_bytes=VMEM)


def cost(flops, count):
    return pl.CostEstimate(flops=flops, bytes_accessed=count, transcendentals=0)


def split_kernel(x_ref, high_ref, low_ref):
    high_ref[...], low_ref[...] = split(x_ref[...])


def split_array(x):
    rows, columns = x.shape
    step = min(rows, 256)
    spec = pl.BlockSpec((step, columns), lambda i: (i, 0))
    return pl.pallas_call(
        split_kernel,
        grid=(rows // step,),
        in_specs=[spec],
        out_specs=[spec, spec],
        out_shape=[jax.ShapeDtypeStruct(x.shape, BF16)] * 2,
        compiler_params=params(),
        cost_estimate=cost(rows * columns * 4, rows * columns * 8),
        name="split_x",
    )(x)


def prepare_kernel(keep_ref, send_ref, high_ref, low_ref, flipped_ref):
    both = jnp.concatenate([keep_ref[...], send_ref[...]], axis=1)
    high_ref[...], low_ref[...] = split(both)
    high, low = split(both.T)
    width = both.shape[1]
    flipped_ref[:width, :] = high
    flipped_ref[width:, :] = low


def prepare(keep, send):
    rows, half = keep.shape
    step = min(rows, 512)
    half_spec = pl.BlockSpec((step, half), lambda i: (i, 0))
    spec = pl.BlockSpec((step, 2 * half), lambda i: (i, 0))
    return pl.pallas_call(
        prepare_kernel,
        grid=(rows // step,),
        in_specs=[half_spec, half_spec],
        out_specs=[spec, spec, pl.BlockSpec((4 * half, step), lambda i: (0, i))],
        out_shape=[
            jax.ShapeDtypeStruct((rows, 2 * half), BF16),
            jax.ShapeDtypeStruct((rows, 2 * half), BF16),
            jax.ShapeDtypeStruct((4 * half, rows), BF16),
        ],
        compiler_params=params(),
        cost_estimate=cost(rows * half * 8, rows * half * 24),
        name="prepare_panel",
    )(keep, send)


def products_kernel(flipped_ref, high_ref, low_ref, keep_ref, send_ref):
    width = flipped_ref.shape[0] // 2
    with_high = dot(flipped_ref[...], high_ref[...])
    with_low = dot(flipped_ref[:width, :], low_ref[...])
    total = with_high[:width] + (with_high[width:] + with_low)
    keep_ref[...] = total[: width // 2]
    send_ref[...] = total[width // 2 :]


def products(flipped, high, low, block, width):
    rows = high.shape[0]
    half = flipped.shape[0] // 4
    step = min(width, 256)
    steps = width // step
    x_spec = pl.BlockSpec((rows, step), lambda i: (0, block * steps + i))
    out_spec = pl.BlockSpec((half, step), lambda i: (0, i))
    return pl.pallas_call(
        products_kernel,
        grid=(steps,),
        in_specs=[pl.BlockSpec((4 * half, rows), lambda i: (0, 0)), x_spec, x_spec],
        out_specs=[out_spec, out_spec],
        out_shape=[jax.ShapeDtypeStruct((half, width), F32)] * 2,
        compiler_params=params(),
        cost_estimate=cost(2 * 6 * half * rows * width, rows * width * 4 + 8 * half * rows),
        name="products",
    )(flipped, high, low)


def update_kernel(place_ref, *refs):
    sums = refs[:6]
    tfac_ref, gram_ref = refs[6:8]
    high_refs, low_refs = refs[8:11], refs[11:14]
    x_ref = refs[14]
    out_ref, w_ref, y_ref, y_high_ref, y_low_ref = refs[-5:]
    half = sums[0].shape[0]
    width = 2 * half

    @pl.when(pl.program_id(0) == 0)
    def _():
        for index, piece in enumerate(sums):
            start = pl.multiple_of(place_ref[index] * half, half)
            w_ref[pl.ds(start, half), :] = piece[...]
        first = dot_three(tfac_ref[0], w_ref[:width, :])
        y_ref[:width, :] = first
        second = dot_three(tfac_ref[1], w_ref[width : 2 * width, :] - dot_three(gram_ref[0], first))
        y_ref[width : 2 * width, :] = second
        third = w_ref[2 * width :, :] - dot_three(gram_ref[1], first) - dot_three(gram_ref[2], second)
        y_ref[2 * width :, :] = dot_three(tfac_ref[2], third)
        for index in range(6):
            start = pl.multiple_of(place_ref[index] * half, half)
            high, low = split(y_ref[pl.ds(start, half), :])
            y_high_ref[index * half : (index + 1) * half, :] = high
            y_low_ref[index * half : (index + 1) * half, :] = low

    high = jnp.concatenate([ref[...] for ref in high_refs], axis=1)
    low = jnp.concatenate([ref[...] for ref in low_refs], axis=1)
    change = dot(high, y_high_ref[...]) + (dot(high, y_low_ref[...]) + dot(low, y_high_ref[...]))
    out_ref[...] = x_ref[...] - change


def update(place, sums, tfac, grams, highs, lows, x, out, block):
    rows, columns = x.shape
    half, width = sums[0].shape
    step = min(rows, 512)
    whole = lambda *shape: pl.BlockSpec(shape, lambda i, place: (0,) * len(shape))
    panel_spec = pl.BlockSpec((step, 2 * half), lambda i, place: (i, 0))
    block_spec = pl.BlockSpec((step, width), lambda i, place: (i, block))
    operands = [place, *sums, tfac, grams, *highs, *lows, x]
    in_specs = (
        [whole(half, width)] * 6
        + [whole(3, 2 * half, 2 * half)] * 2
        + [panel_spec] * 6
        + [block_spec]
    )
    aliases = {}
    if out is not None:
        aliases = {len(operands): 0}
        operands.append(out)
        in_specs.append(pl.BlockSpec(memory_space=pl.ANY))
    return pl.pallas_call(
        update_kernel,
        grid_spec=pltpu.PrefetchScalarGridSpec(
            num_scalar_prefetch=1,
            grid=(rows // step,),
            in_specs=in_specs,
            out_specs=block_spec,
            scratch_shapes=[
                pltpu.VMEM((6 * half, width), F32),
                pltpu.VMEM((6 * half, width), F32),
                pltpu.VMEM((6 * half, width), BF16),
                pltpu.VMEM((6 * half, width), BF16),
            ],
        ),
        out_shape=jax.ShapeDtypeStruct(x.shape, F32),
        input_output_aliases=aliases,
        compiler_params=params(),
        cost_estimate=cost(2 * 18 * half * rows * width, rows * width * 8 + rows * half * 24),
        name="update",
    )(*operands)


def pairs_of(count, step):
    return [(index, index ^ step) for index in range(count)]


def swap_cores(value):
    return lax.ppermute(value, "row", pairs_of(lax.axis_size("row"), 1))


def both_cores(chip_pairs):
    return [(2 * a + core, 2 * b + core) for a, b in chip_pairs for core in range(2)]


def sum_over_rows(keep, send):
    chips = lax.axis_size("row") // 2
    chip = lax.axis_index("row") // 2
    total = keep + swap_cores(send)
    for hop in range(chips // 2 - 1):
        pairs = [(hop, hop + 1), (chips - 1 - hop, chips - 2 - hop)]
        total = total + lax.ppermute(total, "row", both_cores(pairs))
    middle = [(chips // 2 - 1, chips // 2), (chips // 2, chips // 2 - 1)]
    total = total + lax.ppermute(total, "row", both_cores(middle))
    for hop in reversed(range(chips // 2 - 1)):
        pairs = [(hop + 1, hop), (chips - 2 - hop, chips - 1 - hop)]
        arrived = lax.ppermute(total, "row", both_cores(pairs))
        total = jnp.where((chip == hop) | (chip == chips - 1 - hop), arrived, total)
    return total, swap_cores(total)


def pick(index, *cases):
    return lax.select_n(index, *cases)


def fetch_square(slot, roots):
    half = slot.shape[1] // 2
    me = lax.axis_index("col")
    along = lambda value, step: lax.ppermute(value, "col", pairs_of(4, step))
    own = [slot[:, :half], slot[:, half:]]
    near, far = [], []
    for piece in own:
        near.append(along(piece, 1))
        far.append(along(piece, 2))
    cross = [along(far[0], 1), along(near[1], 2)]
    spare = (roots[0] + 3) % 4
    case = me ^ spare
    rounds = [
        (pick(case, near[0], own[0], own[0], own[0]), pick(case, far[0], own[1], own[1], own[1])),
        (pick(case, near[1], far[0], near[0], near[0]), pick(case, far[1], far[1], near[1], far[0])),
        (pick(case, cross[0], cross[0], cross[0], near[1]), pick(case, cross[1], cross[1], cross[1], far[1])),
    ]
    slots = jnp.array([[1, 2, 1, 2, 3, 3], [0, 0, 2, 2, 3, 3], [0, 0, 1, 1, 3, 3], [0, 0, 1, 2, 1, 2]], jnp.int32)
    halves = jnp.array([[0, 0, 1, 1, 0, 1], [0, 1, 0, 1, 0, 1], [0, 1, 0, 1, 0, 1], [0, 1, 0, 0, 1, 1]], jnp.int32)
    panel = ((slots[case] ^ me) - roots[0]) % 4
    places = panel * 2 + halves[case]
    wholes = [jnp.concatenate(pieces, axis=1) for pieces in (own, near, far, cross)]
    panels = [pick(roots[index] ^ me, *wholes) for index in range(PANELS)]
    return rounds, places, panels


def fetch_any(slot, roots):
    half = slot.shape[1] // 2
    me = lax.axis_index("col")
    panels = [lax.psum(jnp.where(me == roots[index], slot, jnp.zeros_like(slot)), "col") for index in range(PANELS)]
    rounds = [(panel[:, :half], panel[:, half:]) for panel in panels]
    return rounds, jnp.arange(2 * PANELS, dtype=jnp.int32), panels


def gram(left, right):
    return lax.dot_general(
        left, right, (((0,), (0,)), ((), ())), precision=lax.Precision.HIGH, preferred_element_type=F32
    )


def shards(eigvec, slots, roots, tfac):
    columns = eigvec.shape[1]
    width = min(columns, BLOCK)
    fetch = fetch_square if lax.axis_size("col") == 4 else fetch_any
    rounds, places, panels = fetch(slots[0], roots)
    core = lax.axis_index("row") % 2
    places = jnp.where(core == 0, places, places.reshape(PANELS, 2)[:, ::-1].reshape(-1))
    x_high, x_low = split_array(eigvec)
    highs, lows, sums = [], [], []
    for first, second in rounds:
        keep = jnp.where(core == 0, first, second)
        send = jnp.where(core == 0, second, first)
        high, low, flipped = prepare(keep, send)
        highs.append(high)
        lows.append(low)
        sums.append([
            sum_over_rows(*products(flipped, x_high, x_low, block, width)) for block in range(columns // width)
        ])
    grams = jnp.stack([gram(panels[1], panels[0]), gram(panels[2], panels[0]), gram(panels[2], panels[1])])
    grams = lax.psum(grams, "row")
    out = None
    for block in range(columns // width):
        pieces = [piece for index in range(PANELS) for piece in sums[index][block]]
        out = update(places, pieces, tfac, grams, highs, lows, eigvec, out, block)
    return out


def solution(mesh):
    in_specs = (P("row", "col"), P("col", "row", None), P(), P())
    out_specs = P("row", "col")
    return jax.shard_map(shards, mesh=mesh, in_specs=in_specs, out_specs=out_specs, check_vma=False)
```

```python
import functools

import jax
import jax.numpy as jnp
from jax import lax
from jax.experimental import pallas as pl
from jax.experimental.pallas import tpu as pltpu
from jax.sharding import PartitionSpec as P

PANELS = 3
BLOCK = 512
VMEM = 40 * 1024 * 1024
F32 = jnp.float32
BF16 = jnp.bfloat16
ANYWHERE = pl.BlockSpec(memory_space=pl.ANY)


def split(value):
    high = value.astype(BF16)
    return high, (value - high.astype(F32)).astype(BF16)


def dot(left, right):
    return jnp.dot(left, right, preferred_element_type=F32)


def dot_three(left, right):
    left_high, left_low = split(left)
    right_high, right_low = split(right)
    return dot(left_high, right_high) + (dot(left_high, right_low) + dot(left_low, right_high))


def params():
    return pltpu.CompilerParams(vmem_limit_bytes=VMEM)


def cost(flops, count):
    return pl.CostEstimate(flops=flops // 64, bytes_accessed=count // 64, transcendentals=0)


def split_kernel(x_ref, high_ref, low_ref):
    high_ref[...], low_ref[...] = split(x_ref[...])


def split_array(x):
    rows, columns = x.shape
    step = min(rows, 256)
    spec = pl.BlockSpec((step, columns), lambda i: (i, 0))
    return pl.pallas_call(
        split_kernel,
        grid=(rows // step,),
        in_specs=[spec],
        out_specs=[spec, spec],
        out_shape=[jax.ShapeDtypeStruct(x.shape, BF16)] * 2,
        compiler_params=params(),
        cost_estimate=cost(rows * columns * 4, rows * columns * 8),
        name="split_x",
    )(x)


def prepare_kernel(keep_ref, send_ref, *refs):
    high_ref, low_ref, flipped_ref = refs[-3:]
    both = jnp.concatenate([keep_ref[...], send_ref[...]], axis=1)
    high_ref[...], low_ref[...] = split(both)
    high, low = split(both.T)
    width = both.shape[1]
    flipped_ref[:width, :] = high
    flipped_ref[width:, :] = low


def prepare(keep, send, after=()):
    rows, half = keep.shape
    step = min(rows, 512)
    half_spec = pl.BlockSpec((step, half), lambda i: (i, 0))
    spec = pl.BlockSpec((step, 2 * half), lambda i: (i, 0))
    return pl.pallas_call(
        prepare_kernel,
        grid=(rows // step,),
        in_specs=[half_spec, half_spec] + [ANYWHERE] * len(after),
        out_specs=[spec, spec, pl.BlockSpec((4 * half, step), lambda i: (0, i))],
        out_shape=[
            jax.ShapeDtypeStruct((rows, 2 * half), BF16),
            jax.ShapeDtypeStruct((rows, 2 * half), BF16),
            jax.ShapeDtypeStruct((4 * half, rows), BF16),
        ],
        compiler_params=params(),
        cost_estimate=cost(rows * half * 8, rows * half * 24),
        name="prepare_panel",
    )(keep, send, *after)


def products_kernel(flipped_ref, high_ref, low_ref, *refs):
    keep_ref, send_ref = refs[-2:]
    width = flipped_ref.shape[0] // 2
    with_high = dot(flipped_ref[...], high_ref[...])
    with_low = dot(flipped_ref[:width, :], low_ref[...])
    total = with_high[:width] + (with_high[width:] + with_low)
    keep_ref[...] = total[: width // 2]
    send_ref[...] = total[width // 2 :]


def products(flipped, high, low, block, width, after=()):
    rows = high.shape[0]
    half = flipped.shape[0] // 4
    step = min(width, 256)
    steps = width // step
    x_spec = pl.BlockSpec((rows, step), lambda i: (0, block * steps + i))
    out_spec = pl.BlockSpec((half, step), lambda i: (0, i))
    return pl.pallas_call(
        products_kernel,
        grid=(steps,),
        in_specs=[pl.BlockSpec((4 * half, rows), lambda i: (0, 0)), x_spec, x_spec]
        + [ANYWHERE] * len(after),
        out_specs=[out_spec, out_spec],
        out_shape=[jax.ShapeDtypeStruct((half, width), F32)] * 2,
        compiler_params=params(),
        cost_estimate=cost(2 * 6 * half * rows * width, rows * width * 4 + 8 * half * rows),
        name="products",
    )(flipped, high, low, *after)


def update_kernel(place_ref, *refs):
    sums = refs[:6]
    tfac_ref, gram_ref = refs[6:8]
    high_refs, low_refs = refs[8:11], refs[11:14]
    x_ref = refs[14]
    out_ref, w_ref, y_ref, y_high_ref, y_low_ref = refs[-5:]
    half = sums[0].shape[0]
    width = 2 * half

    @pl.when(pl.program_id(0) == 0)
    def _():
        for index, piece in enumerate(sums):
            start = pl.multiple_of(place_ref[index] * half, half)
            w_ref[pl.ds(start, half), :] = piece[...]
        first = dot_three(tfac_ref[0], w_ref[:width, :])
        y_ref[:width, :] = first
        second = dot_three(tfac_ref[1], w_ref[width : 2 * width, :] - dot_three(gram_ref[0], first))
        y_ref[width : 2 * width, :] = second
        third = w_ref[2 * width :, :] - dot_three(gram_ref[1], first) - dot_three(gram_ref[2], second)
        y_ref[2 * width :, :] = dot_three(tfac_ref[2], third)
        for index in range(6):
            start = pl.multiple_of(place_ref[index] * half, half)
            high, low = split(y_ref[pl.ds(start, half), :])
            y_high_ref[index * half : (index + 1) * half, :] = high
            y_low_ref[index * half : (index + 1) * half, :] = low

    high = jnp.concatenate([ref[...] for ref in high_refs], axis=1)
    low = jnp.concatenate([ref[...] for ref in low_refs], axis=1)
    change = dot(high, y_high_ref[...]) + (dot(high, y_low_ref[...]) + dot(low, y_high_ref[...]))
    out_ref[...] = x_ref[...] - change


def update(place, sums, tfac, grams, highs, lows, x, out, block, width):
    rows, columns = x.shape
    half = sums[0].shape[0]
    step = min(rows, 512)
    whole = lambda *shape: pl.BlockSpec(shape, lambda i, place: (0,) * len(shape))
    panel_spec = pl.BlockSpec((step, 2 * half), lambda i, place: (i, 0))
    block_spec = pl.BlockSpec((step, width), lambda i, place: (i, block))
    operands = [place, *sums, tfac, grams, *highs, *lows, x]
    in_specs = (
        [whole(half, width)] * 6
        + [whole(3, 2 * half, 2 * half)] * 2
        + [panel_spec] * 6
        + [block_spec]
    )
    aliases = {}
    if out is not None:
        aliases = {len(operands): 0}
        operands.append(out)
        in_specs.append(pl.BlockSpec(memory_space=pl.ANY))
    return pl.pallas_call(
        update_kernel,
        grid_spec=pltpu.PrefetchScalarGridSpec(
            num_scalar_prefetch=1,
            grid=(rows // step,),
            in_specs=in_specs,
            out_specs=block_spec,
            scratch_shapes=[
                pltpu.VMEM((6 * half, width), F32),
                pltpu.VMEM((6 * half, width), F32),
                pltpu.VMEM((6 * half, width), BF16),
                pltpu.VMEM((6 * half, width), BF16),
            ],
        ),
        out_shape=jax.ShapeDtypeStruct(x.shape, F32),
        input_output_aliases=aliases,
        compiler_params=params(),
        cost_estimate=cost(2 * 18 * half * rows * width, rows * width * 8 + rows * half * 24),
        name="update",
    )(*operands)


def pairs_of(count, step):
    return [(index, index ^ step) for index in range(count)]


def swap_cores(value):
    return lax.ppermute(value, "row", pairs_of(lax.axis_size("row"), 1))


def both_cores(chip_pairs):
    return [(2 * a + core, 2 * b + core) for a, b in chip_pairs for core in range(2)]


def sum_over_rows(keep, send):
    chips = lax.axis_size("row") // 2
    chip = lax.axis_index("row") // 2
    total = keep + swap_cores(send)
    for hop in range(chips // 2 - 1):
        pairs = [(hop, hop + 1), (chips - 1 - hop, chips - 2 - hop)]
        total = total + lax.ppermute(total, "row", both_cores(pairs))
    middle = [(chips // 2 - 1, chips // 2), (chips // 2, chips // 2 - 1)]
    total = total + lax.ppermute(total, "row", both_cores(middle))
    for hop in reversed(range(chips // 2 - 1)):
        pairs = [(hop + 1, hop), (chips - 2 - hop, chips - 1 - hop)]
        arrived = lax.ppermute(total, "row", both_cores(pairs))
        total = jnp.where((chip == hop) | (chip == chips - 1 - hop), arrived, total)
    return total, swap_cores(total)


def pick(index, *cases):
    return lax.select_n(index, *cases)


def fetch_square(slot, roots):
    half = slot.shape[1] // 2
    me = lax.axis_index("col")
    along = lambda value, step: lax.ppermute(value, "col", pairs_of(4, step))
    own = [slot[:, :half], slot[:, half:]]
    near, far = [], []
    for piece in own:
        near.append(along(piece, 1))
        far.append(along(piece, 2))
    cross = [along(far[0], 1), along(near[1], 2)]
    spare = (roots[0] + 3) % 4
    case = me ^ spare
    rounds = [
        (pick(case, near[0], own[0], own[0], own[0]), pick(case, far[0], own[1], own[1], own[1])),
        (pick(case, near[1], far[0], near[0], near[0]), pick(case, far[1], far[1], near[1], far[0])),
        (pick(case, cross[0], cross[0], cross[0], near[1]), pick(case, cross[1], cross[1], cross[1], far[1])),
    ]
    slots = jnp.array([[1, 2, 1, 2, 3, 3], [0, 0, 2, 2, 3, 3], [0, 0, 1, 1, 3, 3], [0, 0, 1, 2, 1, 2]], jnp.int32)
    halves = jnp.array([[0, 0, 1, 1, 0, 1], [0, 1, 0, 1, 0, 1], [0, 1, 0, 1, 0, 1], [0, 1, 0, 0, 1, 1]], jnp.int32)
    panel = ((slots[case] ^ me) - roots[0]) % 4
    places = panel * 2 + halves[case]
    later_of = jnp.array([[0, 1, 0, 0], [1, 0, 2, 2]], jnp.int32)[roots[0] - 2, me]
    earlier_of = jnp.array([[2, 2, 0, 1], [0, 0, 1, 0]], jnp.int32)[roots[0] - 2, me]
    later = [pick(later_of, own[h], near[h], far[h]) for h in range(2)]
    earlier = [pick(earlier_of, own[h], near[h], far[h]) for h in range(2)]
    holders = jnp.array([[3, 0, 1], [2, 3, 0]], jnp.int32)[roots[0] - 2]
    return rounds, places, later, earlier, holders


def fetch_any(slot, roots):
    half = slot.shape[1] // 2
    me = lax.axis_index("col")
    panels = [lax.psum(jnp.where(me == roots[index], slot, jnp.zeros_like(slot)), "col") for index in range(PANELS)]
    rounds = [(panel[:, :half], panel[:, half:]) for panel in panels]
    return rounds, jnp.arange(2 * PANELS, dtype=jnp.int32), panels


def gram(left, right):
    return lax.dot_general(
        left, right, (((0,), (0,)), ((), ())), precision=lax.Precision.HIGH, preferred_element_type=F32
    )


def exchange_kernel(step, ends_ref, *refs):
    names, refs = step, list(refs)
    use = dict(zip(names, refs))
    end = ends_ref[0] == 1
    if "acc" in use:
        use["acc"][...] = use["keep"][...] + use["swapped"][...]
    if "part" in use:
        columns = use["part"].shape[1]
        use["part"][...] = use["acc_before"][...] + use["outer"][:, :columns]
    if "total" in use:
        use["total"][...] = use["part_before"][...] + use["inner"][...]
    if "final" in use:
        columns = use["final"].shape[1]
        use["final"][...] = jnp.where(end, use["outer"][:, :columns], use["total_before"][...])
    if "out" in use:
        sources = [use[name] for name in ("acc", "total") if name in use]
        if len(sources) == 1:
            use["out"][...] = sources[0][...]
        else:
            both = min(source.shape[1] for source in sources)
            use["out"][:, :both] = jnp.where(end, sources[0][:, :both], sources[1][:, :both])
            for source in sources:
                if source.shape[1] > both:
                    use["out"][:, both:] = source[:, both:]


def exchange(ends, operands, shapes):
    names = list(operands) + list(shapes)
    in_vmem = pl.BlockSpec(memory_space=pltpu.VMEM)
    results = pl.pallas_call(
        functools.partial(exchange_kernel, names),
        in_specs=[pl.BlockSpec(memory_space=pltpu.SMEM)] + [in_vmem] * len(operands),
        out_specs=[in_vmem] * len(shapes),
        out_shape=[jax.ShapeDtypeStruct(shape, F32) for shape in shapes.values()],
        compiler_params=params(),
        cost_estimate=cost(0, 0),
        name="exchange",
    )(ends, *operands.values())
    return dict(zip(shapes, results))


def shards_square(eigvec, slot, roots, tfac):
    columns = eigvec.shape[1]
    width = columns // 2
    rounds, places, later, earlier, holders = fetch_square(slot, roots)
    chip, core = lax.axis_index("row") // 2, lax.axis_index("row") % 2
    ends = jnp.where((chip == 0) | (chip == 3), 1, 0).astype(jnp.int32).reshape(1)
    places = jnp.where(core == 0, places, places.reshape(PANELS, 2)[:, ::-1].reshape(-1))
    ordered = lambda pair: (jnp.where(core == 0, *pair), jnp.where(core == 0, *pair[::-1]))
    x_high, x_low = split_array(eigvec)
    chunks = [(index, block) for index in range(PANELS) for block in range(columns // width)]
    count = len(chunks)
    gram_chunk = 3
    prepared, keep, swapped, sizes = {}, {}, {}, {}

    def start(number, after):
        index, block = chunks[number]
        if index not in prepared:
            prepared[index] = prepare(*ordered(rounds[index]), after)
        mine, other = products(prepared[index][2], x_high, x_low, block, width, after)
        if number == gram_chunk:
            flipped = prepare(*ordered(later), after)[2]
            high, low, _ = prepare(*earlier, after)
            extra = products(flipped, high, low, 0, high.shape[1])
            mine = jnp.concatenate([mine, extra[0]], axis=1)
            other = jnp.concatenate([other, extra[1]], axis=1)
        keep[number], swapped[number], sizes[number] = mine, swap_cores(other), mine.shape

    outer_pairs = both_cores([(0, 1), (1, 0), (2, 3), (3, 2)])
    inner_pairs = both_cores([(1, 2), (2, 1)])
    acc, part, total, outer, inner, sums = {}, {}, {}, {}, {}, {}
    grams, out = None, None
    start(0, ())
    for step in range(count + 3):
        operands, shapes = {}, {}
        if step < count:
            operands["keep"], operands["swapped"] = keep[step], swapped[step]
            shapes["acc"] = sizes[step]
        if step - 1 in outer:
            operands["outer"] = outer[step - 1]
        if 0 <= step - 1 < count:
            operands["acc_before"] = acc[step - 1]
            shapes["part"] = sizes[step - 1]
        if 0 <= step - 2 < count:
            operands["part_before"], operands["inner"] = part[step - 2], inner[step - 1]
            shapes["total"] = sizes[step - 2]
        if 0 <= step - 3 < count:
            operands["total_before"] = total[step - 3]
            shapes["final"] = sizes[step - 3]
        sent = [shapes[name] for name in ("acc", "total") if name in shapes]
        if sent:
            shapes["out"] = max(sent, key=lambda shape: shape[1])
        results = exchange(ends, operands, shapes)
        if "out" in results:
            outer[step] = lax.ppermute(results["out"], "row", outer_pairs)
        if "acc" in results:
            acc[step] = results["acc"]
        if "part" in results:
            part[step - 1] = results["part"]
            inner[step] = lax.ppermute(results["part"], "row", inner_pairs)
        if "total" in results:
            total[step - 2] = results["total"]
        if step + 1 < count:
            start(step + 1, [next(iter(results.values()))])
        if "final" in results:
            done = step - 3
            own, other = results["final"], swap_cores(results["final"])
            if done == gram_chunk:
                pair = ordered((own[:, width:], other[:, width:]))
                gathered = lax.all_gather(jnp.concatenate(pair, axis=0), "col")
                grams = gathered[holders]
            sums[chunks[done]] = (own, other)
            index, block = chunks[done]
            if index == PANELS - 1:
                pieces = [piece for panel in range(PANELS) for piece in sums[panel, block]]
                highs, lows = zip(*[prepared[panel][:2] for panel in range(PANELS)])
                out = update(places, pieces, tfac, grams, highs, lows, eigvec, out, block, width)
    return out


def shards(eigvec, slots, roots, tfac):
    if lax.axis_size("col") == 4 and lax.axis_size("row") == 8:
        return shards_square(eigvec, slots[0], roots, tfac)
    columns = eigvec.shape[1]
    width = min(columns, BLOCK)
    rounds, places, panels = fetch_any(slots[0], roots)
    core = lax.axis_index("row") % 2
    places = jnp.where(core == 0, places, places.reshape(PANELS, 2)[:, ::-1].reshape(-1))
    x_high, x_low = split_array(eigvec)
    highs, lows, sums = [], [], []
    for first, second in rounds:
        keep = jnp.where(core == 0, first, second)
        send = jnp.where(core == 0, second, first)
        high, low, flipped = prepare(keep, send)
        highs.append(high)
        lows.append(low)
        sums.append([
            sum_over_rows(*products(flipped, x_high, x_low, block, width)) for block in range(columns // width)
        ])
    grams = jnp.stack([gram(panels[1], panels[0]), gram(panels[2], panels[0]), gram(panels[2], panels[1])])
    grams = lax.psum(grams, "row")
    out = None
    for block in range(columns // width):
        pieces = [piece for index in range(PANELS) for piece in sums[index][block]]
        out = update(places, pieces, tfac, grams, highs, lows, eigvec, out, block, width)
    return out


def solution(mesh):
    in_specs = (P("row", "col"), P("col", "row", None), P(), P())
    out_specs = P("row", "col")
    return jax.shard_map(shards, mesh=mesh, in_specs=in_specs, out_specs=out_specs, check_vma=False)
```

```python
import functools

import jax
import jax.numpy as jnp
from jax import lax
from jax.experimental import pallas as pl
from jax.experimental.pallas import tpu as pltpu
from jax.sharding import PartitionSpec as P

PANELS = 3
BLOCK = 512
LAG = 1
PIECE = 512
VMEM = 54 * 1024 * 1024
F32 = jnp.float32
BF16 = jnp.bfloat16
ANYWHERE = pl.BlockSpec(memory_space=pl.ANY)


def split(value):
    high = value.astype(BF16)
    return high, (value - high.astype(F32)).astype(BF16)


def dot(left, right):
    return jnp.dot(left, right, preferred_element_type=F32)


def dot_three(left, right):
    left_high, left_low = split(left)
    right_high, right_low = split(right)
    return dot(left_high, right_high) + (dot(left_high, right_low) + dot(left_low, right_high))


def params():
    return pltpu.CompilerParams(vmem_limit_bytes=VMEM)


def cost(flops, count):
    return pl.CostEstimate(flops=flops // 64, bytes_accessed=count // 64, transcendentals=0)


def split_kernel(x_ref, high_ref, low_ref):
    high_ref[...], low_ref[...] = split(x_ref[...])


def split_array(x):
    rows, columns = x.shape
    step = min(rows, 256)
    spec = pl.BlockSpec((step, columns), lambda i: (i, 0))
    return pl.pallas_call(
        split_kernel,
        grid=(rows // step,),
        in_specs=[spec],
        out_specs=[spec, spec],
        out_shape=[jax.ShapeDtypeStruct(x.shape, BF16)] * 2,
        compiler_params=params(),
        cost_estimate=cost(rows * columns * 4, rows * columns * 8),
        name="split_x",
    )(x)


def prepare_kernel(keep_ref, send_ref, *refs):
    high_ref, low_ref, flipped_ref = refs[-3:]
    both = jnp.concatenate([keep_ref[...], send_ref[...]], axis=1)
    high_ref[...], low_ref[...] = split(both)
    high, low = split(both.T)
    width = both.shape[1]
    flipped_ref[:width, :] = high
    flipped_ref[width:, :] = low


def prepare(keep, send, after=()):
    rows, half = keep.shape
    step = min(rows, 512)
    half_spec = pl.BlockSpec((step, half), lambda i: (i, 0))
    spec = pl.BlockSpec((step, 2 * half), lambda i: (i, 0))
    return pl.pallas_call(
        prepare_kernel,
        grid=(rows // step,),
        in_specs=[half_spec, half_spec] + [ANYWHERE] * len(after),
        out_specs=[spec, spec, pl.BlockSpec((4 * half, step), lambda i: (0, i))],
        out_shape=[
            jax.ShapeDtypeStruct((rows, 2 * half), BF16),
            jax.ShapeDtypeStruct((rows, 2 * half), BF16),
            jax.ShapeDtypeStruct((4 * half, rows), BF16),
        ],
        compiler_params=params(),
        cost_estimate=cost(rows * half * 8, rows * half * 24),
        name="prepare_panel",
    )(keep, send, *after)


def choose_kernel(outputs, count, which_ref, *refs):
    cases, outs, (panel_ref, sem) = refs[:count], refs[-2 - len(outputs) : -2], refs[-2:]
    half = cases[0].shape[1]
    for side in range(2):
        for index, case in enumerate(cases):

            @pl.when(which_ref[side] == index)
            def _(case=case, side=side):
                copy = pltpu.make_async_copy(case, panel_ref.at[:, side * half : (side + 1) * half], sem)
                copy.start()
                copy.wait()

    use = dict(zip(outputs, outs))
    rows, width = panel_ref.shape
    step = min(rows, 256)
    for start in range(0, rows, step):
        here = slice(start, start + step)
        value = panel_ref[here, :]
        high, low = split(value)
        if "high" in use:
            use["high"][here, :] = high
            use["low"][here, :] = low
        if "flipped" in use:
            high, low = split(value.T)
            use["flipped"][:width, here] = high
            use["flipped"][width:, here] = low


def choose(cases, which, outputs, after=()):
    rows, half = cases[0].shape
    shapes = {"high": (rows, 2 * half), "low": (rows, 2 * half), "flipped": (4 * half, rows)}
    in_vmem = pl.BlockSpec(memory_space=pltpu.VMEM)
    return pl.pallas_call(
        functools.partial(choose_kernel, outputs, len(cases)),
        in_specs=[pl.BlockSpec(memory_space=pltpu.SMEM)] + [ANYWHERE] * (len(cases) + len(after)),
        out_specs=[in_vmem] * len(outputs),
        out_shape=[jax.ShapeDtypeStruct(shapes[name], BF16) for name in outputs],
        scratch_shapes=[pltpu.VMEM((rows, 2 * half), F32), pltpu.SemaphoreType.DMA],
        compiler_params=params(),
        cost_estimate=cost(rows * half * 8, rows * half * 24),
        name="choose_panel",
    )(which, *cases, *after)


def products_kernel(flipped_ref, high_ref, low_ref, *refs):
    keep_ref, send_ref = refs[-2:]
    width = flipped_ref.shape[0] // 2
    with_high = dot(flipped_ref[...], high_ref[...])
    with_low = dot(flipped_ref[:width, :], low_ref[...])
    total = with_high[:width] + (with_high[width:] + with_low)
    keep_ref[...] = total[: width // 2]
    send_ref[...] = total[width // 2 :]


def products(flipped, high, low, block, width, after=()):
    rows = high.shape[0]
    half = flipped.shape[0] // 4
    step = min(width, 256)
    steps = width // step
    x_spec = pl.BlockSpec((rows, step), lambda i: (0, block * steps + i))
    out_spec = pl.BlockSpec((half, step), lambda i: (0, i))
    return pl.pallas_call(
        products_kernel,
        grid=(steps,),
        in_specs=[pl.BlockSpec((4 * half, rows), lambda i: (0, 0)), x_spec, x_spec]
        + [ANYWHERE] * len(after),
        out_specs=[out_spec, out_spec],
        out_shape=[jax.ShapeDtypeStruct((half, width), F32)] * 2,
        compiler_params=params(),
        cost_estimate=cost(2 * 6 * half * rows * width, rows * width * 4 + 8 * half * rows),
        name="products",
    )(flipped, high, low, *after)


def update_kernel(place_ref, *refs):
    sums = refs[:6]
    tfac_ref, gram_ref = refs[6:8]
    high_refs, low_refs = refs[8:11], refs[11:14]
    x_ref = refs[14]
    out_ref, w_ref, y_ref, y_high_ref, y_low_ref = refs[-5:]
    half = sums[0].shape[0]
    width = 2 * half

    @pl.when(pl.program_id(0) == 0)
    def _():
        for index, piece in enumerate(sums):
            start = pl.multiple_of(place_ref[index] * half, half)
            w_ref[pl.ds(start, half), :] = piece[...]
        first = dot_three(tfac_ref[0], w_ref[:width, :])
        y_ref[:width, :] = first
        second = dot_three(tfac_ref[1], w_ref[width : 2 * width, :] - dot_three(gram_ref[0], first))
        y_ref[width : 2 * width, :] = second
        third = w_ref[2 * width :, :] - dot_three(gram_ref[1], first) - dot_three(gram_ref[2], second)
        y_ref[2 * width :, :] = dot_three(tfac_ref[2], third)
        for index in range(6):
            start = pl.multiple_of(place_ref[index] * half, half)
            high, low = split(y_ref[pl.ds(start, half), :])
            y_high_ref[index * half : (index + 1) * half, :] = high
            y_low_ref[index * half : (index + 1) * half, :] = low

    high = jnp.concatenate([ref[...] for ref in high_refs], axis=1)
    low = jnp.concatenate([ref[...] for ref in low_refs], axis=1)
    change = dot(high, y_high_ref[...]) + (dot(high, y_low_ref[...]) + dot(low, y_high_ref[...]))
    out_ref[...] = x_ref[...] - change


def update(place, sums, tfac, grams, highs, lows, x, out, block, width):
    rows, columns = x.shape
    half = sums[0].shape[0]
    step = min(rows, 512)
    whole = lambda *shape: pl.BlockSpec(shape, lambda i, place: (0,) * len(shape))
    panel_spec = pl.BlockSpec((step, 2 * half), lambda i, place: (i, 0))
    block_spec = pl.BlockSpec((step, width), lambda i, place: (i, block))
    operands = [place, *sums, tfac, grams, *highs, *lows, x]
    in_specs = (
        [whole(half, width)] * 6
        + [whole(3, 2 * half, 2 * half)] * 2
        + [panel_spec] * 6
        + [block_spec]
    )
    aliases = {}
    if out is not None:
        aliases = {len(operands): 0}
        operands.append(out)
        in_specs.append(pl.BlockSpec(memory_space=pl.ANY))
    return pl.pallas_call(
        update_kernel,
        grid_spec=pltpu.PrefetchScalarGridSpec(
            num_scalar_prefetch=1,
            grid=(rows // step,),
            in_specs=in_specs,
            out_specs=block_spec,
            scratch_shapes=[
                pltpu.VMEM((6 * half, width), F32),
                pltpu.VMEM((6 * half, width), F32),
                pltpu.VMEM((6 * half, width), BF16),
                pltpu.VMEM((6 * half, width), BF16),
            ],
        ),
        out_shape=jax.ShapeDtypeStruct(x.shape, F32),
        input_output_aliases=aliases,
        compiler_params=params(),
        cost_estimate=cost(2 * 18 * half * rows * width, rows * width * 8 + rows * half * 24),
        name="update",
    )(*operands)


def pairs_of(count, step):
    return [(index, index ^ step) for index in range(count)]


def swap_cores(value):
    return lax.ppermute(value, "row", pairs_of(lax.axis_size("row"), 1))


def both_cores(chip_pairs):
    return [(2 * a + core, 2 * b + core) for a, b in chip_pairs for core in range(2)]


def sum_over_rows(keep, send):
    chips = lax.axis_size("row") // 2
    chip = lax.axis_index("row") // 2
    total = keep + swap_cores(send)
    for hop in range(chips // 2 - 1):
        pairs = [(hop, hop + 1), (chips - 1 - hop, chips - 2 - hop)]
        total = total + lax.ppermute(total, "row", both_cores(pairs))
    middle = [(chips // 2 - 1, chips // 2), (chips // 2, chips // 2 - 1)]
    total = total + lax.ppermute(total, "row", both_cores(middle))
    for hop in reversed(range(chips // 2 - 1)):
        pairs = [(hop + 1, hop), (chips - 2 - hop, chips - 1 - hop)]
        arrived = lax.ppermute(total, "row", both_cores(pairs))
        total = jnp.where((chip == hop) | (chip == chips - 1 - hop), arrived, total)
    return total, swap_cores(total)


def pick(index, *cases):
    return lax.select_n(index, *cases)


def fetch_square(slot, roots):
    half = slot.shape[1] // 2
    me = lax.axis_index("col")
    along = lambda value, step: lax.ppermute(value, "col", pairs_of(4, step))
    own = [slot[:, :half], slot[:, half:]]
    near, far = [], []
    for piece in own:
        near.append(along(piece, 1))
        far.append(along(piece, 2))
    cross = [along(far[0], 1), along(near[1], 2)]
    spare = (roots[0] + 3) % 4
    case = me ^ spare
    rounds = [
        ((*own, near[0], far[0]), jnp.array([[2, 3], [0, 1], [0, 1], [0, 1]], jnp.int32)[case]),
        ((*near, *far), jnp.array([[1, 3], [2, 3], [0, 1], [0, 2]], jnp.int32)[case]),
        ((*cross, near[1], far[1]), jnp.array([[0, 1], [0, 1], [0, 1], [2, 3]], jnp.int32)[case]),
    ]
    slots = jnp.array([[1, 2, 1, 2, 3, 3], [0, 0, 2, 2, 3, 3], [0, 0, 1, 1, 3, 3], [0, 0, 1, 2, 1, 2]], jnp.int32)
    halves = jnp.array([[0, 0, 1, 1, 0, 1], [0, 1, 0, 1, 0, 1], [0, 1, 0, 1, 0, 1], [0, 1, 0, 0, 1, 1]], jnp.int32)
    panel = ((slots[case] ^ me) - roots[0]) % 4
    places = panel * 2 + halves[case]
    later_of = jnp.array([[0, 1, 0, 0], [1, 0, 2, 2]], jnp.int32)[roots[0] - 2, me]
    earlier_of = jnp.array([[2, 2, 0, 1], [0, 0, 1, 0]], jnp.int32)[roots[0] - 2, me]
    both = jnp.arange(2, dtype=jnp.int32)
    later = ((*own, *near, *far), 2 * later_of + both)
    earlier = ((*own, *near, *far), 2 * earlier_of + both)
    holders = jnp.array([[3, 0, 1], [2, 3, 0]], jnp.int32)[roots[0] - 2]
    return rounds, places, later, earlier, holders


def fetch_any(slot, roots):
    half = slot.shape[1] // 2
    me = lax.axis_index("col")
    panels = [lax.psum(jnp.where(me == roots[index], slot, jnp.zeros_like(slot)), "col") for index in range(PANELS)]
    rounds = [(panel[:, :half], panel[:, half:]) for panel in panels]
    return rounds, jnp.arange(2 * PANELS, dtype=jnp.int32), panels


def gram(left, right):
    return lax.dot_general(
        left, right, (((0,), (0,)), ((), ())), precision=lax.Precision.HIGH, preferred_element_type=F32
    )


def exchange_kernel(names, pieces, ends_ref, *refs):
    use = dict(zip(names, refs))
    end = ends_ref[0] == 1
    if "acc" in use:
        start = 0
        for index in range(pieces):
            keep, swapped = use["keep", index], use["swapped", index]
            columns = slice(start, start + keep.shape[1])
            use["acc"][:, columns] = keep[...] + swapped[...]
            start = columns.stop
    if "part" in use:
        columns = use["part"].shape[1]
        use["part"][...] = use["acc_before"][...] + use["outer"][:, :columns]
    if "total" in use:
        use["total"][...] = use["part_before"][...] + use["inner"][...]
    if "final" in use:
        columns = use["final"].shape[1]
        use["final"][...] = jnp.where(end, use["outer"][:, :columns], use["total_before"][...])
    if "out" in use:
        sources = [use[name] for name in ("acc", "total") if name in use]
        if len(sources) == 1:
            use["out"][...] = sources[0][...]
        else:
            both = min(source.shape[1] for source in sources)
            use["out"][:, :both] = jnp.where(end, sources[0][:, :both], sources[1][:, :both])
            for source in sources:
                if source.shape[1] > both:
                    use["out"][:, both:] = source[:, both:]


def exchange(ends, operands, shapes, after):
    names = list(operands) + [None] * len(after) + list(shapes)
    pieces = sum(name[0] == "keep" for name in operands)
    in_vmem = pl.BlockSpec(memory_space=pltpu.VMEM)
    results = pl.pallas_call(
        functools.partial(exchange_kernel, names, pieces),
        in_specs=[pl.BlockSpec(memory_space=pltpu.SMEM)] + [in_vmem] * len(operands)
        + [ANYWHERE] * len(after),
        out_specs=[in_vmem] * len(shapes),
        out_shape=[jax.ShapeDtypeStruct(shape, F32) for shape in shapes.values()],
        compiler_params=params(),
        cost_estimate=cost(0, 0),
        name="exchange",
    )(ends, *operands.values(), *after)
    return dict(zip(shapes, results))


def shards_square(eigvec, slot, roots, tfac):
    columns = eigvec.shape[1]
    width = columns // 2
    rounds, places, later, earlier, holders = fetch_square(slot, roots)
    chip, core = lax.axis_index("row") // 2, lax.axis_index("row") % 2
    ends = jnp.where((chip == 0) | (chip == 3), 1, 0).astype(jnp.int32).reshape(1)
    places = jnp.where(core == 0, places, places.reshape(PANELS, 2)[:, ::-1].reshape(-1))
    ordered = lambda pair: jnp.where(core == 0, pair, pair[::-1])
    x_high, x_low = split_array(eigvec)
    chunks = [(index, block) for index in range(PANELS) for block in range(columns // width)]
    count = len(chunks)
    gram_chunk = 3
    prepared, arrived, sizes, gram_pieces = {}, {}, {}, []
    half = slot.shape[1] // 2

    def start(number, after):
        index, block = chunks[number]
        pieces = []
        if index not in prepared:
            cases, which = rounds[index]
            prepared[index] = choose(cases, ordered(which), ("high", "low", "flipped"), after)
        for part in range(width // PIECE):
            pieces.append(products(prepared[index][2], x_high, x_low, block * (width // PIECE) + part, PIECE, after))
        if number == gram_chunk - 1:
            (flipped,) = choose(later[0], ordered(later[1]), ("flipped",), after)
            high, low = choose(*earlier, ("high", "low"), after)
            gram_pieces.append(products(flipped, high, low, 0, high.shape[1]))
        if number == gram_chunk:
            pieces.extend(gram_pieces)
        arrived[number] = [(mine, swap_cores(other)) for mine, other in pieces]
        sizes[number] = (half, sum(mine.shape[1] for mine, other in pieces))

    outer_pairs = both_cores([(0, 1), (1, 0), (2, 3), (3, 2)])
    inner_pairs = both_cores([(1, 2), (2, 1)])
    acc, part, total, outer, inner, sums = {}, {}, {}, {}, {}, {}
    grams, out = None, None
    start(0, ())
    for step in range(count + 3 * LAG):
        operands, shapes = {}, {}
        inward, middle, outward = step - LAG, step - 2 * LAG, step - 3 * LAG
        if step < count:
            for number, (mine, other) in enumerate(arrived[step]):
                operands["keep", number], operands["swapped", number] = mine, other
            shapes["acc"] = sizes[step]
        if step - LAG in outer:
            operands["outer"] = outer[step - LAG]
        if 0 <= inward < count:
            operands["acc_before"] = acc[inward]
            shapes["part"] = sizes[inward]
        if 0 <= middle < count:
            operands["part_before"], operands["inner"] = part[middle], inner[step - LAG]
            shapes["total"] = sizes[middle]
        if 0 <= outward < count:
            operands["total_before"] = total[outward]
            shapes["final"] = sizes[outward]
        sent = [shapes[name] for name in ("acc", "total") if name in shapes]
        if sent:
            shapes["out"] = max(sent, key=lambda shape: shape[1])
        ahead = [] if out is None else [out]
        if step == gram_chunk - 1:
            ahead.append(gram_pieces[0][0])
        results = exchange(ends, operands, shapes, ahead)
        if "out" in results:
            outer[step] = lax.ppermute(results["out"], "row", outer_pairs)
        if "acc" in results:
            acc[step] = results["acc"]
        if "part" in results:
            part[inward] = results["part"]
            inner[step] = lax.ppermute(results["part"], "row", inner_pairs)
        if "total" in results:
            total[middle] = results["total"]
        if step + 1 < count:
            start(step + 1, [next(iter(results.values()))])
        if "final" in results:
            done = outward
            own, other = results["final"], swap_cores(results["final"])
            if done == gram_chunk:
                pair = own[:, width:], other[:, width:]
                block = jnp.where(core == 0, jnp.concatenate(pair, axis=0), jnp.concatenate(pair[::-1], axis=0))
                spread = [block] + [lax.ppermute(block, "col", pairs_of(4, shift)) for shift in range(1, 4)]
                places_of = holders ^ lax.axis_index("col")
                grams = jnp.stack([pick(places_of[number], *spread) for number in range(PANELS)])
            sums[chunks[done]] = (own, other)
            index, block = chunks[done]
            if index == PANELS - 1:
                pieces = [piece for panel in range(PANELS) for piece in sums[panel, block]]
                highs, lows = zip(*[prepared[panel][:2] for panel in range(PANELS)])
                out = update(places, pieces, tfac, grams, highs, lows, eigvec, out, block, width)
    return out


def shards(eigvec, slots, roots, tfac):
    if lax.axis_size("col") == 4 and lax.axis_size("row") == 8:
        return shards_square(eigvec, slots[0], roots, tfac)
    columns = eigvec.shape[1]
    width = min(columns, BLOCK)
    rounds, places, panels = fetch_any(slots[0], roots)
    core = lax.axis_index("row") % 2
    places = jnp.where(core == 0, places, places.reshape(PANELS, 2)[:, ::-1].reshape(-1))
    x_high, x_low = split_array(eigvec)
    highs, lows, sums = [], [], []
    for first, second in rounds:
        keep = jnp.where(core == 0, first, second)
        send = jnp.where(core == 0, second, first)
        high, low, flipped = prepare(keep, send)
        highs.append(high)
        lows.append(low)
        sums.append([
            sum_over_rows(*products(flipped, x_high, x_low, block, width)) for block in range(columns // width)
        ])
    grams = jnp.stack([gram(panels[1], panels[0]), gram(panels[2], panels[0]), gram(panels[2], panels[1])])
    grams = lax.psum(grams, "row")
    out = None
    for block in range(columns // width):
        pieces = [piece for index in range(PANELS) for piece in sums[index][block]]
        out = update(places, pieces, tfac, grams, highs, lows, eigvec, out, block, width)
    return out


def solution(mesh):
    in_specs = (P("row", "col"), P("col", "row", None), P(), P())
    out_specs = P("row", "col")
    return jax.shard_map(shards, mesh=mesh, in_specs=in_specs, out_specs=out_specs, check_vma=False)
```

```python
import functools

import jax
import jax.numpy as jnp
from jax import lax
from jax.experimental import pallas as pl
from jax.experimental.pallas import tpu as pltpu
from jax.sharding import PartitionSpec as P

PANELS = 3
BLOCK = 512
LAG = 1
PIECE = 512
MIB = 1024 * 1024
F32 = jnp.float32
BF16 = jnp.bfloat16
ANYWHERE = pl.BlockSpec(memory_space=pl.ANY)


def split(value):
    high = value.astype(BF16)
    return high, (value - high.astype(F32)).astype(BF16)


def dot(left, right):
    return jnp.dot(left, right, preferred_element_type=F32)


def dot_three(left, right):
    left_high, left_low = split(left)
    right_high, right_low = split(right)
    return dot(
        jnp.concatenate([left_high, left_low, left_high], axis=1),
        jnp.concatenate([right_high, right_high, right_low], axis=0),
    )


def params(mib):
    return pltpu.CompilerParams(vmem_limit_bytes=mib * MIB)


def cost(flops, count):
    return pl.CostEstimate(flops=flops // 64, bytes_accessed=count // 64, transcendentals=0)


def split_kernel(x_ref, high_ref, low_ref):
    high_ref[...], low_ref[...] = split(x_ref[...])


def split_array(x):
    rows, columns = x.shape
    step = min(rows, 256)
    spec = pl.BlockSpec((step, columns), lambda i: (i, 0))
    return pl.pallas_call(
        split_kernel,
        grid=(rows // step,),
        in_specs=[spec],
        out_specs=[spec, spec],
        out_shape=[jax.ShapeDtypeStruct(x.shape, BF16)] * 2,
        compiler_params=params(16),
        cost_estimate=cost(rows * columns * 4, rows * columns * 8),
        name="split_x",
    )(x)


def prepare_kernel(keep_ref, send_ref, *refs):
    high_ref, low_ref, flipped_ref = refs[-3:]
    both = jnp.concatenate([keep_ref[...], send_ref[...]], axis=1)
    high_ref[...], low_ref[...] = split(both)
    high, low = split(both.T)
    width = both.shape[1]
    flipped_ref[:width, :] = high
    flipped_ref[width:, :] = low


def prepare(keep, send, after=()):
    rows, half = keep.shape
    step = min(rows, 512)
    half_spec = pl.BlockSpec((step, half), lambda i: (i, 0))
    spec = pl.BlockSpec((step, 2 * half), lambda i: (i, 0))
    return pl.pallas_call(
        prepare_kernel,
        grid=(rows // step,),
        in_specs=[half_spec, half_spec] + [ANYWHERE] * len(after),
        out_specs=[spec, spec, pl.BlockSpec((4 * half, step), lambda i: (0, i))],
        out_shape=[
            jax.ShapeDtypeStruct((rows, 2 * half), BF16),
            jax.ShapeDtypeStruct((rows, 2 * half), BF16),
            jax.ShapeDtypeStruct((4 * half, rows), BF16),
        ],
        compiler_params=params(16),
        cost_estimate=cost(rows * half * 8, rows * half * 24),
        name="prepare_panel",
    )(keep, send, *after)


def choose_kernel(outputs, count, which_ref, *refs):
    cases, outs, (panel_ref, sem) = refs[:count], refs[-2 - len(outputs) : -2], refs[-2:]
    half = cases[0].shape[1]
    for side in range(2):
        for index, case in enumerate(cases):

            @pl.when(which_ref[side] == index)
            def _(case=case, side=side):
                copy = pltpu.make_async_copy(case, panel_ref.at[:, side * half : (side + 1) * half], sem)
                copy.start()
                copy.wait()

    use = dict(zip(outputs, outs))
    rows, width = panel_ref.shape
    step = min(rows, 256)
    for start in range(0, rows, step):
        here = slice(start, start + step)
        value = panel_ref[here, :]
        high, low = split(value)
        if "high" in use:
            use["high"][here, :] = high
            use["low"][here, :] = low
        if "flipped" in use:
            high, low = split(value.T)
            use["flipped"][:width, here] = high
            use["flipped"][width:, here] = low


def choose(cases, which, outputs, after=()):
    rows, half = cases[0].shape
    shapes = {"high": (rows, 2 * half), "low": (rows, 2 * half), "flipped": (4 * half, rows)}
    in_vmem = pl.BlockSpec(memory_space=pltpu.VMEM)
    return pl.pallas_call(
        functools.partial(choose_kernel, outputs, len(cases)),
        in_specs=[pl.BlockSpec(memory_space=pltpu.SMEM)] + [ANYWHERE] * (len(cases) + len(after)),
        out_specs=[in_vmem] * len(outputs),
        out_shape=[jax.ShapeDtypeStruct(shapes[name], BF16) for name in outputs],
        scratch_shapes=[pltpu.VMEM((rows, 2 * half), F32), pltpu.SemaphoreType.DMA],
        compiler_params=params(14),
        cost_estimate=cost(rows * half * 8, rows * half * 24),
        name="choose_panel",
    )(which, *cases, *after)


def products_kernel(columns, flipped_ref, high_ref, low_ref, *refs):
    keep_ref, send_ref = refs[-2:]
    width = flipped_ref.shape[0] // 2
    with_high = dot(flipped_ref[...], high_ref[:, columns])
    with_low = dot(flipped_ref[:width, :], low_ref[:, columns])
    total = with_high[:width] + (with_high[width:] + with_low)
    keep_ref[...] = total[: width // 2]
    send_ref[...] = total[width // 2 :]


def products(flipped, high, low, block, width, after=()):
    rows = high.shape[0]
    half = flipped.shape[0] // 4
    in_vmem = pl.BlockSpec(memory_space=pltpu.VMEM)
    return pl.pallas_call(
        functools.partial(products_kernel, slice(block * width, (block + 1) * width)),
        in_specs=[in_vmem] * 3 + [ANYWHERE] * len(after),
        out_specs=[in_vmem] * 2,
        out_shape=[jax.ShapeDtypeStruct((half, width), F32)] * 2,
        compiler_params=params(28),
        cost_estimate=cost(2 * 6 * half * rows * width, rows * width * 4 + 8 * half * rows),
        name="products",
    )(flipped, high, low, *after)


def update_kernel(place_ref, *refs):
    sums = refs[:6]
    tfac_ref, gram_ref = refs[6:8]
    high_refs, low_refs = refs[8:11], refs[11:14]
    x_ref = refs[14]
    out_ref, w_ref, y_ref, y_split_ref = refs[-4:]
    half = sums[0].shape[0]
    width = 2 * half

    @pl.when(pl.program_id(0) == 0)
    def _():
        for index, piece in enumerate(sums):
            start = pl.multiple_of(place_ref[index] * half, half)
            w_ref[pl.ds(start, half), :] = piece[...]
        first = dot_three(tfac_ref[0], w_ref[:width, :])
        y_ref[:width, :] = first
        second = dot_three(tfac_ref[1], w_ref[width : 2 * width, :] - dot_three(gram_ref[0], first))
        y_ref[width : 2 * width, :] = second
        third = w_ref[2 * width :, :] - dot_three(gram_ref[1], first) - dot_three(gram_ref[2], second)
        y_ref[2 * width :, :] = dot_three(tfac_ref[2], third)
        for index in range(6):
            start = pl.multiple_of(place_ref[index] * half, half)
            high, low = split(y_ref[pl.ds(start, half), :])
            for number, value in enumerate((high, high, low)):
                y_split_ref[(6 * number + index) * half : (6 * number + index + 1) * half, :] = value

    sides = [ref[...] for ref in (*high_refs, *low_refs, *high_refs)]
    out_ref[...] = x_ref[...] - dot(jnp.concatenate(sides, axis=1), y_split_ref[...])


def update(place, sums, tfac, grams, highs, lows, x, out, block, width):
    rows, columns = x.shape
    half = sums[0].shape[0]
    step = min(rows, 512)
    whole = lambda *shape: pl.BlockSpec(shape, lambda i, place: (0,) * len(shape))
    panel_spec = pl.BlockSpec((step, 2 * half), lambda i, place: (i, 0))
    block_spec = pl.BlockSpec((step, width), lambda i, place: (i, block))
    operands = [place, *sums, tfac, grams, *highs, *lows, x]
    in_specs = (
        [whole(half, width)] * 6
        + [whole(3, 2 * half, 2 * half)] * 2
        + [panel_spec] * 6
        + [block_spec]
    )
    aliases = {}
    if out is not None:
        aliases = {len(operands): 0}
        operands.append(out)
        in_specs.append(pl.BlockSpec(memory_space=pl.ANY))
    return pl.pallas_call(
        update_kernel,
        grid_spec=pltpu.PrefetchScalarGridSpec(
            num_scalar_prefetch=1,
            grid=(rows // step,),
            in_specs=in_specs,
            out_specs=block_spec,
            scratch_shapes=[
                pltpu.VMEM((6 * half, width), F32),
                pltpu.VMEM((6 * half, width), F32),
                pltpu.VMEM((18 * half, width), BF16),
            ],
        ),
        out_shape=jax.ShapeDtypeStruct(x.shape, F32),
        input_output_aliases=aliases,
        compiler_params=params(40),
        cost_estimate=cost(2 * 18 * half * rows * width, rows * width * 8 + rows * half * 24),
        name="update",
    )(*operands)


def pairs_of(count, step):
    return [(index, index ^ step) for index in range(count)]


def swap_cores(value):
    return lax.ppermute(value, "row", pairs_of(lax.axis_size("row"), 1))


def both_cores(chip_pairs):
    return [(2 * a + core, 2 * b + core) for a, b in chip_pairs for core in range(2)]


def sum_over_rows(keep, send):
    chips = lax.axis_size("row") // 2
    chip = lax.axis_index("row") // 2
    total = keep + swap_cores(send)
    for hop in range(chips // 2 - 1):
        pairs = [(hop, hop + 1), (chips - 1 - hop, chips - 2 - hop)]
        total = total + lax.ppermute(total, "row", both_cores(pairs))
    middle = [(chips // 2 - 1, chips // 2), (chips // 2, chips // 2 - 1)]
    total = total + lax.ppermute(total, "row", both_cores(middle))
    for hop in reversed(range(chips // 2 - 1)):
        pairs = [(hop + 1, hop), (chips - 2 - hop, chips - 1 - hop)]
        arrived = lax.ppermute(total, "row", both_cores(pairs))
        total = jnp.where((chip == hop) | (chip == chips - 1 - hop), arrived, total)
    return total, swap_cores(total)


def pick(index, *cases):
    return lax.select_n(index, *cases)


def fetch_square(slot, roots):
    half = slot.shape[1] // 2
    me = lax.axis_index("col")
    along = lambda value, step: lax.ppermute(value, "col", pairs_of(4, step))
    own = [slot[:, :half], slot[:, half:]]
    near, far = [], []
    for piece in own:
        near.append(along(piece, 1))
        far.append(along(piece, 2))
    cross = [along(far[0], 1), along(near[1], 2)]
    spare = (roots[0] + 3) % 4
    case = me ^ spare
    rounds = [
        ((*own, near[0], far[0]), jnp.array([[2, 3], [0, 1], [0, 1], [0, 1]], jnp.int32)[case]),
        ((*near, *far), jnp.array([[1, 3], [2, 3], [0, 1], [0, 2]], jnp.int32)[case]),
        ((*cross, near[1], far[1]), jnp.array([[0, 1], [0, 1], [0, 1], [2, 3]], jnp.int32)[case]),
    ]
    slots = jnp.array([[1, 2, 1, 2, 3, 3], [0, 0, 2, 2, 3, 3], [0, 0, 1, 1, 3, 3], [0, 0, 1, 2, 1, 2]], jnp.int32)
    halves = jnp.array([[0, 0, 1, 1, 0, 1], [0, 1, 0, 1, 0, 1], [0, 1, 0, 1, 0, 1], [0, 1, 0, 0, 1, 1]], jnp.int32)
    panel = ((slots[case] ^ me) - roots[0]) % 4
    places = panel * 2 + halves[case]
    later_of = jnp.array([[0, 1, 0, 0], [1, 0, 2, 2]], jnp.int32)[roots[0] - 2, me]
    earlier_of = jnp.array([[2, 2, 0, 1], [0, 0, 1, 0]], jnp.int32)[roots[0] - 2, me]
    both = jnp.arange(2, dtype=jnp.int32)
    later = ((*own, *near, *far), 2 * later_of + both)
    earlier = ((*own, *near, *far), 2 * earlier_of + both)
    holders = jnp.array([[3, 0, 1], [2, 3, 0]], jnp.int32)[roots[0] - 2]
    return rounds, places, later, earlier, holders


def fetch_any(slot, roots):
    half = slot.shape[1] // 2
    me = lax.axis_index("col")
    panels = [lax.psum(jnp.where(me == roots[index], slot, jnp.zeros_like(slot)), "col") for index in range(PANELS)]
    rounds = [(panel[:, :half], panel[:, half:]) for panel in panels]
    return rounds, jnp.arange(2 * PANELS, dtype=jnp.int32), panels


def gram(left, right):
    return lax.dot_general(
        left, right, (((0,), (0,)), ((), ())), precision=lax.Precision.HIGH, preferred_element_type=F32
    )


def exchange_kernel(names, pieces, ends_ref, *refs):
    use = dict(zip(names, refs))
    end = ends_ref[0] == 1
    if "acc" in use:
        start = 0
        for index in range(pieces):
            keep, swapped = use["keep", index], use["swapped", index]
            columns = slice(start, start + keep.shape[1])
            use["acc"][:, columns] = keep[...] + swapped[...]
            start = columns.stop
    if "part" in use:
        columns = use["part"].shape[1]
        use["part"][...] = use["acc_before"][...] + use["outer"][:, :columns]
    if "total" in use:
        use["total"][...] = use["part_before"][...] + use["inner"][...]
    if "final" in use:
        columns = use["final"].shape[1]
        use["final"][...] = jnp.where(end, use["outer"][:, :columns], use["total_before"][...])
    if "out" in use:
        sources = [use[name] for name in ("acc", "total") if name in use]
        if len(sources) == 1:
            use["out"][...] = sources[0][...]
        else:
            both = min(source.shape[1] for source in sources)
            use["out"][:, :both] = jnp.where(end, sources[0][:, :both], sources[1][:, :both])
            for source in sources:
                if source.shape[1] > both:
                    use["out"][:, both:] = source[:, both:]


def exchange(ends, operands, shapes, after):
    names = list(operands) + [None] * len(after) + list(shapes)
    pieces = sum(name[0] == "keep" for name in operands)
    in_vmem = pl.BlockSpec(memory_space=pltpu.VMEM)
    results = pl.pallas_call(
        functools.partial(exchange_kernel, names, pieces),
        in_specs=[pl.BlockSpec(memory_space=pltpu.SMEM)] + [in_vmem] * len(operands)
        + [ANYWHERE] * len(after),
        out_specs=[in_vmem] * len(shapes),
        out_shape=[jax.ShapeDtypeStruct(shape, F32) for shape in shapes.values()],
        compiler_params=params(14),
        cost_estimate=cost(0, 0),
        name="exchange",
    )(ends, *operands.values(), *after)
    return dict(zip(shapes, results))


def shards_square(eigvec, slot, roots, tfac):
    columns = eigvec.shape[1]
    width = columns // 2
    rounds, places, later, earlier, holders = fetch_square(slot, roots)
    chip, core = lax.axis_index("row") // 2, lax.axis_index("row") % 2
    ends = jnp.where((chip == 0) | (chip == 3), 1, 0).astype(jnp.int32).reshape(1)
    places = jnp.where(core == 0, places, places.reshape(PANELS, 2)[:, ::-1].reshape(-1))
    ordered = lambda pair: jnp.where(core == 0, pair, pair[::-1])
    x_high, x_low = split_array(eigvec)
    chunks = [(index, block) for index in range(PANELS) for block in range(columns // width)]
    count = len(chunks)
    gram_chunk = 3
    prepared, arrived, sizes, gram_pieces = {}, {}, {}, []
    half = slot.shape[1] // 2

    def start(number, after):
        index, block = chunks[number]
        pieces = []
        if index not in prepared:
            cases, which = rounds[index]
            prepared[index] = choose(cases, ordered(which), ("high", "low", "flipped"), after)
        for part in range(width // PIECE):
            pieces.append(products(prepared[index][2], x_high, x_low, block * (width // PIECE) + part, PIECE, after))
        if number == gram_chunk - 1:
            (flipped,) = choose(later[0], ordered(later[1]), ("flipped",), after)
            high, low = choose(*earlier, ("high", "low"), after)
            gram_pieces.append(products(flipped, high, low, 0, high.shape[1]))
        if number == gram_chunk:
            pieces.extend(gram_pieces)
        arrived[number] = [(mine, swap_cores(other)) for mine, other in pieces]
        sizes[number] = (half, sum(mine.shape[1] for mine, other in pieces))

    outer_pairs = both_cores([(0, 1), (1, 0), (2, 3), (3, 2)])
    inner_pairs = both_cores([(1, 2), (2, 1)])
    acc, part, total, outer, inner, sums = {}, {}, {}, {}, {}, {}
    grams, out = None, None
    start(0, ())
    for step in range(count + 3 * LAG):
        operands, shapes = {}, {}
        inward, middle, outward = step - LAG, step - 2 * LAG, step - 3 * LAG
        if step < count:
            for number, (mine, other) in enumerate(arrived[step]):
                operands["keep", number], operands["swapped", number] = mine, other
            shapes["acc"] = sizes[step]
        if step - LAG in outer:
            operands["outer"] = outer[step - LAG]
        if 0 <= inward < count:
            operands["acc_before"] = acc[inward]
            shapes["part"] = sizes[inward]
        if 0 <= middle < count:
            operands["part_before"], operands["inner"] = part[middle], inner[step - LAG]
            shapes["total"] = sizes[middle]
        if 0 <= outward < count:
            operands["total_before"] = total[outward]
            shapes["final"] = sizes[outward]
        sent = [shapes[name] for name in ("acc", "total") if name in shapes]
        if sent:
            shapes["out"] = max(sent, key=lambda shape: shape[1])
        ahead = [] if out is None else [out]
        if step == gram_chunk - 1:
            ahead.append(gram_pieces[0][0])
        results = exchange(ends, operands, shapes, ahead)
        if "out" in results:
            outer[step] = lax.ppermute(results["out"], "row", outer_pairs)
        if "acc" in results:
            acc[step] = results["acc"]
        if "part" in results:
            part[inward] = results["part"]
            inner[step] = lax.ppermute(results["part"], "row", inner_pairs)
        if "total" in results:
            total[middle] = results["total"]
        if step + 1 < count:
            start(step + 1, [next(iter(results.values()))])
        if "final" in results:
            done = outward
            own, other = results["final"], swap_cores(results["final"])
            if done == gram_chunk:
                pair = own[:, width:], other[:, width:]
                block = jnp.where(core == 0, jnp.concatenate(pair, axis=0), jnp.concatenate(pair[::-1], axis=0))
                spread = [block] + [lax.ppermute(block, "col", pairs_of(4, shift)) for shift in range(1, 4)]
                places_of = holders ^ lax.axis_index("col")
                grams = jnp.stack([pick(places_of[number], *spread) for number in range(PANELS)])
            sums[chunks[done]] = (own, other)
            index, block = chunks[done]
            if index == PANELS - 1:
                pieces = [piece for panel in range(PANELS) for piece in sums[panel, block]]
                highs, lows = zip(*[prepared[panel][:2] for panel in range(PANELS)])
                out = update(places, pieces, tfac, grams, highs, lows, eigvec, out, block, width)
    return out


def shards(eigvec, slots, roots, tfac):
    if lax.axis_size("col") == 4 and lax.axis_size("row") == 8:
        return shards_square(eigvec, slots[0], roots, tfac)
    columns = eigvec.shape[1]
    width = min(columns, BLOCK)
    rounds, places, panels = fetch_any(slots[0], roots)
    core = lax.axis_index("row") % 2
    places = jnp.where(core == 0, places, places.reshape(PANELS, 2)[:, ::-1].reshape(-1))
    x_high, x_low = split_array(eigvec)
    highs, lows, sums = [], [], []
    for first, second in rounds:
        keep = jnp.where(core == 0, first, second)
        send = jnp.where(core == 0, second, first)
        high, low, flipped = prepare(keep, send)
        highs.append(high)
        lows.append(low)
        sums.append([
            sum_over_rows(*products(flipped, x_high, x_low, block, width)) for block in range(columns // width)
        ])
    grams = jnp.stack([gram(panels[1], panels[0]), gram(panels[2], panels[0]), gram(panels[2], panels[1])])
    grams = lax.psum(grams, "row")
    out = None
    for block in range(columns // width):
        pieces = [piece for index in range(PANELS) for piece in sums[index][block]]
        out = update(places, pieces, tfac, grams, highs, lows, eigvec, out, block, width)
    return out


def solution(mesh):
    in_specs = (P("row", "col"), P("col", "row", None), P(), P())
    out_specs = P("row", "col")
    return jax.shard_map(shards, mesh=mesh, in_specs=in_specs, out_specs=out_specs, check_vma=False)
```

```python
import functools

import jax
import jax.numpy as jnp
from jax import lax
from jax.experimental import pallas as pl
from jax.experimental.pallas import tpu as pltpu
from jax.sharding import PartitionSpec as P

PANELS = 3
BLOCK = 512
LAG = 1
PIECE = 512
MIB = 1024 * 1024
F32 = jnp.float32
BF16 = jnp.bfloat16
ANYWHERE = pl.BlockSpec(memory_space=pl.ANY)
IN_HBM = pl.BlockSpec(memory_space=pltpu.HBM)


def split(value):
    high = value.astype(BF16)
    return high, (value - high.astype(F32)).astype(BF16)


def dot(left, right):
    return jnp.dot(left, right, preferred_element_type=F32)


def dot_three(left, right):
    left_high, left_low = split(left)
    right_high, right_low = split(right)
    return dot(
        jnp.concatenate([left_high, left_low, left_high], axis=1),
        jnp.concatenate([right_high, right_high, right_low], axis=0),
    )


def params(mib):
    return pltpu.CompilerParams(vmem_limit_bytes=mib * MIB)


def cost(flops, count):
    return pl.CostEstimate(flops=flops // 64, bytes_accessed=count // 64, transcendentals=0)


def split_kernel(x_ref, high_ref, low_ref):
    high_ref[...], low_ref[...] = split(x_ref[...])


def split_array(x):
    rows, columns = x.shape
    step = min(rows, 256)
    spec = pl.BlockSpec((step, columns), lambda i: (i, 0))
    return pl.pallas_call(
        split_kernel,
        grid=(rows // step,),
        in_specs=[spec],
        out_specs=[spec, spec],
        out_shape=[jax.ShapeDtypeStruct(x.shape, BF16)] * 2,
        compiler_params=params(16),
        cost_estimate=cost(rows * columns * 4, rows * columns * 8),
        name="split_x",
    )(x)


def prepare_kernel(keep_ref, send_ref, *refs):
    high_ref, low_ref, flipped_ref = refs[-3:]
    both = jnp.concatenate([keep_ref[...], send_ref[...]], axis=1)
    high_ref[...], low_ref[...] = split(both)
    high, low = split(both.T)
    width = both.shape[1]
    flipped_ref[:width, :] = high
    flipped_ref[width:, :] = low


def prepare(keep, send, after=()):
    rows, half = keep.shape
    step = min(rows, 512)
    half_spec = pl.BlockSpec((step, half), lambda i: (i, 0))
    spec = pl.BlockSpec((step, 2 * half), lambda i: (i, 0))
    return pl.pallas_call(
        prepare_kernel,
        grid=(rows // step,),
        in_specs=[half_spec, half_spec] + [ANYWHERE] * len(after),
        out_specs=[spec, spec, pl.BlockSpec((4 * half, step), lambda i: (0, i))],
        out_shape=[
            jax.ShapeDtypeStruct((rows, 2 * half), BF16),
            jax.ShapeDtypeStruct((rows, 2 * half), BF16),
            jax.ShapeDtypeStruct((4 * half, rows), BF16),
        ],
        compiler_params=params(16),
        cost_estimate=cost(rows * half * 8, rows * half * 24),
        name="prepare_panel",
    )(keep, send, *after)


def choose_kernel(outputs, count, which_ref, *refs):
    cases, outs, (panel_ref, sem) = refs[:count], refs[-2 - len(outputs) : -2], refs[-2:]
    half = cases[0].shape[1]
    for side in range(2):
        for index, case in enumerate(cases):

            @pl.when(which_ref[side] == index)
            def _(case=case, side=side):
                copy = pltpu.make_async_copy(case, panel_ref.at[:, side * half : (side + 1) * half], sem)
                copy.start()
                copy.wait()

    use = dict(zip(outputs, outs))
    rows, width = panel_ref.shape
    step = min(rows, 256)
    for start in range(0, rows, step):
        here = slice(start, start + step)
        value = panel_ref[here, :]
        high, low = split(value)
        if "high" in use:
            use["high"][here, :] = high
            use["low"][here, :] = low
        if "flipped" in use:
            high, low = split(value.T)
            use["flipped"][:width, here] = high
            use["flipped"][width:, here] = low


def choose(cases, which, outputs, after=()):
    rows, half = cases[0].shape
    shapes = {"high": (rows, 2 * half), "low": (rows, 2 * half), "flipped": (4 * half, rows)}
    in_vmem = pl.BlockSpec(memory_space=pltpu.VMEM)
    return pl.pallas_call(
        functools.partial(choose_kernel, outputs, len(cases)),
        in_specs=[pl.BlockSpec(memory_space=pltpu.SMEM)] + [ANYWHERE] * (len(cases) + len(after)),
        out_specs=[in_vmem] * len(outputs),
        out_shape=[jax.ShapeDtypeStruct(shapes[name], BF16) for name in outputs],
        scratch_shapes=[pltpu.VMEM((rows, 2 * half), F32), pltpu.SemaphoreType.DMA],
        compiler_params=params(14),
        cost_estimate=cost(rows * half * 8, rows * half * 24),
        name="choose_panel",
    )(which, *cases, *after)


def products_kernel(first, flipped_ref, high_ref, low_ref, *refs):
    keep_ref, send_ref, high_block, low_block, sems = refs[-5:]
    half, width = keep_ref.shape
    step = high_block.shape[2]
    copies = []
    for index in range(width // step):
        columns = slice(first + index * step, first + (index + 1) * step)
        copies.append([
            pltpu.make_async_copy(source.at[:, columns], target.at[index], sems.at[index, side])
            for side, (source, target) in enumerate(((high_ref, high_block), (low_ref, low_block)))
        ])
    for pair in copies:
        for copy in pair:
            copy.start()
    for index, pair in enumerate(copies):
        columns = slice(index * step, (index + 1) * step)
        pair[0].wait()
        with_high = dot(flipped_ref[...], high_block[index])
        pair[1].wait()
        with_low = dot(flipped_ref[: 2 * half, :], low_block[index])
        total = with_high[: 2 * half] + (with_high[2 * half :] + with_low)
        keep_ref[:, columns] = total[:half]
        send_ref[:, columns] = total[half:]


def products(flipped, high, low, block, width, after=()):
    rows = high.shape[0]
    half = flipped.shape[0] // 4
    step = min(width, 256)
    in_vmem = pl.BlockSpec(memory_space=pltpu.VMEM)
    blocks = pltpu.VMEM((width // step, rows, step), BF16)
    return pl.pallas_call(
        functools.partial(products_kernel, block * width),
        in_specs=[in_vmem] + [IN_HBM] * 2 + [ANYWHERE] * len(after),
        out_specs=[in_vmem] * 2,
        out_shape=[jax.ShapeDtypeStruct((half, width), F32)] * 2,
        scratch_shapes=[blocks, blocks, pltpu.SemaphoreType.DMA((width // step, 2))],
        compiler_params=params(14),
        cost_estimate=cost(2 * 6 * half * rows * width, rows * width * 4 + 8 * half * rows),
        name="products",
    )(flipped, high, low, *after)


def update_kernel(place_ref, *refs):
    sums = refs[:6]
    tfac_ref, gram_ref = refs[6:8]
    high_refs, low_refs = refs[8:11], refs[11:14]
    x_ref = refs[14]
    out_ref, done_ref, w_ref, y_ref, y_split_ref = refs[-5:]
    half = sums[0].shape[0]
    width = 2 * half

    @pl.when(pl.program_id(0) == 0)
    def _():
        for index, piece in enumerate(sums):
            start = pl.multiple_of(place_ref[index] * half, half)
            w_ref[pl.ds(start, half), :] = piece[:, : w_ref.shape[1]]
        first = dot_three(tfac_ref[0], w_ref[:width, :])
        y_ref[:width, :] = first
        second = dot_three(tfac_ref[1], w_ref[width : 2 * width, :] - dot_three(gram_ref[0], first))
        y_ref[width : 2 * width, :] = second
        third = w_ref[2 * width :, :] - dot_three(gram_ref[1], first) - dot_three(gram_ref[2], second)
        y_ref[2 * width :, :] = dot_three(tfac_ref[2], third)
        for index in range(6):
            start = pl.multiple_of(place_ref[index] * half, half)
            high, low = split(y_ref[pl.ds(start, half), :])
            for number, value in enumerate((high, high, low)):
                y_split_ref[(6 * number + index) * half : (6 * number + index + 1) * half, :] = value

    sides = [ref[...] for ref in (*high_refs, *low_refs, *high_refs)]
    out_ref[...] = x_ref[...] - dot(jnp.concatenate(sides, axis=1), y_split_ref[...])
    done_ref[...] = jnp.zeros(done_ref.shape, F32)


def update(place, sums, tfac, grams, highs, lows, x, out, block, width):
    rows, columns = x.shape
    half = sums[0].shape[0]
    step = min(rows, 512)
    panel_spec = pl.BlockSpec((step, 2 * half), lambda i, place: (i, 0))
    block_spec = pl.BlockSpec((step, width), lambda i, place: (i, block))
    operands = [place, *sums, tfac, grams, *highs, *lows, x]
    in_specs = (
        [pl.BlockSpec(memory_space=pltpu.VMEM)] * 8
        + [panel_spec] * 6
        + [block_spec]
    )
    aliases = {}
    if out is not None:
        aliases = {len(operands): 0}
        operands.append(out)
        in_specs.append(IN_HBM)
    return pl.pallas_call(
        update_kernel,
        grid_spec=pltpu.PrefetchScalarGridSpec(
            num_scalar_prefetch=1,
            grid=(rows // step,),
            in_specs=in_specs,
            out_specs=[block_spec, pl.BlockSpec((8, 128), lambda i, place: (0, 0))],
            scratch_shapes=[
                pltpu.VMEM((6 * half, width), F32),
                pltpu.VMEM((6 * half, width), F32),
                pltpu.VMEM((18 * half, width), BF16),
            ],
        ),
        out_shape=[jax.ShapeDtypeStruct(x.shape, F32), jax.ShapeDtypeStruct((8, 128), F32)],
        input_output_aliases=aliases,
        compiler_params=params(40),
        cost_estimate=cost(2 * 18 * half * rows * width, rows * width * 8 + rows * half * 24),
        name="update",
    )(*operands)


def pairs_of(count, step):
    return [(index, index ^ step) for index in range(count)]


def swap_cores(value):
    return lax.ppermute(value, "row", pairs_of(lax.axis_size("row"), 1))


def both_cores(chip_pairs):
    return [(2 * a + core, 2 * b + core) for a, b in chip_pairs for core in range(2)]


def sum_over_rows(keep, send):
    chips = lax.axis_size("row") // 2
    chip = lax.axis_index("row") // 2
    total = keep + swap_cores(send)
    for hop in range(chips // 2 - 1):
        pairs = [(hop, hop + 1), (chips - 1 - hop, chips - 2 - hop)]
        total = total + lax.ppermute(total, "row", both_cores(pairs))
    middle = [(chips // 2 - 1, chips // 2), (chips // 2, chips // 2 - 1)]
    total = total + lax.ppermute(total, "row", both_cores(middle))
    for hop in reversed(range(chips // 2 - 1)):
        pairs = [(hop + 1, hop), (chips - 2 - hop, chips - 1 - hop)]
        arrived = lax.ppermute(total, "row", both_cores(pairs))
        total = jnp.where((chip == hop) | (chip == chips - 1 - hop), arrived, total)
    return total, swap_cores(total)


def pick(index, *cases):
    return lax.select_n(index, *cases)


def fetch_square(slot, roots):
    half = slot.shape[1] // 2
    me = lax.axis_index("col")
    along = lambda value, step: lax.ppermute(value, "col", pairs_of(4, step))
    own = [slot[:, :half], slot[:, half:]]
    near, far = [], []
    for piece in own:
        near.append(along(piece, 1))
        far.append(along(piece, 2))
    cross = [along(far[0], 1), along(near[1], 2)]
    spare = (roots[0] + 3) % 4
    case = me ^ spare
    rounds = [
        ((*own, near[0], far[0]), jnp.array([[2, 3], [0, 1], [0, 1], [0, 1]], jnp.int32)[case]),
        ((*near, *far), jnp.array([[1, 3], [2, 3], [0, 1], [0, 2]], jnp.int32)[case]),
        ((*cross, near[1], far[1]), jnp.array([[0, 1], [0, 1], [0, 1], [2, 3]], jnp.int32)[case]),
    ]
    slots = jnp.array([[1, 2, 1, 2, 3, 3], [0, 0, 2, 2, 3, 3], [0, 0, 1, 1, 3, 3], [0, 0, 1, 2, 1, 2]], jnp.int32)
    halves = jnp.array([[0, 0, 1, 1, 0, 1], [0, 1, 0, 1, 0, 1], [0, 1, 0, 1, 0, 1], [0, 1, 0, 0, 1, 1]], jnp.int32)
    panel = ((slots[case] ^ me) - roots[0]) % 4
    places = panel * 2 + halves[case]
    later_of = jnp.array([[0, 1, 0, 0], [1, 0, 2, 2]], jnp.int32)[roots[0] - 2, me]
    earlier_of = jnp.array([[2, 2, 0, 1], [0, 0, 1, 0]], jnp.int32)[roots[0] - 2, me]
    both = jnp.arange(2, dtype=jnp.int32)
    later = ((*own, *near, *far), 2 * later_of + both)
    earlier = ((*own, *near, *far), 2 * earlier_of + both)
    holders = jnp.array([[3, 0, 1], [2, 3, 0]], jnp.int32)[roots[0] - 2]
    return rounds, places, later, earlier, holders


def fetch_any(slot, roots):
    half = slot.shape[1] // 2
    me = lax.axis_index("col")
    panels = [lax.psum(jnp.where(me == roots[index], slot, jnp.zeros_like(slot)), "col") for index in range(PANELS)]
    rounds = [(panel[:, :half], panel[:, half:]) for panel in panels]
    return rounds, jnp.arange(2 * PANELS, dtype=jnp.int32), panels


def gram(left, right):
    return lax.dot_general(
        left, right, (((0,), (0,)), ((), ())), precision=lax.Precision.HIGH, preferred_element_type=F32
    )


def exchange_kernel(names, pieces, ends_ref, *refs):
    use = dict(zip(names, refs))
    end = ends_ref[0] == 1
    if "acc" in use:
        start = 0
        for index in range(pieces):
            keep, swapped = use["keep", index], use["swapped", index]
            columns = slice(start, start + keep.shape[1])
            use["acc"][:, columns] = keep[...] + swapped[...]
            start = columns.stop
    if "part" in use:
        columns = use["part"].shape[1]
        use["part"][...] = use["acc_before"][...] + use["outer"][:, :columns]
    if "total" in use:
        use["total"][...] = use["part_before"][...] + use["inner"][...]
    if "final" in use:
        columns = use["final"].shape[1]
        use["final"][...] = jnp.where(end, use["outer"][:, :columns], use["total_before"][...])
    if "out" in use:
        sources = [use[name] for name in ("acc", "total") if name in use]
        if len(sources) == 1:
            use["out"][...] = sources[0][...]
        else:
            both = min(source.shape[1] for source in sources)
            use["out"][:, :both] = jnp.where(end, sources[0][:, :both], sources[1][:, :both])
            for source in sources:
                if source.shape[1] > both:
                    use["out"][:, both:] = source[:, both:]


def exchange(ends, operands, shapes, after):
    names = list(operands) + [None] * len(after) + list(shapes)
    pieces = sum(name[0] == "keep" for name in operands)
    in_vmem = pl.BlockSpec(memory_space=pltpu.VMEM)
    results = pl.pallas_call(
        functools.partial(exchange_kernel, names, pieces),
        in_specs=[pl.BlockSpec(memory_space=pltpu.SMEM)] + [in_vmem] * len(operands)
        + [ANYWHERE] * len(after),
        out_specs=[in_vmem] * len(shapes),
        out_shape=[jax.ShapeDtypeStruct(shape, F32) for shape in shapes.values()],
        compiler_params=params(14),
        cost_estimate=cost(0, 0),
        name="exchange",
    )(ends, *operands.values(), *after)
    return dict(zip(shapes, results))


def shards_square(eigvec, slot, roots, tfac):
    columns = eigvec.shape[1]
    width = columns // 2
    rounds, places, later, earlier, holders = fetch_square(slot, roots)
    chip, core = lax.axis_index("row") // 2, lax.axis_index("row") % 2
    ends = jnp.where((chip == 0) | (chip == 3), 1, 0).astype(jnp.int32).reshape(1)
    places = jnp.where(core == 0, places, places.reshape(PANELS, 2)[:, ::-1].reshape(-1))
    ordered = lambda pair: jnp.where(core == 0, pair, pair[::-1])
    x_high, x_low = split_array(eigvec)
    chunks = [(index, block) for index in range(PANELS) for block in range(columns // width)]
    count = len(chunks)
    gram_chunk = 3
    prepared, arrived, sizes, gram_pieces = {}, {}, {}, []
    half = slot.shape[1] // 2

    def start(number, after):
        index, block = chunks[number]
        pieces = []
        if index not in prepared:
            cases, which = rounds[index]
            prepared[index] = choose(cases, ordered(which), ("high", "low", "flipped"), after)
        for part in range(width // PIECE):
            pieces.append(products(prepared[index][2], x_high, x_low, block * (width // PIECE) + part, PIECE, after))
        if number == gram_chunk - 1:
            (flipped,) = choose(later[0], ordered(later[1]), ("flipped",), after)
            high, low = choose(*earlier, ("high", "low"), after)
            gram_pieces.append(products(flipped, high, low, 0, high.shape[1]))
        if number == gram_chunk:
            pieces.extend(gram_pieces)
        arrived[number] = [(mine, swap_cores(other)) for mine, other in pieces]
        sizes[number] = (half, sum(mine.shape[1] for mine, other in pieces))

    outer_pairs = both_cores([(0, 1), (1, 0), (2, 3), (3, 2)])
    inner_pairs = both_cores([(1, 2), (2, 1)])
    acc, part, total, outer, inner, sums = {}, {}, {}, {}, {}, {}
    grams, out = None, None
    start(0, ())
    for step in range(count + 3 * LAG):
        operands, shapes = {}, {}
        inward, middle, outward = step - LAG, step - 2 * LAG, step - 3 * LAG
        if step < count:
            for number, (mine, other) in enumerate(arrived[step]):
                operands["keep", number], operands["swapped", number] = mine, other
            shapes["acc"] = sizes[step]
        if step - LAG in outer:
            operands["outer"] = outer[step - LAG]
        if 0 <= inward < count:
            operands["acc_before"] = acc[inward]
            shapes["part"] = sizes[inward]
        if 0 <= middle < count:
            operands["part_before"], operands["inner"] = part[middle], inner[step - LAG]
            shapes["total"] = sizes[middle]
        if 0 <= outward < count:
            operands["total_before"] = total[outward]
            shapes["final"] = sizes[outward]
        sent = [shapes[name] for name in ("acc", "total") if name in shapes]
        if sent:
            shapes["out"] = max(sent, key=lambda shape: shape[1])
        ahead = [] if out is None else [finished]
        if step == gram_chunk - 1:
            ahead.append(gram_pieces[0][0])
        results = exchange(ends, operands, shapes, ahead)
        if "out" in results:
            outer[step] = lax.ppermute(results["out"], "row", outer_pairs)
        if "acc" in results:
            acc[step] = results["acc"]
        if "part" in results:
            part[inward] = results["part"]
            inner[step] = lax.ppermute(results["part"], "row", inner_pairs)
        if "total" in results:
            total[middle] = results["total"]
        if step + 1 < count:
            start(step + 1, [next(iter(results.values()))])
        if "final" in results:
            done = outward
            own, other = results["final"], swap_cores(results["final"])
            if done == gram_chunk:
                pair = own[:, width:], other[:, width:]
                block = jnp.where(core == 0, jnp.concatenate(pair, axis=0), jnp.concatenate(pair[::-1], axis=0))
                spread = [block] + [lax.ppermute(block, "col", pairs_of(4, shift)) for shift in range(1, 4)]
                places_of = holders ^ lax.axis_index("col")
                grams = jnp.stack([pick(places_of[number], *spread) for number in range(PANELS)])
            sums[chunks[done]] = (own, other)
            index, block = chunks[done]
            if index == PANELS - 1:
                pieces = [piece for panel in range(PANELS) for piece in sums[panel, block]]
                highs, lows = zip(*[prepared[panel][:2] for panel in range(PANELS)])
                out, finished = update(places, pieces, tfac, grams, highs, lows, eigvec, out, block, width)
    return out


def shards(eigvec, slots, roots, tfac):
    if lax.axis_size("col") == 4 and lax.axis_size("row") == 8:
        return shards_square(eigvec, slots[0], roots, tfac)
    columns = eigvec.shape[1]
    width = min(columns, BLOCK)
    rounds, places, panels = fetch_any(slots[0], roots)
    core = lax.axis_index("row") % 2
    places = jnp.where(core == 0, places, places.reshape(PANELS, 2)[:, ::-1].reshape(-1))
    x_high, x_low = split_array(eigvec)
    highs, lows, sums = [], [], []
    for first, second in rounds:
        keep = jnp.where(core == 0, first, second)
        send = jnp.where(core == 0, second, first)
        high, low, flipped = prepare(keep, send)
        highs.append(high)
        lows.append(low)
        sums.append([
            sum_over_rows(*products(flipped, x_high, x_low, block, width)) for block in range(columns // width)
        ])
    grams = jnp.stack([gram(panels[1], panels[0]), gram(panels[2], panels[0]), gram(panels[2], panels[1])])
    grams = lax.psum(grams, "row")
    out = None
    for block in range(columns // width):
        pieces = [piece for index in range(PANELS) for piece in sums[index][block]]
        out, _ = update(places, pieces, tfac, grams, highs, lows, eigvec, out, block, width)
    return out


def solution(mesh):
    in_specs = (P("row", "col"), P("col", "row", None), P(), P())
    out_specs = P("row", "col")
    return jax.shard_map(shards, mesh=mesh, in_specs=in_specs, out_specs=out_specs, check_vma=False)
```

```python
import functools

import jax
import jax.numpy as jnp
from jax import lax
from jax.experimental import pallas as pl
from jax.experimental.pallas import tpu as pltpu
from jax.sharding import PartitionSpec as P

PANELS = 3
BLOCK = 512
LAG = 1
PIECE = 512
MIB = 1024 * 1024
F32 = jnp.float32
BF16 = jnp.bfloat16
ANYWHERE = pl.BlockSpec(memory_space=pl.ANY)
IN_HBM = pl.BlockSpec(memory_space=pltpu.HBM)


def split(value):
    high = value.astype(BF16)
    return high, (value - high.astype(F32)).astype(BF16)


def dot(left, right):
    return jnp.dot(left, right, preferred_element_type=F32)


def dot_three(left, right):
    left_high, left_low = split(left)
    right_high, right_low = split(right)
    return dot(
        jnp.concatenate([left_high, left_low, left_high], axis=1),
        jnp.concatenate([right_high, right_high, right_low], axis=0),
    )


def params(mib):
    return pltpu.CompilerParams(vmem_limit_bytes=mib * MIB)


def cost(flops, count):
    return pl.CostEstimate(flops=flops // 64, bytes_accessed=count // 64, transcendentals=0)


def split_kernel(x_ref, both_ref):
    columns = x_ref.shape[1]
    both_ref[:, :columns], both_ref[:, columns:] = split(x_ref[...])


def split_array(x):
    rows, columns = x.shape
    step = min(rows, 256)
    return pl.pallas_call(
        split_kernel,
        grid=(rows // step,),
        in_specs=[pl.BlockSpec((step, columns), lambda i: (i, 0))],
        out_specs=pl.BlockSpec((step, 2 * columns), lambda i: (i, 0)),
        out_shape=jax.ShapeDtypeStruct((rows, 2 * columns), BF16),
        compiler_params=params(49),
        cost_estimate=cost(rows * columns * 4, rows * columns * 8),
        name="split_x",
    )(x)


def prepare_kernel(keep_ref, send_ref, *refs):
    high_ref, low_ref, flipped_ref = refs[-3:]
    both = jnp.concatenate([keep_ref[...], send_ref[...]], axis=1)
    high_ref[...], low_ref[...] = split(both)
    high, low = split(both.T)
    width = both.shape[1]
    flipped_ref[:width, :] = high
    flipped_ref[width:, :] = low


def prepare(keep, send, after=()):
    rows, half = keep.shape
    step = min(rows, 512)
    half_spec = pl.BlockSpec((step, half), lambda i: (i, 0))
    spec = pl.BlockSpec((step, 2 * half), lambda i: (i, 0))
    return pl.pallas_call(
        prepare_kernel,
        grid=(rows // step,),
        in_specs=[half_spec, half_spec] + [ANYWHERE] * len(after),
        out_specs=[spec, spec, pl.BlockSpec((4 * half, step), lambda i: (0, i))],
        out_shape=[
            jax.ShapeDtypeStruct((rows, 2 * half), BF16),
            jax.ShapeDtypeStruct((rows, 2 * half), BF16),
            jax.ShapeDtypeStruct((4 * half, rows), BF16),
        ],
        compiler_params=params(16),
        cost_estimate=cost(rows * half * 8, rows * half * 24),
        name="prepare_panel",
    )(keep, send, *after)


def choose_kernel(outputs, count, which_ref, *refs):
    cases, outs, (panel_ref, sem) = refs[:count], refs[-2 - len(outputs) : -2], refs[-2:]
    half = cases[0].shape[1]
    for side in range(2):
        for index, case in enumerate(cases):

            @pl.when(which_ref[side] == index)
            def _(case=case, side=side):
                copy = pltpu.make_async_copy(case, panel_ref.at[:, side * half : (side + 1) * half], sem)
                copy.start()
                copy.wait()

    use = dict(zip(outputs, outs))
    rows, width = panel_ref.shape
    step = min(rows, 256)
    for start in range(0, rows, step):
        here = slice(start, start + step)
        value = panel_ref[here, :]
        high, low = split(value)
        if "high" in use:
            use["high"][here, :] = high
            use["low"][here, :] = low
        if "both" in use:
            use["both"][here, :width] = high
            use["both"][here, width:] = low
        if "flipped" in use:
            high, low = split(value.T)
            use["flipped"][:width, here] = high
            use["flipped"][width:, here] = low


def choose(cases, which, outputs, after=()):
    rows, half = cases[0].shape
    shapes = {"high": (rows, 2 * half), "low": (rows, 2 * half), "both": (rows, 4 * half), "flipped": (4 * half, rows)}
    in_vmem = pl.BlockSpec(memory_space=pltpu.VMEM)
    return pl.pallas_call(
        functools.partial(choose_kernel, outputs, len(cases)),
        in_specs=[pl.BlockSpec(memory_space=pltpu.SMEM)] + [ANYWHERE] * (len(cases) + len(after)),
        out_specs=[in_vmem] * len(outputs),
        out_shape=[jax.ShapeDtypeStruct(shapes[name], BF16) for name in outputs],
        scratch_shapes=[pltpu.VMEM((rows, 2 * half), F32), pltpu.SemaphoreType.DMA],
        compiler_params=params(14),
        cost_estimate=cost(rows * half * 8, rows * half * 24),
        name="choose_panel",
    )(which, *cases, *after)


def products_kernel(first, flipped_ref, both_ref, *refs):
    keep_ref, send_ref, high_block, low_block, sems = refs[-5:]
    half, width = keep_ref.shape
    step = high_block.shape[2]
    copies = []
    for index in range(width // step):
        start = first + index * step
        copies.append([])
        for side, target in enumerate((high_block, low_block)):
            source = both_ref.at[:, start : start + step]
            copies[-1].append(pltpu.make_async_copy(source, target.at[index], sems.at[index, side]))
            start += both_ref.shape[1] // 2
    for pair in copies:
        for copy in pair:
            copy.start()
    for index, pair in enumerate(copies):
        columns = slice(index * step, (index + 1) * step)
        pair[0].wait()
        with_high = dot(flipped_ref[...], high_block[index])
        pair[1].wait()
        with_low = dot(flipped_ref[: 2 * half, :], low_block[index])
        total = with_high[: 2 * half] + (with_high[2 * half :] + with_low)
        keep_ref[:, columns] = total[:half]
        send_ref[:, columns] = total[half:]


def products(flipped, both, block, width, after=()):
    rows = both.shape[0]
    half = flipped.shape[0] // 4
    step = min(width, 256)
    in_vmem = pl.BlockSpec(memory_space=pltpu.VMEM)
    blocks = pltpu.VMEM((width // step, rows, step), BF16)
    return pl.pallas_call(
        functools.partial(products_kernel, block * width),
        in_specs=[in_vmem, IN_HBM] + [ANYWHERE] * len(after),
        out_specs=[in_vmem] * 2,
        out_shape=[jax.ShapeDtypeStruct((half, width), F32)] * 2,
        scratch_shapes=[blocks, blocks, pltpu.SemaphoreType.DMA((width // step, 2))],
        compiler_params=params(49),
        cost_estimate=cost(2 * 6 * half * rows * width, rows * width * 4 + 8 * half * rows),
        name="products",
    )(flipped, both, *after)


def update_kernel(place_ref, *refs):
    sums = refs[:6]
    tfac_ref, gram_ref = refs[6:8]
    high_refs, low_refs = refs[8:11], refs[11:14]
    x_ref = refs[14]
    out_ref, done_ref, w_ref, y_ref, y_split_ref = refs[-5:]
    half = sums[0].shape[0]
    width = 2 * half

    @pl.when(pl.program_id(0) == 0)
    def _():
        for index, piece in enumerate(sums):
            start = pl.multiple_of(place_ref[index] * half, half)
            w_ref[pl.ds(start, half), :] = piece[:, : w_ref.shape[1]]
        first = dot_three(tfac_ref[0], w_ref[:width, :])
        y_ref[:width, :] = first
        second = dot_three(tfac_ref[1], w_ref[width : 2 * width, :] - dot_three(gram_ref[0], first))
        y_ref[width : 2 * width, :] = second
        third = w_ref[2 * width :, :] - dot_three(gram_ref[1], first) - dot_three(gram_ref[2], second)
        y_ref[2 * width :, :] = dot_three(tfac_ref[2], third)
        for index in range(6):
            start = pl.multiple_of(place_ref[index] * half, half)
            high, low = split(y_ref[pl.ds(start, half), :])
            for number, value in enumerate((high, high, low)):
                y_split_ref[(6 * number + index) * half : (6 * number + index + 1) * half, :] = value

    sides = [ref[...] for ref in (*high_refs, *low_refs, *high_refs)]
    out_ref[...] = x_ref[...] - dot(jnp.concatenate(sides, axis=1), y_split_ref[...])
    done_ref[...] = jnp.zeros(done_ref.shape, F32)


def update(place, sums, tfac, grams, highs, lows, x, out, block, width):
    rows, columns = x.shape
    half = sums[0].shape[0]
    step = min(rows, 512)
    panel_spec = pl.BlockSpec((step, 2 * half), lambda i, place: (i, 0))
    block_spec = pl.BlockSpec((step, width), lambda i, place: (i, block))
    operands = [place, *sums, tfac, grams, *highs, *lows, x]
    in_specs = (
        [pl.BlockSpec(memory_space=pltpu.VMEM)] * 8
        + [panel_spec] * 6
        + [block_spec]
    )
    aliases = {}
    if out is not None:
        aliases = {len(operands): 0}
        operands.append(out)
        in_specs.append(IN_HBM)
    return pl.pallas_call(
        update_kernel,
        grid_spec=pltpu.PrefetchScalarGridSpec(
            num_scalar_prefetch=1,
            grid=(rows // step,),
            in_specs=in_specs,
            out_specs=[block_spec, pl.BlockSpec((8, 128), lambda i, place: (0, 0))],
            scratch_shapes=[
                pltpu.VMEM((6 * half, width), F32),
                pltpu.VMEM((6 * half, width), F32),
                pltpu.VMEM((18 * half, width), BF16),
            ],
        ),
        out_shape=[jax.ShapeDtypeStruct(x.shape, F32), jax.ShapeDtypeStruct((8, 128), F32)],
        input_output_aliases=aliases,
        compiler_params=params(40),
        cost_estimate=cost(2 * 18 * half * rows * width, rows * width * 8 + rows * half * 24),
        name="update",
    )(*operands)


def pairs_of(count, step):
    return [(index, index ^ step) for index in range(count)]


def swap_cores(value):
    return lax.ppermute(value, "row", pairs_of(lax.axis_size("row"), 1))


def both_cores(chip_pairs):
    return [(2 * a + core, 2 * b + core) for a, b in chip_pairs for core in range(2)]


def sum_over_rows(keep, send):
    chips = lax.axis_size("row") // 2
    chip = lax.axis_index("row") // 2
    total = keep + swap_cores(send)
    for hop in range(chips // 2 - 1):
        pairs = [(hop, hop + 1), (chips - 1 - hop, chips - 2 - hop)]
        total = total + lax.ppermute(total, "row", both_cores(pairs))
    middle = [(chips // 2 - 1, chips // 2), (chips // 2, chips // 2 - 1)]
    total = total + lax.ppermute(total, "row", both_cores(middle))
    for hop in reversed(range(chips // 2 - 1)):
        pairs = [(hop + 1, hop), (chips - 2 - hop, chips - 1 - hop)]
        arrived = lax.ppermute(total, "row", both_cores(pairs))
        total = jnp.where((chip == hop) | (chip == chips - 1 - hop), arrived, total)
    return total, swap_cores(total)


def pick(index, *cases):
    return lax.select_n(index, *cases)


def fetch_square(slot, roots):
    half = slot.shape[1] // 2
    me = lax.axis_index("col")
    along = lambda value, step: lax.ppermute(value, "col", pairs_of(4, step))
    own = [slot[:, :half], slot[:, half:]]
    near, far = [], []
    for piece in own:
        near.append(along(piece, 1))
        far.append(along(piece, 2))
    cross = [along(far[0], 1), along(near[1], 2)]
    spare = (roots[0] + 3) % 4
    case = me ^ spare
    rounds = [
        ((*own, near[0], far[0]), jnp.array([[2, 3], [0, 1], [0, 1], [0, 1]], jnp.int32)[case]),
        ((*near, *far), jnp.array([[1, 3], [2, 3], [0, 1], [0, 2]], jnp.int32)[case]),
        ((*cross, near[1], far[1]), jnp.array([[0, 1], [0, 1], [0, 1], [2, 3]], jnp.int32)[case]),
    ]
    slots = jnp.array([[1, 2, 1, 2, 3, 3], [0, 0, 2, 2, 3, 3], [0, 0, 1, 1, 3, 3], [0, 0, 1, 2, 1, 2]], jnp.int32)
    halves = jnp.array([[0, 0, 1, 1, 0, 1], [0, 1, 0, 1, 0, 1], [0, 1, 0, 1, 0, 1], [0, 1, 0, 0, 1, 1]], jnp.int32)
    panel = ((slots[case] ^ me) - roots[0]) % 4
    places = panel * 2 + halves[case]
    later_of = jnp.array([[0, 1, 0, 0], [1, 0, 2, 2]], jnp.int32)[roots[0] - 2, me]
    earlier_of = jnp.array([[2, 2, 0, 1], [0, 0, 1, 0]], jnp.int32)[roots[0] - 2, me]
    both = jnp.arange(2, dtype=jnp.int32)
    later = ((*own, *near, *far), 2 * later_of + both)
    earlier = ((*own, *near, *far), 2 * earlier_of + both)
    holders = jnp.array([[3, 0, 1], [2, 3, 0]], jnp.int32)[roots[0] - 2]
    return rounds, places, later, earlier, holders


def fetch_any(slot, roots):
    half = slot.shape[1] // 2
    me = lax.axis_index("col")
    panels = [lax.psum(jnp.where(me == roots[index], slot, jnp.zeros_like(slot)), "col") for index in range(PANELS)]
    rounds = [(panel[:, :half], panel[:, half:]) for panel in panels]
    return rounds, jnp.arange(2 * PANELS, dtype=jnp.int32), panels


def gram(left, right):
    return lax.dot_general(
        left, right, (((0,), (0,)), ((), ())), precision=lax.Precision.HIGH, preferred_element_type=F32
    )


def exchange_kernel(names, pieces, ends_ref, *refs):
    use = dict(zip(names, refs))
    end = ends_ref[0] == 1
    if "acc" in use:
        start = 0
        for index in range(pieces):
            keep, swapped = use["keep", index], use["swapped", index]
            columns = slice(start, start + keep.shape[1])
            use["acc"][:, columns] = keep[...] + swapped[...]
            start = columns.stop
    if "part" in use:
        columns = use["part"].shape[1]
        use["part"][...] = use["acc_before"][...] + use["outer"][:, :columns]
    if "total" in use:
        use["total"][...] = use["part_before"][...] + use["inner"][...]
    if "final" in use:
        columns = use["final"].shape[1]
        use["final"][...] = jnp.where(end, use["outer"][:, :columns], use["total_before"][...])
    if "out" in use:
        sources = [use[name] for name in ("acc", "total") if name in use]
        if len(sources) == 1:
            use["out"][...] = sources[0][...]
        else:
            both = min(source.shape[1] for source in sources)
            use["out"][:, :both] = jnp.where(end, sources[0][:, :both], sources[1][:, :both])
            for source in sources:
                if source.shape[1] > both:
                    use["out"][:, both:] = source[:, both:]


def exchange(ends, operands, shapes, after):
    names = list(operands) + [None] * len(after) + list(shapes)
    pieces = sum(name[0] == "keep" for name in operands)
    in_vmem = pl.BlockSpec(memory_space=pltpu.VMEM)
    results = pl.pallas_call(
        functools.partial(exchange_kernel, names, pieces),
        in_specs=[pl.BlockSpec(memory_space=pltpu.SMEM)] + [in_vmem] * len(operands)
        + [ANYWHERE] * len(after),
        out_specs=[in_vmem] * len(shapes),
        out_shape=[jax.ShapeDtypeStruct(shape, F32) for shape in shapes.values()],
        compiler_params=params(14),
        cost_estimate=cost(0, 0),
        name="exchange",
    )(ends, *operands.values(), *after)
    return dict(zip(shapes, results))


def shards_square(eigvec, slot, roots, tfac):
    columns = eigvec.shape[1]
    width = columns // 2
    rounds, places, later, earlier, holders = fetch_square(slot, roots)
    chip, core = lax.axis_index("row") // 2, lax.axis_index("row") % 2
    ends = jnp.where((chip == 0) | (chip == 3), 1, 0).astype(jnp.int32).reshape(1)
    places = jnp.where(core == 0, places, places.reshape(PANELS, 2)[:, ::-1].reshape(-1))
    ordered = lambda pair: jnp.where(core == 0, pair, pair[::-1])
    x_both = split_array(eigvec)
    chunks = [(index, block) for index in range(PANELS) for block in range(columns // width)]
    count = len(chunks)
    gram_chunk = 2
    prepared, arrived, sizes = {}, {}, {}
    half = slot.shape[1] // 2

    def start(number, after):
        index, block = chunks[number]
        pieces = []
        if index not in prepared:
            cases, which = rounds[index]
            prepared[index] = choose(cases, ordered(which), ("high", "low", "flipped"), after)
        for part in range(width // PIECE):
            pieces.append(products(prepared[index][2], x_both, block * (width // PIECE) + part, PIECE, after))
        if number == gram_chunk:
            (flipped,) = choose(later[0], ordered(later[1]), ("flipped",), after)
            (both,) = choose(*earlier, ("both",), after)
            pieces.append(products(flipped, both, 0, 2 * half))
        arrived[number] = [(mine, swap_cores(other)) for mine, other in pieces]
        sizes[number] = (half, sum(mine.shape[1] for mine, other in pieces))

    outer_pairs = both_cores([(0, 1), (1, 0), (2, 3), (3, 2)])
    inner_pairs = both_cores([(1, 2), (2, 1)])
    acc, part, total, outer, inner, sums = {}, {}, {}, {}, {}, {}
    grams, out = None, None
    start(0, ())
    for step in range(count + 3 * LAG):
        operands, shapes = {}, {}
        inward, middle, outward = step - LAG, step - 2 * LAG, step - 3 * LAG
        if step < count:
            for number, (mine, other) in enumerate(arrived[step]):
                operands["keep", number], operands["swapped", number] = mine, other
            shapes["acc"] = sizes[step]
        if step - LAG in outer:
            operands["outer"] = outer[step - LAG]
        if 0 <= inward < count:
            operands["acc_before"] = acc[inward]
            shapes["part"] = sizes[inward]
        if 0 <= middle < count:
            operands["part_before"], operands["inner"] = part[middle], inner[step - LAG]
            shapes["total"] = sizes[middle]
        if 0 <= outward < count:
            operands["total_before"] = total[outward]
            shapes["final"] = sizes[outward]
        sent = [shapes[name] for name in ("acc", "total") if name in shapes]
        if sent:
            shapes["out"] = max(sent, key=lambda shape: shape[1])
        ahead = [] if out is None else [finished]
        if step + 1 == chunks.index((PANELS - 1, 0)):
            ahead.extend(rounds[-1][0][:2])
        if step == count + 1:
            ahead.append(grams)
        if 0 <= outward - 1 < count - 2:
            ahead.append(sums[chunks[outward - 1]][1])
        results = exchange(ends, operands, shapes, ahead)
        if "out" in results:
            outer[step] = lax.ppermute(results["out"], "row", outer_pairs)
        if "acc" in results:
            acc[step] = results["acc"]
        if "part" in results:
            part[inward] = results["part"]
            inner[step] = lax.ppermute(results["part"], "row", inner_pairs)
        if "total" in results:
            total[middle] = results["total"]
        if step + 1 < count:
            start(step + 1, [next(iter(results.values()))])
        if "final" in results:
            done = outward
            own, other = results["final"], swap_cores(results["final"])
            if done == gram_chunk:
                pair = own[:, width:], other[:, width:]
                block = jnp.where(core == 0, jnp.concatenate(pair, axis=0), jnp.concatenate(pair[::-1], axis=0))
                spread = [block] + [lax.ppermute(block, "col", pairs_of(4, shift)) for shift in range(1, 4)]
                places_of = holders ^ lax.axis_index("col")
                grams = jnp.stack([pick(places_of[number], *spread) for number in range(PANELS)])
            sums[chunks[done]] = (own, other)
            index, block = chunks[done]
            if index == PANELS - 1:
                pieces = [piece for panel in range(PANELS) for piece in sums[panel, block]]
                highs, lows = zip(*[prepared[panel][:2] for panel in range(PANELS)])
                out, finished = update(places, pieces, tfac, grams, highs, lows, eigvec, out, block, width)
    return out


def shards(eigvec, slots, roots, tfac):
    if lax.axis_size("col") == 4 and lax.axis_size("row") == 8:
        return shards_square(eigvec, slots[0], roots, tfac)
    columns = eigvec.shape[1]
    width = min(columns, BLOCK)
    rounds, places, panels = fetch_any(slots[0], roots)
    core = lax.axis_index("row") % 2
    places = jnp.where(core == 0, places, places.reshape(PANELS, 2)[:, ::-1].reshape(-1))
    x_both = split_array(eigvec)
    highs, lows, sums = [], [], []
    for first, second in rounds:
        keep = jnp.where(core == 0, first, second)
        send = jnp.where(core == 0, second, first)
        high, low, flipped = prepare(keep, send)
        highs.append(high)
        lows.append(low)
        sums.append([
            sum_over_rows(*products(flipped, x_both, block, width)) for block in range(columns // width)
        ])
    grams = jnp.stack([gram(panels[1], panels[0]), gram(panels[2], panels[0]), gram(panels[2], panels[1])])
    grams = lax.psum(grams, "row")
    out = None
    for block in range(columns // width):
        pieces = [piece for index in range(PANELS) for piece in sums[index][block]]
        out, _ = update(places, pieces, tfac, grams, highs, lows, eigvec, out, block, width)
    return out


def solution(mesh):
    in_specs = (P("row", "col"), P("col", "row", None), P(), P())
    out_specs = P("row", "col")
    return jax.shard_map(shards, mesh=mesh, in_specs=in_specs, out_specs=out_specs, check_vma=False)
```

```python
import functools

import jax
import jax.numpy as jnp
from jax import lax
from jax.experimental import pallas as pl
from jax.experimental.pallas import tpu as pltpu
from jax.sharding import PartitionSpec as P

PANELS = 3
BLOCK = 512
LAG = 1
PIECE = 512
MIB = 1024 * 1024
F32 = jnp.float32
BF16 = jnp.bfloat16
ANYWHERE = pl.BlockSpec(memory_space=pl.ANY)
IN_HBM = pl.BlockSpec(memory_space=pltpu.HBM)


def split(value):
    high = value.astype(BF16)
    return high, (value - high.astype(F32)).astype(BF16)


def dot(left, right):
    return jnp.dot(left, right, preferred_element_type=F32)


def dot_three(left, right):
    left_high, left_low = split(left)
    right_high, right_low = split(right)
    return dot(
        jnp.concatenate([left_high, left_low, left_high], axis=1),
        jnp.concatenate([right_high, right_high, right_low], axis=0),
    )


def params(mib):
    return pltpu.CompilerParams(vmem_limit_bytes=mib * MIB)


def cost(flops, count):
    return pl.CostEstimate(flops=flops // 64, bytes_accessed=count // 64, transcendentals=0)


def pinned(value):
    return pltpu.with_memory_space_constraint(value, memory_space=pltpu.HBM)


def split_kernel(x_ref, both_ref):
    blocks, _, _, width = both_ref.shape
    for index in range(blocks):
        both_ref[index, 0], both_ref[index, 1] = split(x_ref[:, index * width : (index + 1) * width])


def split_array(x, width):
    rows, columns = x.shape
    step, blocks = min(rows, 256), columns // width
    return pl.pallas_call(
        split_kernel,
        grid=(rows // step,),
        in_specs=[pl.BlockSpec((step, columns), lambda i: (i, 0))],
        out_specs=pl.BlockSpec((blocks, 2, step, width), lambda i: (0, 0, i, 0)),
        out_shape=pltpu.HBM((blocks, 2, rows, width), BF16),
        compiler_params=params(49),
        cost_estimate=cost(rows * columns * 4, rows * columns * 8),
        name="split_x",
    )(x)


def choose_kernel(outputs, count, which_ref, *refs):
    cases, (panel_ref, split_ref, sem) = refs[:count], refs[-3:]
    use = dict(zip(outputs, refs[-3 - len(outputs) :]))
    half = cases[0].shape[1]
    for side in range(2):
        for index, case in enumerate(cases):

            @pl.when(which_ref[side] == index)
            def _(case=case, side=side):
                copy = pltpu.make_async_copy(case, panel_ref.at[:, side * half : (side + 1) * half], sem)
                copy.start()
                copy.wait()

    rows, width = panel_ref.shape
    step = min(rows, 256)
    for start in range(0, rows, step):
        here = slice(start, start + step)
        value = panel_ref[here, :]
        if "both" in use:
            split_ref[0, 0, here, :], split_ref[0, 1, here, :] = split(value)
        if "flipped" in use:
            high, low = split(value.T)
            use["flipped"][:width, here] = high
            use["flipped"][width:, here] = low
    if "both" in use:
        copy = pltpu.make_async_copy(split_ref, use["both"], sem)
        copy.start()
        copy.wait()


def choose(cases, which, outputs, after=()):
    rows, half = cases[0].shape
    shapes = {"both": (1, 2, rows, 2 * half), "flipped": (4 * half, rows)}
    spaces = {"both": pltpu.HBM, "flipped": pltpu.VMEM}
    return pl.pallas_call(
        functools.partial(choose_kernel, outputs, len(cases)),
        in_specs=[pl.BlockSpec(memory_space=pltpu.SMEM)] + [ANYWHERE] * (len(cases) + len(after)),
        out_specs=[pl.BlockSpec(memory_space=spaces[name]) for name in outputs],
        out_shape=[spaces[name](shapes[name], BF16) for name in outputs],
        scratch_shapes=[
            pltpu.VMEM((rows, 2 * half), F32),
            pltpu.VMEM(shapes["both"], BF16),
            pltpu.SemaphoreType.DMA,
        ],
        compiler_params=params(14),
        cost_estimate=cost(rows * half * 8, rows * half * 24),
        name="choose_panel",
    )(which, *cases, *after)


def products_kernel(first, flipped_ref, both_ref, *refs):
    keep_ref, send_ref, block_ref, sems = refs[-4:]
    half = keep_ref.shape[0]
    count, step = block_ref.shape[0], block_ref.shape[3]
    copies = []
    for index in range(count):
        for side in range(2):
            source, target = both_ref.at[first + index, side], block_ref.at[index, side]
            copies.append(pltpu.make_async_copy(source, target, sems.at[index, side]))
            copies[-1].start()
    for index in range(count):
        columns = slice(index * step, (index + 1) * step)
        copies[2 * index].wait()
        with_high = dot(flipped_ref[...], block_ref[index, 0])
        copies[2 * index + 1].wait()
        with_low = dot(flipped_ref[: 2 * half, :], block_ref[index, 1])
        total = with_high[: 2 * half] + (with_high[2 * half :] + with_low)
        keep_ref[:, columns] = total[:half]
        send_ref[:, columns] = total[half:]


def products(flipped, both, block, width, after=()):
    rows, step = both.shape[2:]
    half, count = flipped.shape[0] // 4, width // step
    in_vmem = pl.BlockSpec(memory_space=pltpu.VMEM)
    return pl.pallas_call(
        functools.partial(products_kernel, block * count),
        in_specs=[in_vmem, IN_HBM] + [ANYWHERE] * len(after),
        out_specs=[in_vmem] * 2,
        out_shape=[jax.ShapeDtypeStruct((half, width), F32)] * 2,
        scratch_shapes=[pltpu.VMEM((count, 2, rows, step), BF16), pltpu.SemaphoreType.DMA((count, 2))],
        compiler_params=params(16),
        cost_estimate=cost(2 * 6 * half * rows * width, rows * width * 4 + 8 * half * rows),
        name="products",
    )(flipped, pinned(both), *after)


def update_kernel(place_ref, *refs):
    sums = refs[:6]
    tfac_ref, gram_ref = refs[6:8]
    panel_refs, x_ref = refs[8:11], refs[11]
    out_ref, done_ref, w_ref, y_ref, y_split_ref = refs[-5:]
    half = sums[0].shape[0]
    width = 2 * half

    @pl.when(pl.program_id(0) == 0)
    def _():
        for index, piece in enumerate(sums):
            start = pl.multiple_of(place_ref[index] * half, half)
            w_ref[pl.ds(start, half), :] = piece[:, : w_ref.shape[1]]
        first = dot_three(tfac_ref[0], w_ref[:width, :])
        y_ref[:width, :] = first
        second = dot_three(tfac_ref[1], w_ref[width : 2 * width, :] - dot_three(gram_ref[0], first))
        y_ref[width : 2 * width, :] = second
        third = w_ref[2 * width :, :] - dot_three(gram_ref[1], first) - dot_three(gram_ref[2], second)
        y_ref[2 * width :, :] = dot_three(tfac_ref[2], third)
        for index in range(6):
            start = pl.multiple_of(place_ref[index] * half, half)
            high, low = split(y_ref[pl.ds(start, half), :])
            for number, value in enumerate((high, high, low)):
                y_split_ref[(6 * number + index) * half : (6 * number + index + 1) * half, :] = value

    sides = [ref[0, side] for side in (0, 1, 0) for ref in panel_refs]
    out_ref[...] = x_ref[...] - dot(jnp.concatenate(sides, axis=1), y_split_ref[...])
    done_ref[...] = jnp.zeros(done_ref.shape, F32)


def update(place, sums, tfac, grams, panels, x, out, block, width):
    rows, columns = x.shape
    half = sums[0].shape[0]
    step = min(rows, 512)
    panel_spec = pl.BlockSpec((1, 2, step, 2 * half), lambda i, place: (0, 0, i, 0))
    block_spec = pl.BlockSpec((step, width), lambda i, place: (i, block))
    operands = [place, *sums, tfac, grams, *map(pinned, panels), x]
    in_specs = (
        [pl.BlockSpec(memory_space=pltpu.VMEM)] * 8
        + [panel_spec] * 3
        + [block_spec]
    )
    aliases = {}
    if out is not None:
        aliases = {len(operands): 0}
        operands.append(out)
        in_specs.append(IN_HBM)
    return pl.pallas_call(
        update_kernel,
        grid_spec=pltpu.PrefetchScalarGridSpec(
            num_scalar_prefetch=1,
            grid=(rows // step,),
            in_specs=in_specs,
            out_specs=[block_spec, pl.BlockSpec((8, 128), lambda i, place: (0, 0))],
            scratch_shapes=[
                pltpu.VMEM((6 * half, width), F32),
                pltpu.VMEM((6 * half, width), F32),
                pltpu.VMEM((18 * half, width), BF16),
            ],
        ),
        out_shape=[jax.ShapeDtypeStruct(x.shape, F32), jax.ShapeDtypeStruct((8, 128), F32)],
        input_output_aliases=aliases,
        compiler_params=params(40),
        cost_estimate=cost(2 * 18 * half * rows * width, rows * width * 8 + rows * half * 24),
        name="update",
    )(*operands)


def pairs_of(count, step):
    return [(index, index ^ step) for index in range(count)]


def swap_cores(value):
    return lax.ppermute(value, "row", pairs_of(lax.axis_size("row"), 1))


def both_cores(chip_pairs):
    return [(2 * a + core, 2 * b + core) for a, b in chip_pairs for core in range(2)]


def sum_over_rows(keep, send):
    chips = lax.axis_size("row") // 2
    chip = lax.axis_index("row") // 2
    total = keep + swap_cores(send)
    for hop in range(chips // 2 - 1):
        pairs = [(hop, hop + 1), (chips - 1 - hop, chips - 2 - hop)]
        total = total + lax.ppermute(total, "row", both_cores(pairs))
    middle = [(chips // 2 - 1, chips // 2), (chips // 2, chips // 2 - 1)]
    total = total + lax.ppermute(total, "row", both_cores(middle))
    for hop in reversed(range(chips // 2 - 1)):
        pairs = [(hop + 1, hop), (chips - 2 - hop, chips - 1 - hop)]
        arrived = lax.ppermute(total, "row", both_cores(pairs))
        total = jnp.where((chip == hop) | (chip == chips - 1 - hop), arrived, total)
    return total, swap_cores(total)


def pick(index, *cases):
    return lax.select_n(index, *cases)


def fetch_square(slot, roots):
    half = slot.shape[1] // 2
    me = lax.axis_index("col")
    along = lambda value, step: lax.ppermute(value, "col", pairs_of(4, step))
    own = [slot[:, :half], slot[:, half:]]
    near, far = [], []
    for piece in own:
        near.append(along(piece, 1))
        far.append(along(piece, 2))
    cross = [along(far[0], 1), along(near[1], 2)]
    spare = (roots[0] + 3) % 4
    case = me ^ spare
    rounds = [
        ((*own, near[0], far[0]), jnp.array([[2, 3], [0, 1], [0, 1], [0, 1]], jnp.int32)[case]),
        ((*near, *far), jnp.array([[1, 3], [2, 3], [0, 1], [0, 2]], jnp.int32)[case]),
        ((*cross, near[1], far[1]), jnp.array([[0, 1], [0, 1], [0, 1], [2, 3]], jnp.int32)[case]),
    ]
    slots = jnp.array([[1, 2, 1, 2, 3, 3], [0, 0, 2, 2, 3, 3], [0, 0, 1, 1, 3, 3], [0, 0, 1, 2, 1, 2]], jnp.int32)
    halves = jnp.array([[0, 0, 1, 1, 0, 1], [0, 1, 0, 1, 0, 1], [0, 1, 0, 1, 0, 1], [0, 1, 0, 0, 1, 1]], jnp.int32)
    panel = ((slots[case] ^ me) - roots[0]) % 4
    places = panel * 2 + halves[case]
    later_of = jnp.array([[0, 1, 0, 0], [1, 0, 2, 2]], jnp.int32)[roots[0] - 2, me]
    earlier_of = jnp.array([[2, 2, 0, 1], [0, 0, 1, 0]], jnp.int32)[roots[0] - 2, me]
    both = jnp.arange(2, dtype=jnp.int32)
    later = ((*own, *near, *far), 2 * later_of + both)
    earlier = ((*own, *near, *far), 2 * earlier_of + both)
    holders = jnp.array([[3, 0, 1], [2, 3, 0]], jnp.int32)[roots[0] - 2]
    return rounds, places, later, earlier, holders


def fetch_any(slot, roots):
    half = slot.shape[1] // 2
    me = lax.axis_index("col")
    panels = [lax.psum(jnp.where(me == roots[index], slot, jnp.zeros_like(slot)), "col") for index in range(PANELS)]
    rounds = [(panel[:, :half], panel[:, half:]) for panel in panels]
    return rounds, jnp.arange(2 * PANELS, dtype=jnp.int32), panels


def gram(left, right):
    return lax.dot_general(
        left, right, (((0,), (0,)), ((), ())), precision=lax.Precision.HIGH, preferred_element_type=F32
    )


def exchange_kernel(names, pieces, ends_ref, *refs):
    use = dict(zip(names, refs))
    end = ends_ref[0] == 1
    if "acc" in use:
        start = 0
        for index in range(pieces):
            keep, swapped = use["keep", index], use["swapped", index]
            columns = slice(start, start + keep.shape[1])
            use["acc"][:, columns] = keep[...] + swapped[...]
            start = columns.stop
    if "part" in use:
        columns = use["part"].shape[1]
        use["part"][...] = use["acc_before"][...] + use["outer"][:, :columns]
    if "total" in use:
        use["total"][...] = use["part_before"][...] + use["inner"][...]
    if "final" in use:
        columns = use["final"].shape[1]
        use["final"][...] = jnp.where(end, use["outer"][:, :columns], use["total_before"][...])
    if "out" in use:
        sources = [use[name] for name in ("acc", "total") if name in use]
        if len(sources) == 1:
            use["out"][...] = sources[0][...]
        else:
            both = min(source.shape[1] for source in sources)
            use["out"][:, :both] = jnp.where(end, sources[0][:, :both], sources[1][:, :both])
            for source in sources:
                if source.shape[1] > both:
                    use["out"][:, both:] = source[:, both:]


def exchange(ends, operands, shapes, after):
    names = list(operands) + [None] * len(after) + list(shapes)
    pieces = sum(name[0] == "keep" for name in operands)
    in_vmem = pl.BlockSpec(memory_space=pltpu.VMEM)
    results = pl.pallas_call(
        functools.partial(exchange_kernel, names, pieces),
        in_specs=[pl.BlockSpec(memory_space=pltpu.SMEM)] + [in_vmem] * len(operands)
        + [ANYWHERE] * len(after),
        out_specs=[in_vmem] * len(shapes),
        out_shape=[jax.ShapeDtypeStruct(shape, F32) for shape in shapes.values()],
        compiler_params=params(14),
        cost_estimate=cost(0, 0),
        name="exchange",
    )(ends, *operands.values(), *after)
    return dict(zip(shapes, results))


def shards_square(eigvec, slot, roots, tfac):
    columns = eigvec.shape[1]
    width, half = columns // 2, slot.shape[1] // 2
    rounds, places, later, earlier, holders = fetch_square(slot, roots)
    chip, core = lax.axis_index("row") // 2, lax.axis_index("row") % 2
    ends = jnp.where((chip == 0) | (chip == 3), 1, 0).astype(jnp.int32).reshape(1)
    places = jnp.where(core == 0, places, places.reshape(PANELS, 2)[:, ::-1].reshape(-1))
    ordered = lambda pair: jnp.where(core == 0, pair, pair[::-1])
    x_both = split_array(eigvec, 2 * half)
    chunks = [(index, block) for index in range(PANELS) for block in range(columns // width)]
    count = len(chunks)
    gram_chunk = 2
    prepared, arrived, sizes = {}, {}, {}

    def start(number, after):
        index, block = chunks[number]
        pieces = []
        if index not in prepared:
            cases, which = rounds[index]
            prepared[index] = choose(cases, ordered(which), ("both", "flipped"), after)
        for part in range(width // PIECE):
            pieces.append(products(prepared[index][1], x_both, block * (width // PIECE) + part, PIECE, after))
        if number == gram_chunk:
            (flipped,) = choose(later[0], ordered(later[1]), ("flipped",), after)
            (both,) = choose(*earlier, ("both",), after)
            pieces.append(products(flipped, both, 0, 2 * half))
        arrived[number] = [(mine, swap_cores(other)) for mine, other in pieces]
        sizes[number] = (half, sum(mine.shape[1] for mine, other in pieces))

    outer_pairs = both_cores([(0, 1), (1, 0), (2, 3), (3, 2)])
    inner_pairs = both_cores([(1, 2), (2, 1)])
    acc, part, total, outer, inner, sums = {}, {}, {}, {}, {}, {}
    grams, out = None, None
    start(0, ())
    for step in range(count + 3 * LAG):
        operands, shapes = {}, {}
        inward, middle, outward = step - LAG, step - 2 * LAG, step - 3 * LAG
        if step < count:
            for number, (mine, other) in enumerate(arrived[step]):
                operands["keep", number], operands["swapped", number] = mine, other
            shapes["acc"] = sizes[step]
        if step - LAG in outer:
            operands["outer"] = outer[step - LAG]
        if 0 <= inward < count:
            operands["acc_before"] = acc[inward]
            shapes["part"] = sizes[inward]
        if 0 <= middle < count:
            operands["part_before"], operands["inner"] = part[middle], inner[step - LAG]
            shapes["total"] = sizes[middle]
        if 0 <= outward < count:
            operands["total_before"] = total[outward]
            shapes["final"] = sizes[outward]
        sent = [shapes[name] for name in ("acc", "total") if name in shapes]
        if sent:
            shapes["out"] = max(sent, key=lambda shape: shape[1])
        ahead = [] if out is None else [finished]
        if step + 1 == chunks.index((PANELS - 1, 0)):
            ahead.extend(rounds[-1][0][:2])
        if step == count + 1:
            ahead.append(grams)
        if 0 <= outward - 1 < count - 2:
            ahead.append(sums[chunks[outward - 1]][1])
        results = exchange(ends, operands, shapes, ahead)
        if "out" in results:
            outer[step] = lax.ppermute(results["out"], "row", outer_pairs)
        if "acc" in results:
            acc[step] = results["acc"]
        if "part" in results:
            part[inward] = results["part"]
            inner[step] = lax.ppermute(results["part"], "row", inner_pairs)
        if "total" in results:
            total[middle] = results["total"]
        if step + 1 < count:
            start(step + 1, [next(iter(results.values()))])
        if "final" in results:
            done = outward
            own, other = results["final"], swap_cores(results["final"])
            if done == gram_chunk:
                pair = own[:, width:], other[:, width:]
                block = jnp.where(core == 0, jnp.concatenate(pair, axis=0), jnp.concatenate(pair[::-1], axis=0))
                spread = [block] + [lax.ppermute(block, "col", pairs_of(4, shift)) for shift in range(1, 4)]
                places_of = holders ^ lax.axis_index("col")
                grams = jnp.stack([pick(places_of[number], *spread) for number in range(PANELS)])
            sums[chunks[done]] = (own, other)
            index, block = chunks[done]
            if index == PANELS - 1:
                pieces = [piece for panel in range(PANELS) for piece in sums[panel, block]]
                panels = [prepared[panel][0] for panel in range(PANELS)]
                out, finished = update(places, pieces, tfac, grams, panels, eigvec, out, block, width)
    return out


def shards(eigvec, slots, roots, tfac):
    if lax.axis_size("col") == 4 and lax.axis_size("row") == 8:
        return shards_square(eigvec, slots[0], roots, tfac)
    columns = eigvec.shape[1]
    width = min(columns, BLOCK)
    rounds, places, panels = fetch_any(slots[0], roots)
    core = lax.axis_index("row") % 2
    places = jnp.where(core == 0, places, places.reshape(PANELS, 2)[:, ::-1].reshape(-1))
    x_both = split_array(eigvec, slots.shape[2])
    prepared, sums = [], []
    for pair in rounds:
        which = jnp.where(core == 0, jnp.arange(2), jnp.arange(1, -1, -1)).astype(jnp.int32)
        prepared.append(choose(pair, which, ("both", "flipped")))
        sums.append([
            sum_over_rows(*products(prepared[-1][1], x_both, block, width)) for block in range(columns // width)
        ])
    grams = jnp.stack([gram(panels[1], panels[0]), gram(panels[2], panels[0]), gram(panels[2], panels[1])])
    grams = lax.psum(grams, "row")
    out = None
    for block in range(columns // width):
        pieces = [piece for index in range(PANELS) for piece in sums[index][block]]
        out, _ = update(places, pieces, tfac, grams, [both for both, _ in prepared], eigvec, out, block, width)
    return out


def solution(mesh):
    in_specs = (P("row", "col"), P("col", "row", None), P(), P())
    out_specs = P("row", "col")
    return jax.shard_map(shards, mesh=mesh, in_specs=in_specs, out_specs=out_specs, check_vma=False)
```

```python
import functools

import jax
import jax.numpy as jnp
from jax import lax
from jax.experimental import pallas as pl
from jax.experimental.pallas import tpu as pltpu
from jax.sharding import PartitionSpec as P

PANELS = 3
BLOCK = 512
LAG = 1
PIECE = 512
MIB = 1024 * 1024
F32 = jnp.float32
BF16 = jnp.bfloat16
ANYWHERE = pl.BlockSpec(memory_space=pl.ANY)
IN_HBM = pl.BlockSpec(memory_space=pltpu.HBM)


def split(value):
    high = value.astype(BF16)
    return high, (value - high.astype(F32)).astype(BF16)


def dot(left, right):
    return jnp.dot(left, right, preferred_element_type=F32)


def dot_three(left, right):
    left_high, left_low = split(left)
    right_high, right_low = split(right)
    return dot(
        jnp.concatenate([left_high, left_low, left_high], axis=1),
        jnp.concatenate([right_high, right_high, right_low], axis=0),
    )


def params(mib):
    return pltpu.CompilerParams(vmem_limit_bytes=mib * MIB)


def cost(flops, count):
    return pl.CostEstimate(flops=flops // 64, bytes_accessed=count // 64, transcendentals=0)


def pinned(value):
    return pltpu.with_memory_space_constraint(value, memory_space=pltpu.HBM)


def split_kernel(x_ref, both_ref):
    blocks, _, _, width = both_ref.shape
    for index in range(blocks):
        both_ref[index, 0], both_ref[index, 1] = split(x_ref[:, index * width : (index + 1) * width])


def split_array(x, width):
    rows, columns = x.shape
    step, blocks = min(rows, 256), columns // width
    return pl.pallas_call(
        split_kernel,
        grid=(rows // step,),
        in_specs=[pl.BlockSpec((step, columns), lambda i: (i, 0))],
        out_specs=pl.BlockSpec((blocks, 2, step, width), lambda i: (0, 0, i, 0)),
        out_shape=pltpu.HBM((blocks, 2, rows, width), BF16),
        compiler_params=params(49),
        cost_estimate=cost(rows * columns * 4, rows * columns * 8),
        name="split_x",
    )(x)


def choose_kernel(outputs, count, which_ref, *refs):
    cases, (panel_ref, split_ref, sem) = refs[:count], refs[-3:]
    use = dict(zip(outputs, refs[-3 - len(outputs) :]))
    half = cases[0].shape[1]
    for side in range(2):
        for index, case in enumerate(cases):

            @pl.when(which_ref[side] == index)
            def _(case=case, side=side):
                copy = pltpu.make_async_copy(case, panel_ref.at[:, side * half : (side + 1) * half], sem)
                copy.start()
                copy.wait()

    rows, width = panel_ref.shape
    step = min(rows, 256)
    for start in range(0, rows, step):
        here = slice(start, start + step)
        value = panel_ref[here, :]
        if "both" in use:
            split_ref[0, 0, here, :], split_ref[0, 1, here, :] = split(value)
        if "flipped" in use:
            high, low = split(value.T)
            use["flipped"][:width, here] = high
            use["flipped"][width:, here] = low
    if "both" in use:
        copy = pltpu.make_async_copy(split_ref, use["both"], sem)
        copy.start()
        copy.wait()


def choose(cases, which, outputs, after=()):
    rows, half = cases[0].shape
    shapes = {"both": (1, 2, rows, 2 * half), "flipped": (4 * half, rows)}
    spaces = {"both": pltpu.HBM, "flipped": pltpu.VMEM}
    return pl.pallas_call(
        functools.partial(choose_kernel, outputs, len(cases)),
        in_specs=[pl.BlockSpec(memory_space=pltpu.SMEM)] + [ANYWHERE] * (len(cases) + len(after)),
        out_specs=[pl.BlockSpec(memory_space=spaces[name]) for name in outputs],
        out_shape=[spaces[name](shapes[name], BF16) for name in outputs],
        scratch_shapes=[
            pltpu.VMEM((rows, 2 * half), F32),
            pltpu.VMEM(shapes["both"], BF16),
            pltpu.SemaphoreType.DMA,
        ],
        compiler_params=params(14),
        cost_estimate=cost(rows * half * 8, rows * half * 24),
        name="choose_panel",
    )(which, *cases, *after)


def products_kernel(block, flipped_ref, both_ref, *refs):
    keep_ref, send_ref, block_ref, sems = refs[-4:]
    half = keep_ref.shape[0]
    rows = block_ref.shape[1] // 2
    copies = []
    for index in range(2):
        here = slice(index * rows, (index + 1) * rows)
        for side in range(2):
            source, target = both_ref.at[block, side, here], block_ref.at[side, here]
            copies.append(pltpu.make_async_copy(source, target, sems.at[index, side]))
            copies[-1].start()
    total = None
    for index in range(2):
        here = slice(index * rows, (index + 1) * rows)
        copies[2 * index].wait()
        with_high = dot(flipped_ref[:, here], block_ref[0, here, :])
        copies[2 * index + 1].wait()
        with_low = dot(flipped_ref[: 2 * half, here], block_ref[1, here, :])
        part = with_high[: 2 * half] + (with_high[2 * half :] + with_low)
        total = part if total is None else total + part
    keep_ref[...] = total[:half]
    send_ref[...] = total[half:]


def products(flipped, both, block, after=()):
    rows, width = both.shape[2:]
    half = flipped.shape[0] // 4
    in_vmem = pl.BlockSpec(memory_space=pltpu.VMEM)
    return pl.pallas_call(
        functools.partial(products_kernel, block),
        in_specs=[in_vmem, IN_HBM] + [ANYWHERE] * len(after),
        out_specs=[in_vmem] * 2,
        out_shape=[jax.ShapeDtypeStruct((half, width), F32)] * 2,
        scratch_shapes=[pltpu.VMEM((2, rows, width), BF16), pltpu.SemaphoreType.DMA((2, 2))],
        compiler_params=params(16),
        cost_estimate=cost(2 * 6 * half * rows * width, rows * width * 4 + 8 * half * rows),
        name="products",
    )(flipped, pinned(both), *after)


def update_kernel(place_ref, *refs):
    sums = refs[:6]
    tfac_ref, gram_ref = refs[6:8]
    panel_refs, x_ref = refs[8:11], refs[11]
    out_ref, done_ref, w_ref, y_ref, y_split_ref = refs[-5:]
    half = sums[0].shape[0]
    width = 2 * half

    @pl.when(pl.program_id(0) == 0)
    def _():
        for index, piece in enumerate(sums):
            start = pl.multiple_of(place_ref[index] * half, half)
            w_ref[pl.ds(start, half), :] = piece[:, : w_ref.shape[1]]
        first = dot_three(tfac_ref[0], w_ref[:width, :])
        y_ref[:width, :] = first
        second = dot_three(tfac_ref[1], w_ref[width : 2 * width, :] - dot_three(gram_ref[0], first))
        y_ref[width : 2 * width, :] = second
        third = w_ref[2 * width :, :] - dot_three(gram_ref[1], first) - dot_three(gram_ref[2], second)
        y_ref[2 * width :, :] = dot_three(tfac_ref[2], third)
        for index in range(6):
            start = pl.multiple_of(place_ref[index] * half, half)
            high, low = split(y_ref[pl.ds(start, half), :])
            for number, value in enumerate((high, high, low)):
                y_split_ref[(6 * number + index) * half : (6 * number + index + 1) * half, :] = value

    sides = [ref[0, side] for side in (0, 1, 0) for ref in panel_refs]
    out_ref[...] = x_ref[...] - dot(jnp.concatenate(sides, axis=1), y_split_ref[...])
    done_ref[...] = jnp.zeros(done_ref.shape, F32)


def update(place, sums, tfac, grams, panels, x, out, block, width):
    rows, columns = x.shape
    half = sums[0].shape[0]
    step = min(rows, 512)
    panel_spec = pl.BlockSpec((1, 2, step, 2 * half), lambda i, place: (0, 0, i, 0))
    block_spec = pl.BlockSpec((step, width), lambda i, place: (i, block))
    operands = [place, *sums, tfac, grams, *map(pinned, panels), x]
    in_specs = (
        [pl.BlockSpec(memory_space=pltpu.VMEM)] * 8
        + [panel_spec] * 3
        + [block_spec]
    )
    aliases = {}
    if out is not None:
        aliases = {len(operands): 0}
        operands.append(out)
        in_specs.append(IN_HBM)
    return pl.pallas_call(
        update_kernel,
        grid_spec=pltpu.PrefetchScalarGridSpec(
            num_scalar_prefetch=1,
            grid=(rows // step,),
            in_specs=in_specs,
            out_specs=[block_spec, pl.BlockSpec((8, 128), lambda i, place: (0, 0))],
            scratch_shapes=[
                pltpu.VMEM((6 * half, width), F32),
                pltpu.VMEM((6 * half, width), F32),
                pltpu.VMEM((18 * half, width), BF16),
            ],
        ),
        out_shape=[jax.ShapeDtypeStruct(x.shape, F32), jax.ShapeDtypeStruct((8, 128), F32)],
        input_output_aliases=aliases,
        compiler_params=params(40),
        cost_estimate=cost(2 * 18 * half * rows * width, rows * width * 8 + rows * half * 24),
        name="update",
    )(*operands)


def pairs_of(count, step):
    return [(index, index ^ step) for index in range(count)]


def swap_cores(value):
    return lax.ppermute(value, "row", pairs_of(lax.axis_size("row"), 1))


def both_cores(chip_pairs):
    return [(2 * a + core, 2 * b + core) for a, b in chip_pairs for core in range(2)]


def sum_over_rows(keep, send):
    chips = lax.axis_size("row") // 2
    chip = lax.axis_index("row") // 2
    total = keep + swap_cores(send)
    for hop in range(chips // 2 - 1):
        pairs = [(hop, hop + 1), (chips - 1 - hop, chips - 2 - hop)]
        total = total + lax.ppermute(total, "row", both_cores(pairs))
    middle = [(chips // 2 - 1, chips // 2), (chips // 2, chips // 2 - 1)]
    total = total + lax.ppermute(total, "row", both_cores(middle))
    for hop in reversed(range(chips // 2 - 1)):
        pairs = [(hop + 1, hop), (chips - 2 - hop, chips - 1 - hop)]
        arrived = lax.ppermute(total, "row", both_cores(pairs))
        total = jnp.where((chip == hop) | (chip == chips - 1 - hop), arrived, total)
    return total, swap_cores(total)


def pick(index, *cases):
    return lax.select_n(index, *cases)


def fetch_square(slot, roots):
    half = slot.shape[1] // 2
    me = lax.axis_index("col")
    along = lambda value, step: lax.ppermute(value, "col", pairs_of(4, step))
    own = [slot[:, :half], slot[:, half:]]
    near, far = [], []
    for piece in own:
        near.append(along(piece, 1))
        far.append(along(piece, 2))
    cross = [along(far[0], 1), along(near[1], 2)]
    spare = (roots[0] + 3) % 4
    case = me ^ spare
    rounds = [
        ((*own, near[0], far[0]), jnp.array([[2, 3], [0, 1], [0, 1], [0, 1]], jnp.int32)[case]),
        ((*near, *far), jnp.array([[1, 3], [2, 3], [0, 1], [0, 2]], jnp.int32)[case]),
        ((*cross, near[1], far[1]), jnp.array([[0, 1], [0, 1], [0, 1], [2, 3]], jnp.int32)[case]),
    ]
    slots = jnp.array([[1, 2, 1, 2, 3, 3], [0, 0, 2, 2, 3, 3], [0, 0, 1, 1, 3, 3], [0, 0, 1, 2, 1, 2]], jnp.int32)
    halves = jnp.array([[0, 0, 1, 1, 0, 1], [0, 1, 0, 1, 0, 1], [0, 1, 0, 1, 0, 1], [0, 1, 0, 0, 1, 1]], jnp.int32)
    panel = ((slots[case] ^ me) - roots[0]) % 4
    places = panel * 2 + halves[case]
    later_of = jnp.array([[0, 1, 0, 0], [1, 0, 2, 2]], jnp.int32)[roots[0] - 2, me]
    earlier_of = jnp.array([[2, 2, 0, 1], [0, 0, 1, 0]], jnp.int32)[roots[0] - 2, me]
    both = jnp.arange(2, dtype=jnp.int32)
    later = ((*own, *near, *far), 2 * later_of + both)
    earlier = ((*own, *near, *far), 2 * earlier_of + both)
    holders = jnp.array([[3, 0, 1], [2, 3, 0]], jnp.int32)[roots[0] - 2]
    return rounds, places, later, earlier, holders


def fetch_any(slot, roots):
    half = slot.shape[1] // 2
    me = lax.axis_index("col")
    panels = [lax.psum(jnp.where(me == roots[index], slot, jnp.zeros_like(slot)), "col") for index in range(PANELS)]
    rounds = [(panel[:, :half], panel[:, half:]) for panel in panels]
    return rounds, jnp.arange(2 * PANELS, dtype=jnp.int32), panels


def gram(left, right):
    return lax.dot_general(
        left, right, (((0,), (0,)), ((), ())), precision=lax.Precision.HIGH, preferred_element_type=F32
    )


def exchange_kernel(names, pieces, ends_ref, *refs):
    use = dict(zip(names, refs))
    end = ends_ref[0] == 1
    if "acc" in use:
        start = 0
        for index in range(pieces):
            keep, swapped = use["keep", index], use["swapped", index]
            columns = slice(start, start + keep.shape[1])
            use["acc"][:, columns] = keep[...] + swapped[...]
            start = columns.stop
    if "part" in use:
        columns = use["part"].shape[1]
        use["part"][...] = use["acc_before"][...] + use["outer"][:, :columns]
    if "total" in use:
        use["total"][...] = use["part_before"][...] + use["inner"][...]
    if "final" in use:
        columns = use["final"].shape[1]
        use["final"][...] = jnp.where(end, use["outer"][:, :columns], use["total_before"][...])
    if "out" in use:
        sources = [use[name] for name in ("acc", "total") if name in use]
        if len(sources) == 1:
            use["out"][...] = sources[0][...]
        else:
            both = min(source.shape[1] for source in sources)
            use["out"][:, :both] = jnp.where(end, sources[0][:, :both], sources[1][:, :both])
            for source in sources:
                if source.shape[1] > both:
                    use["out"][:, both:] = source[:, both:]


def exchange(ends, operands, shapes, after):
    names = list(operands) + [None] * len(after) + list(shapes)
    pieces = sum(name[0] == "keep" for name in operands)
    in_vmem = pl.BlockSpec(memory_space=pltpu.VMEM)
    results = pl.pallas_call(
        functools.partial(exchange_kernel, names, pieces),
        in_specs=[pl.BlockSpec(memory_space=pltpu.SMEM)] + [in_vmem] * len(operands)
        + [ANYWHERE] * len(after),
        out_specs=[in_vmem] * len(shapes),
        out_shape=[jax.ShapeDtypeStruct(shape, F32) for shape in shapes.values()],
        compiler_params=params(14),
        cost_estimate=cost(0, 0),
        name="exchange",
    )(ends, *operands.values(), *after)
    return dict(zip(shapes, results))


def shards_square(eigvec, slot, roots, tfac):
    columns = eigvec.shape[1]
    width, half = columns // 2, slot.shape[1] // 2
    rounds, places, later, earlier, holders = fetch_square(slot, roots)
    chip, core = lax.axis_index("row") // 2, lax.axis_index("row") % 2
    ends = jnp.where((chip == 0) | (chip == 3), 1, 0).astype(jnp.int32).reshape(1)
    places = jnp.where(core == 0, places, places.reshape(PANELS, 2)[:, ::-1].reshape(-1))
    ordered = lambda pair: jnp.where(core == 0, pair, pair[::-1])
    x_both = split_array(eigvec, PIECE)
    chunks = [(index, block) for index in range(PANELS) for block in range(columns // width)]
    count = len(chunks)
    gram_chunk = 2
    prepared, arrived, sizes, gram_sides = {}, {}, {}, []

    def start(number, after):
        index, block = chunks[number]
        pieces = []
        if index not in prepared:
            cases, which = rounds[index]
            prepared[index] = choose(cases, ordered(which), ("both", "flipped"), after)
        for part in range(width // PIECE):
            pieces.append(products(prepared[index][1], x_both, block * (width // PIECE) + part, after))
        if number == gram_chunk - 1:
            gram_sides.append(choose(later[0], ordered(later[1]), ("flipped",), after)[0])
            gram_sides.append(choose(*earlier, ("both",), after)[0])
        if number == gram_chunk:
            pieces.append(products(*gram_sides, 0, after))
        arrived[number] = [(mine, swap_cores(other)) for mine, other in pieces]
        sizes[number] = (half, sum(mine.shape[1] for mine, other in pieces))

    outer_pairs = both_cores([(0, 1), (1, 0), (2, 3), (3, 2)])
    inner_pairs = both_cores([(1, 2), (2, 1)])
    acc, part, total, outer, inner, sums = {}, {}, {}, {}, {}, {}
    grams, out = None, None
    start(0, ())
    for step in range(count + 3 * LAG):
        operands, shapes = {}, {}
        inward, middle, outward = step - LAG, step - 2 * LAG, step - 3 * LAG
        if step < count:
            for number, (mine, other) in enumerate(arrived[step]):
                operands["keep", number], operands["swapped", number] = mine, other
            shapes["acc"] = sizes[step]
        if step - LAG in outer:
            operands["outer"] = outer[step - LAG]
        if 0 <= inward < count:
            operands["acc_before"] = acc[inward]
            shapes["part"] = sizes[inward]
        if 0 <= middle < count:
            operands["part_before"], operands["inner"] = part[middle], inner[step - LAG]
            shapes["total"] = sizes[middle]
        if 0 <= outward < count:
            operands["total_before"] = total[outward]
            shapes["final"] = sizes[outward]
        sent = [shapes[name] for name in ("acc", "total") if name in shapes]
        if sent:
            shapes["out"] = max(sent, key=lambda shape: shape[1])
        ahead = [] if out is None else [finished]
        if step + 1 == chunks.index((PANELS - 1, 0)):
            ahead.extend(rounds[-1][0][:2])
        if step == gram_chunk - 1:
            ahead.extend(gram_sides)
        if step == count + 1:
            ahead.append(grams)
        if 0 <= outward - 1 < count - 2:
            ahead.append(sums[chunks[outward - 1]][1])
        results = exchange(ends, operands, shapes, ahead)
        if "out" in results:
            outer[step] = lax.ppermute(results["out"], "row", outer_pairs)
        if "acc" in results:
            acc[step] = results["acc"]
        if "part" in results:
            part[inward] = results["part"]
            inner[step] = lax.ppermute(results["part"], "row", inner_pairs)
        if "total" in results:
            total[middle] = results["total"]
        if step + 1 < count:
            start(step + 1, [next(iter(results.values()))])
        if "final" in results:
            done = outward
            own, other = results["final"], swap_cores(results["final"])
            if done == gram_chunk:
                pair = own[:, width:], other[:, width:]
                block = jnp.where(core == 0, jnp.concatenate(pair, axis=0), jnp.concatenate(pair[::-1], axis=0))
                spread = [block] + [lax.ppermute(block, "col", pairs_of(4, shift)) for shift in range(1, 4)]
                places_of = holders ^ lax.axis_index("col")
                grams = jnp.stack([pick(places_of[number], *spread) for number in range(PANELS)])
            sums[chunks[done]] = (own, other)
            index, block = chunks[done]
            if index == PANELS - 1:
                pieces = [piece for panel in range(PANELS) for piece in sums[panel, block]]
                panels = [prepared[panel][0] for panel in range(PANELS)]
                out, finished = update(places, pieces, tfac, grams, panels, eigvec, out, block, width)
    return out


def shards(eigvec, slots, roots, tfac):
    if lax.axis_size("col") == 4 and lax.axis_size("row") == 8:
        return shards_square(eigvec, slots[0], roots, tfac)
    columns = eigvec.shape[1]
    width = min(columns, BLOCK)
    rounds, places, panels = fetch_any(slots[0], roots)
    core = lax.axis_index("row") % 2
    places = jnp.where(core == 0, places, places.reshape(PANELS, 2)[:, ::-1].reshape(-1))
    x_both = split_array(eigvec, width)
    prepared, sums = [], []
    for pair in rounds:
        which = jnp.where(core == 0, jnp.arange(2), jnp.arange(1, -1, -1)).astype(jnp.int32)
        prepared.append(choose(pair, which, ("both", "flipped")))
        sums.append([
            sum_over_rows(*products(prepared[-1][1], x_both, block)) for block in range(columns // width)
        ])
    grams = jnp.stack([gram(panels[1], panels[0]), gram(panels[2], panels[0]), gram(panels[2], panels[1])])
    grams = lax.psum(grams, "row")
    out = None
    for block in range(columns // width):
        pieces = [piece for index in range(PANELS) for piece in sums[index][block]]
        out, _ = update(places, pieces, tfac, grams, [both for both, _ in prepared], eigvec, out, block, width)
    return out


def solution(mesh):
    in_specs = (P("row", "col"), P("col", "row", None), P(), P())
    out_specs = P("row", "col")
    return jax.shard_map(shards, mesh=mesh, in_specs=in_specs, out_specs=out_specs, check_vma=False)
```

```python
import functools

import jax
import jax.numpy as jnp
from jax import lax
from jax.experimental import pallas as pl
from jax.experimental.pallas import tpu as pltpu
from jax.sharding import PartitionSpec as P

PANELS = 3
BLOCK = 512
LAG = 1
PIECE = 512
MIB = 1024 * 1024
F32 = jnp.float32
BF16 = jnp.bfloat16
ANYWHERE = pl.BlockSpec(memory_space=pl.ANY)
IN_HBM = pl.BlockSpec(memory_space=pltpu.HBM)


def split(value):
    high = value.astype(BF16)
    return high, (value - high.astype(F32)).astype(BF16)


def dot(left, right):
    return jnp.dot(left, right, preferred_element_type=F32)


def dot_three(left, right):
    left_high, left_low = split(left)
    right_high, right_low = split(right)
    return dot(
        jnp.concatenate([left_high, left_low, left_high], axis=1),
        jnp.concatenate([right_high, right_high, right_low], axis=0),
    )


def params(mib):
    return pltpu.CompilerParams(vmem_limit_bytes=mib * MIB)


def cost(flops, count):
    return pl.CostEstimate(flops=flops // 64, bytes_accessed=count // 64, transcendentals=0)


def pinned(value):
    return pltpu.with_memory_space_constraint(value, memory_space=pltpu.HBM)


def split_kernel(x_ref, both_ref):
    blocks, _, _, width = both_ref.shape
    for index in range(blocks):
        both_ref[index, 0], both_ref[index, 1] = split(x_ref[:, index * width : (index + 1) * width])


def split_array(x, width):
    rows, columns = x.shape
    step, blocks = min(rows, 256), columns // width
    return pl.pallas_call(
        split_kernel,
        grid=(rows // step,),
        in_specs=[pl.BlockSpec((step, columns), lambda i: (i, 0))],
        out_specs=pl.BlockSpec((blocks, 2, step, width), lambda i: (0, 0, i, 0)),
        out_shape=pltpu.HBM((blocks, 2, rows, width), BF16),
        compiler_params=params(49),
        cost_estimate=cost(rows * columns * 4, rows * columns * 8),
        name="split_x",
    )(x)


def choose_kernel(outputs, count, which_ref, *refs):
    cases, (panel_ref, split_ref, sem) = refs[:count], refs[-3:]
    use = dict(zip(outputs, refs[-3 - len(outputs) :]))
    half = cases[0].shape[1]
    for side in range(2):
        for index, case in enumerate(cases):

            @pl.when(which_ref[side] == index)
            def _(case=case, side=side):
                copy = pltpu.make_async_copy(case, panel_ref.at[:, side * half : (side + 1) * half], sem)
                copy.start()
                copy.wait()

    rows, width = panel_ref.shape
    step = min(rows, 256)
    for start in range(0, rows, step):
        here = slice(start, start + step)
        value = panel_ref[here, :]
        if "both" in use:
            split_ref[0, 0, here, :], split_ref[0, 1, here, :] = split(value)
        if "flipped" in use:
            high, low = split(value.T)
            use["flipped"][:width, here] = high
            use["flipped"][width:, here] = low
    if "both" in use:
        copy = pltpu.make_async_copy(split_ref, use["both"], sem)
        copy.start()
        copy.wait()


def choose(cases, which, outputs, after=()):
    rows, half = cases[0].shape
    shapes = {"both": (1, 2, rows, 2 * half), "flipped": (4 * half, rows)}
    spaces = {"both": pltpu.HBM, "flipped": pltpu.VMEM}
    return pl.pallas_call(
        functools.partial(choose_kernel, outputs, len(cases)),
        in_specs=[pl.BlockSpec(memory_space=pltpu.SMEM)] + [ANYWHERE] * (len(cases) + len(after)),
        out_specs=[pl.BlockSpec(memory_space=spaces[name]) for name in outputs],
        out_shape=[spaces[name](shapes[name], BF16) for name in outputs],
        scratch_shapes=[
            pltpu.VMEM((rows, 2 * half), F32),
            pltpu.VMEM(shapes["both"], BF16),
            pltpu.SemaphoreType.DMA,
        ],
        compiler_params=params(14),
        cost_estimate=cost(rows * half * 8, rows * half * 24),
        name="choose_panel",
    )(which, *cases, *after)


def products_kernel(block, flipped_ref, both_ref, *refs):
    keep_ref, send_ref, block_ref, sems = refs[-4:]
    half = keep_ref.shape[0]
    rows = block_ref.shape[1] // 2
    copies = []
    for index in range(2):
        here = slice(index * rows, (index + 1) * rows)
        for side in range(2):
            source, target = both_ref.at[block, side, here], block_ref.at[side, here]
            copies.append(pltpu.make_async_copy(source, target, sems.at[index, side]))
            copies[-1].start()
    total = None
    for index in range(2):
        here = slice(index * rows, (index + 1) * rows)
        copies[2 * index].wait()
        with_high = dot(flipped_ref[:, here], block_ref[0, here, :])
        copies[2 * index + 1].wait()
        with_low = dot(flipped_ref[: 2 * half, here], block_ref[1, here, :])
        part = with_high[: 2 * half] + (with_high[2 * half :] + with_low)
        total = part if total is None else total + part
    keep_ref[...] = total[:half]
    send_ref[...] = total[half:]


def products(flipped, both, block, after=()):
    rows, width = both.shape[2:]
    half = flipped.shape[0] // 4
    in_vmem = pl.BlockSpec(memory_space=pltpu.VMEM)
    return pl.pallas_call(
        functools.partial(products_kernel, block),
        in_specs=[in_vmem, IN_HBM] + [ANYWHERE] * len(after),
        out_specs=[in_vmem] * 2,
        out_shape=[jax.ShapeDtypeStruct((half, width), F32)] * 2,
        scratch_shapes=[pltpu.VMEM((2, rows, width), BF16), pltpu.SemaphoreType.DMA((2, 2))],
        compiler_params=params(16),
        cost_estimate=cost(2 * 6 * half * rows * width, rows * width * 4 + 8 * half * rows),
        name="products",
    )(flipped, pinned(both), *after)


def update_kernel(offset, place_ref, *refs):
    sums = refs[:6]
    tfac_ref, gram_ref = refs[6:8]
    panel_refs, x_ref = refs[8:11], refs[11]
    out_ref, done_ref, w_ref, y_ref, y_split_ref = refs[-5:]
    half = sums[0].shape[0]
    width = 2 * half

    @pl.when(pl.program_id(0) == 0)
    def _():
        for index, piece in enumerate(sums):
            start = pl.multiple_of(place_ref[index] * half, half)
            w_ref[pl.ds(start, half), :] = piece[:, offset : offset + w_ref.shape[1]]
        first = dot_three(tfac_ref[0], w_ref[:width, :])
        y_ref[:width, :] = first
        second = dot_three(tfac_ref[1], w_ref[width : 2 * width, :] - dot_three(gram_ref[0], first))
        y_ref[width : 2 * width, :] = second
        third = w_ref[2 * width :, :] - dot_three(gram_ref[1], first) - dot_three(gram_ref[2], second)
        y_ref[2 * width :, :] = dot_three(tfac_ref[2], third)
        for index in range(6):
            start = pl.multiple_of(place_ref[index] * half, half)
            high, low = split(y_ref[pl.ds(start, half), :])
            for number, value in enumerate((high, high, low)):
                y_split_ref[(6 * number + index) * half : (6 * number + index + 1) * half, :] = value

    sides = [ref[0, side] for side in (0, 1, 0) for ref in panel_refs]
    out_ref[...] = x_ref[...] - dot(jnp.concatenate(sides, axis=1), y_split_ref[...])
    done_ref[...] = jnp.zeros(done_ref.shape, F32)


def update(place, sums, tfac, grams, panels, x, out, block, width, offset=0):
    rows, columns = x.shape
    half = sums[0].shape[0]
    step = min(rows, 512)
    panel_spec = pl.BlockSpec((1, 2, step, 2 * half), lambda i, place: (0, 0, i, 0))
    block_spec = pl.BlockSpec((step, width), lambda i, place: (i, block))
    operands = [place, *sums, tfac, grams, *map(pinned, panels), x]
    in_specs = (
        [pl.BlockSpec(memory_space=pltpu.VMEM)] * 8
        + [panel_spec] * 3
        + [block_spec]
    )
    aliases = {}
    if out is not None:
        aliases = {len(operands): 0}
        operands.append(out)
        in_specs.append(IN_HBM)
    return pl.pallas_call(
        functools.partial(update_kernel, offset),
        grid_spec=pltpu.PrefetchScalarGridSpec(
            num_scalar_prefetch=1,
            grid=(rows // step,),
            in_specs=in_specs,
            out_specs=[block_spec, pl.BlockSpec((8, 128), lambda i, place: (0, 0))],
            scratch_shapes=[
                pltpu.VMEM((6 * half, width), F32),
                pltpu.VMEM((6 * half, width), F32),
                pltpu.VMEM((18 * half, width), BF16),
            ],
        ),
        out_shape=[jax.ShapeDtypeStruct(x.shape, F32), jax.ShapeDtypeStruct((8, 128), F32)],
        input_output_aliases=aliases,
        compiler_params=params(40),
        cost_estimate=cost(2 * 18 * half * rows * width, rows * width * 8 + rows * half * 24),
        name="update",
    )(*operands)


def pairs_of(count, step):
    return [(index, index ^ step) for index in range(count)]


def swap_cores(value):
    return lax.ppermute(value, "row", pairs_of(lax.axis_size("row"), 1))


def both_cores(chip_pairs):
    return [(2 * a + core, 2 * b + core) for a, b in chip_pairs for core in range(2)]


def sum_over_rows(keep, send):
    chips = lax.axis_size("row") // 2
    chip = lax.axis_index("row") // 2
    total = keep + swap_cores(send)
    for hop in range(chips // 2 - 1):
        pairs = [(hop, hop + 1), (chips - 1 - hop, chips - 2 - hop)]
        total = total + lax.ppermute(total, "row", both_cores(pairs))
    middle = [(chips // 2 - 1, chips // 2), (chips // 2, chips // 2 - 1)]
    total = total + lax.ppermute(total, "row", both_cores(middle))
    for hop in reversed(range(chips // 2 - 1)):
        pairs = [(hop + 1, hop), (chips - 2 - hop, chips - 1 - hop)]
        arrived = lax.ppermute(total, "row", both_cores(pairs))
        total = jnp.where((chip == hop) | (chip == chips - 1 - hop), arrived, total)
    return total, swap_cores(total)


def pick(index, *cases):
    return lax.select_n(index, *cases)


def fetch_square(slot, roots):
    half = slot.shape[1] // 2
    me = lax.axis_index("col")
    along = lambda value, step: lax.ppermute(value, "col", pairs_of(4, step))
    own = [slot[:, :half], slot[:, half:]]
    near, far = [], []
    for piece in own:
        near.append(along(piece, 1))
        far.append(along(piece, 2))
    cross = [along(far[0], 1), along(near[1], 2)]
    spare = (roots[0] + 3) % 4
    case = me ^ spare
    rounds = [
        ((*own, near[0], far[0]), jnp.array([[2, 3], [0, 1], [0, 1], [0, 1]], jnp.int32)[case]),
        ((*near, *far), jnp.array([[1, 3], [2, 3], [0, 1], [0, 2]], jnp.int32)[case]),
        ((*cross, near[1], far[1]), jnp.array([[0, 1], [0, 1], [0, 1], [2, 3]], jnp.int32)[case]),
    ]
    slots = jnp.array([[1, 2, 1, 2, 3, 3], [0, 0, 2, 2, 3, 3], [0, 0, 1, 1, 3, 3], [0, 0, 1, 2, 1, 2]], jnp.int32)
    halves = jnp.array([[0, 0, 1, 1, 0, 1], [0, 1, 0, 1, 0, 1], [0, 1, 0, 1, 0, 1], [0, 1, 0, 0, 1, 1]], jnp.int32)
    panel = ((slots[case] ^ me) - roots[0]) % 4
    places = panel * 2 + halves[case]
    later_of = jnp.array([[0, 1, 0, 0], [1, 0, 2, 2]], jnp.int32)[roots[0] - 2, me]
    earlier_of = jnp.array([[2, 2, 0, 1], [0, 0, 1, 0]], jnp.int32)[roots[0] - 2, me]
    both = jnp.arange(2, dtype=jnp.int32)
    later = ((*own, *near, *far), 2 * later_of + both)
    earlier = ((*own, *near, *far), 2 * earlier_of + both)
    holders = jnp.array([[3, 0, 1], [2, 3, 0]], jnp.int32)[roots[0] - 2]
    return rounds, places, later, earlier, holders


def fetch_any(slot, roots):
    half = slot.shape[1] // 2
    me = lax.axis_index("col")
    panels = [lax.psum(jnp.where(me == roots[index], slot, jnp.zeros_like(slot)), "col") for index in range(PANELS)]
    rounds = [(panel[:, :half], panel[:, half:]) for panel in panels]
    return rounds, jnp.arange(2 * PANELS, dtype=jnp.int32), panels


def gram(left, right):
    return lax.dot_general(
        left, right, (((0,), (0,)), ((), ())), precision=lax.Precision.HIGH, preferred_element_type=F32
    )


def exchange_kernel(names, pieces, ends_ref, *refs):
    use = dict(zip(names, refs))
    end = ends_ref[0] == 1
    if "acc" in use:
        start = 0
        for index in range(pieces):
            keep, swapped = use["keep", index], use["swapped", index]
            columns = slice(start, start + keep.shape[1])
            use["acc"][:, columns] = keep[...] + swapped[...]
            start = columns.stop
    if "part" in use:
        columns = use["part"].shape[1]
        use["part"][...] = use["acc_before"][...] + use["outer"][:, :columns]
    if "total" in use:
        use["total"][...] = use["part_before"][...] + use["inner"][...]
    if "final" in use:
        columns = use["final"].shape[1]
        use["final"][...] = jnp.where(end, use["outer"][:, :columns], use["total_before"][...])
    if "out" in use:
        sources = [use[name] for name in ("acc", "total") if name in use]
        if len(sources) == 1:
            use["out"][...] = sources[0][...]
        else:
            both = min(source.shape[1] for source in sources)
            use["out"][:, :both] = jnp.where(end, sources[0][:, :both], sources[1][:, :both])
            for source in sources:
                if source.shape[1] > both:
                    use["out"][:, both:] = source[:, both:]


def exchange(ends, operands, shapes, after):
    names = list(operands) + [None] * len(after) + list(shapes)
    pieces = sum(name[0] == "keep" for name in operands)
    in_vmem = pl.BlockSpec(memory_space=pltpu.VMEM)
    results = pl.pallas_call(
        functools.partial(exchange_kernel, names, pieces),
        in_specs=[pl.BlockSpec(memory_space=pltpu.SMEM)] + [in_vmem] * len(operands)
        + [ANYWHERE] * len(after),
        out_specs=[in_vmem] * len(shapes),
        out_shape=[jax.ShapeDtypeStruct(shape, F32) for shape in shapes.values()],
        compiler_params=params(14),
        cost_estimate=cost(0, 0),
        name="exchange",
    )(ends, *operands.values(), *after)
    return dict(zip(shapes, results))


def shards_square(eigvec, slot, roots, tfac):
    columns = eigvec.shape[1]
    width, half = columns // 2, slot.shape[1] // 2
    rounds, places, later, earlier, holders = fetch_square(slot, roots)
    chip, core = lax.axis_index("row") // 2, lax.axis_index("row") % 2
    ends = jnp.where((chip == 0) | (chip == 3), 1, 0).astype(jnp.int32).reshape(1)
    places = jnp.where(core == 0, places, places.reshape(PANELS, 2)[:, ::-1].reshape(-1))
    ordered = lambda pair: jnp.where(core == 0, pair, pair[::-1])
    x_both = split_array(eigvec, PIECE)
    chunks = [(0, 0), (0, 1), (1, 0), (2, 0), (1, 1), (2, 1)]
    count = len(chunks)
    gram_chunk = 2
    prepared, arrived, sizes, gram_sides = {}, {}, {}, []

    def start(number, after):
        index, block = chunks[number]
        pieces = []
        if index not in prepared:
            cases, which = rounds[index]
            prepared[index] = choose(cases, ordered(which), ("both", "flipped"), after)
        for part in range(width // PIECE):
            pieces.append(products(prepared[index][1], x_both, block * (width // PIECE) + part, after))
        if number == gram_chunk - 1:
            gram_sides.append(choose(later[0], ordered(later[1]), ("flipped",), after)[0])
            gram_sides.append(choose(*earlier, ("both",), after)[0])
        if number == gram_chunk:
            pieces.append(products(*gram_sides, 0, after))
        arrived[number] = [(mine, swap_cores(other)) for mine, other in pieces]
        sizes[number] = (half, sum(mine.shape[1] for mine, other in pieces))

    outer_pairs = both_cores([(0, 1), (1, 0), (2, 3), (3, 2)])
    inner_pairs = both_cores([(1, 2), (2, 1)])
    acc, part, total, outer, inner, sums = {}, {}, {}, {}, {}, {}
    grams, out = None, None
    start(0, ())
    for step in range(count + 3 * LAG):
        operands, shapes = {}, {}
        inward, middle, outward = step - LAG, step - 2 * LAG, step - 3 * LAG
        if step < count:
            for number, (mine, other) in enumerate(arrived[step]):
                operands["keep", number], operands["swapped", number] = mine, other
            shapes["acc"] = sizes[step]
        if step - LAG in outer:
            operands["outer"] = outer[step - LAG]
        if 0 <= inward < count:
            operands["acc_before"] = acc[inward]
            shapes["part"] = sizes[inward]
        if 0 <= middle < count:
            operands["part_before"], operands["inner"] = part[middle], inner[step - LAG]
            shapes["total"] = sizes[middle]
        if 0 <= outward < count:
            operands["total_before"] = total[outward]
            shapes["final"] = sizes[outward]
        sent = [shapes[name] for name in ("acc", "total") if name in shapes]
        if sent:
            shapes["out"] = max(sent, key=lambda shape: shape[1])
        ahead = [] if out is None else [finished]
        if step + 1 == chunks.index((PANELS - 1, 0)):
            ahead.extend(rounds[-1][0][:2])
        if step == gram_chunk - 1:
            ahead.extend(gram_sides)
        if 0 <= outward - 1 < count - 2:
            ahead.append(sums[chunks[outward - 1]][1])
        results = exchange(ends, operands, shapes, ahead)
        if "out" in results:
            outer[step] = lax.ppermute(results["out"], "row", outer_pairs)
        if "acc" in results:
            acc[step] = results["acc"]
        if "part" in results:
            part[inward] = results["part"]
            inner[step] = lax.ppermute(results["part"], "row", inner_pairs)
        if "total" in results:
            total[middle] = results["total"]
        if step + 1 < count:
            start(step + 1, [next(iter(results.values()))])
        if "final" in results:
            done = outward
            own, other = results["final"], swap_cores(results["final"])
            if done == gram_chunk:
                pair = own[:, width:], other[:, width:]
                block = jnp.where(core == 0, jnp.concatenate(pair, axis=0), jnp.concatenate(pair[::-1], axis=0))
                spread = [block] + [lax.ppermute(block, "col", pairs_of(4, shift)) for shift in range(1, 4)]
                places_of = holders ^ lax.axis_index("col")
                grams = jnp.stack([pick(places_of[number], *spread) for number in range(PANELS)])
            sums[chunks[done]] = (own, other)
            index, block = chunks[done]
            ready = block if index == PANELS - 1 else 0
            if step >= count:
                pieces = [piece for panel in range(PANELS) for piece in sums[panel, ready]]
                panels = [prepared[panel][0] for panel in range(PANELS)]
                if ready == 0:
                    place, size, offset = step - count, width // 2, (step - count) * (width // 2)
                else:
                    place, size, offset = 1, width, 0
                out, finished = update(places, pieces, tfac, grams, panels, eigvec, out, place, size, offset)
    return out


def shards(eigvec, slots, roots, tfac):
    if lax.axis_size("col") == 4 and lax.axis_size("row") == 8:
        return shards_square(eigvec, slots[0], roots, tfac)
    columns = eigvec.shape[1]
    width = min(columns, BLOCK)
    rounds, places, panels = fetch_any(slots[0], roots)
    core = lax.axis_index("row") % 2
    places = jnp.where(core == 0, places, places.reshape(PANELS, 2)[:, ::-1].reshape(-1))
    x_both = split_array(eigvec, width)
    prepared, sums = [], []
    for pair in rounds:
        which = jnp.where(core == 0, jnp.arange(2), jnp.arange(1, -1, -1)).astype(jnp.int32)
        prepared.append(choose(pair, which, ("both", "flipped")))
        sums.append([
            sum_over_rows(*products(prepared[-1][1], x_both, block)) for block in range(columns // width)
        ])
    grams = jnp.stack([gram(panels[1], panels[0]), gram(panels[2], panels[0]), gram(panels[2], panels[1])])
    grams = lax.psum(grams, "row")
    out = None
    for block in range(columns // width):
        pieces = [piece for index in range(PANELS) for piece in sums[index][block]]
        out, _ = update(places, pieces, tfac, grams, [both for both, _ in prepared], eigvec, out, block, width)
    return out


def solution(mesh):
    in_specs = (P("row", "col"), P("col", "row", None), P(), P())
    out_specs = P("row", "col")
    return jax.shard_map(shards, mesh=mesh, in_specs=in_specs, out_specs=out_specs, check_vma=False)
```

```python
import functools

import jax
import jax.numpy as jnp
from jax import lax
from jax.experimental import pallas as pl
from jax.experimental.pallas import tpu as pltpu
from jax.sharding import PartitionSpec as P

PANELS = 3
BLOCK = 512
LAG = 1
PIECE = 512
MIB = 1024 * 1024
F32 = jnp.float32
BF16 = jnp.bfloat16
ANYWHERE = pl.BlockSpec(memory_space=pl.ANY)
IN_HBM = pl.BlockSpec(memory_space=pltpu.HBM)


def split(value):
    high = value.astype(BF16)
    return high, (value - high.astype(F32)).astype(BF16)


def dot(left, right):
    return jnp.dot(left, right, preferred_element_type=F32)


def dot_three(left, right):
    left_high, left_low = split(left)
    right_high, right_low = split(right)
    return dot(
        jnp.concatenate([left_high, left_low, left_high], axis=1),
        jnp.concatenate([right_high, right_high, right_low], axis=0),
    )


def params(mib):
    return pltpu.CompilerParams(vmem_limit_bytes=mib * MIB)


def cost(flops, count):
    return pl.CostEstimate(flops=flops // 64, bytes_accessed=count // 64, transcendentals=0)


def pinned(value):
    return pltpu.with_memory_space_constraint(value, memory_space=pltpu.HBM)


def split_kernel(x_ref, both_ref):
    blocks, _, _, width = both_ref.shape
    for index in range(blocks):
        both_ref[index, 0], both_ref[index, 1] = split(x_ref[:, index * width : (index + 1) * width])


def split_array(x, width):
    rows, columns = x.shape
    step, blocks = min(rows, 256), columns // width
    return pl.pallas_call(
        split_kernel,
        grid=(rows // step,),
        in_specs=[pl.BlockSpec((step, columns), lambda i: (i, 0))],
        out_specs=pl.BlockSpec((blocks, 2, step, width), lambda i: (0, 0, i, 0)),
        out_shape=pltpu.HBM((blocks, 2, rows, width), BF16),
        compiler_params=params(63),
        cost_estimate=cost(rows * columns * 4, rows * columns * 8),
        name="split_x",
    )(x)


def choose_kernel(outputs, count, which_ref, *refs):
    cases, (panel_ref, split_ref, sem) = refs[:count], refs[-3:]
    use = dict(zip(outputs, refs[-3 - len(outputs) :]))
    half = cases[0].shape[1]
    for side in range(2):
        for index, case in enumerate(cases):

            @pl.when(which_ref[side] == index)
            def _(case=case, side=side):
                copy = pltpu.make_async_copy(case, panel_ref.at[:, side * half : (side + 1) * half], sem)
                copy.start()
                copy.wait()

    rows, width = panel_ref.shape
    step = min(rows, 256)
    for start in range(0, rows, step):
        here = slice(start, start + step)
        value = panel_ref[here, :]
        if "both" in use:
            split_ref[0, 0, here, :], split_ref[0, 1, here, :] = split(value)
        if "flipped" in use:
            high, low = split(value.T)
            use["flipped"][:width, here] = high
            use["flipped"][width:, here] = low
    if "both" in use:
        copy = pltpu.make_async_copy(split_ref, use["both"], sem)
        copy.start()
        copy.wait()


def choose(cases, which, outputs, after=()):
    rows, half = cases[0].shape
    shapes = {"both": (1, 2, rows, 2 * half), "flipped": (4 * half, rows)}
    spaces = {"both": pltpu.HBM, "flipped": pltpu.VMEM}
    return pl.pallas_call(
        functools.partial(choose_kernel, outputs, len(cases)),
        in_specs=[pl.BlockSpec(memory_space=pltpu.SMEM)] + [ANYWHERE] * (len(cases) + len(after)),
        out_specs=[pl.BlockSpec(memory_space=spaces[name]) for name in outputs],
        out_shape=[spaces[name](shapes[name], BF16) for name in outputs],
        scratch_shapes=[
            pltpu.VMEM((rows, 2 * half), F32),
            pltpu.VMEM(shapes["both"], BF16),
            pltpu.SemaphoreType.DMA,
        ],
        compiler_params=params(14),
        cost_estimate=cost(rows * half * 8, rows * half * 24),
        name="choose_panel",
    )(which, *cases, *after)


def products_kernel(block, flipped_ref, both_ref, *refs):
    keep_ref, send_ref, block_ref, sems = refs[-4:]
    half = keep_ref.shape[0]
    rows = block_ref.shape[1] // 2
    copies = []
    for index in range(2):
        here = slice(index * rows, (index + 1) * rows)
        for side in range(2):
            source, target = both_ref.at[block, side, here], block_ref.at[side, here]
            copies.append(pltpu.make_async_copy(source, target, sems.at[index, side]))
            copies[-1].start()
    total = None
    for index in range(2):
        here = slice(index * rows, (index + 1) * rows)
        copies[2 * index].wait()
        with_high = dot(flipped_ref[:, here], block_ref[0, here, :])
        copies[2 * index + 1].wait()
        with_low = dot(flipped_ref[: 2 * half, here], block_ref[1, here, :])
        part = with_high[: 2 * half] + (with_high[2 * half :] + with_low)
        total = part if total is None else total + part
    keep_ref[...] = total[:half]
    send_ref[...] = total[half:]


def products(flipped, both, block, after=()):
    rows, width = both.shape[2:]
    half = flipped.shape[0] // 4
    in_vmem = pl.BlockSpec(memory_space=pltpu.VMEM)
    return pl.pallas_call(
        functools.partial(products_kernel, block),
        in_specs=[in_vmem, IN_HBM] + [ANYWHERE] * len(after),
        out_specs=[in_vmem] * 2,
        out_shape=[jax.ShapeDtypeStruct((half, width), F32)] * 2,
        scratch_shapes=[pltpu.VMEM((2, rows, width), BF16), pltpu.SemaphoreType.DMA((2, 2))],
        compiler_params=params(16),
        cost_estimate=cost(2 * 6 * half * rows * width, rows * width * 4 + 8 * half * rows),
        name="products",
    )(flipped, pinned(both), *after)


def update_kernel(offset, place_ref, *refs):
    sums = refs[:6]
    tfac_ref, gram_ref = refs[6:8]
    panel_refs, x_ref = refs[8:11], refs[11]
    out_ref, done_ref, w_ref, y_ref, y_split_ref = refs[-5:]
    half = sums[0].shape[0]
    width = 2 * half

    @pl.when(pl.program_id(0) == 0)
    def _():
        for index, piece in enumerate(sums):
            start = pl.multiple_of(place_ref[index] * half, half)
            w_ref[pl.ds(start, half), :] = piece[:, offset : offset + w_ref.shape[1]]
        first = dot_three(tfac_ref[0], w_ref[:width, :])
        y_ref[:width, :] = first
        second = dot_three(tfac_ref[1], w_ref[width : 2 * width, :] - dot_three(gram_ref[0], first))
        y_ref[width : 2 * width, :] = second
        third = w_ref[2 * width :, :] - dot_three(gram_ref[1], first) - dot_three(gram_ref[2], second)
        y_ref[2 * width :, :] = dot_three(tfac_ref[2], third)
        for index in range(6):
            start = pl.multiple_of(place_ref[index] * half, half)
            high, low = split(y_ref[pl.ds(start, half), :])
            for number, value in enumerate((high, high, low)):
                y_split_ref[(6 * number + index) * half : (6 * number + index + 1) * half, :] = value

    sides = [ref[0, side] for side in (0, 1, 0) for ref in panel_refs]
    out_ref[...] = x_ref[...] - dot(jnp.concatenate(sides, axis=1), y_split_ref[...])
    done_ref[...] = jnp.zeros(done_ref.shape, F32)


def update(place, sums, tfac, grams, panels, x, out, block, width, offset=0):
    rows, columns = x.shape
    half = sums[0].shape[0]
    step = min(rows, 512)
    panel_spec = pl.BlockSpec((1, 2, step, 2 * half), lambda i, place: (0, 0, i, 0))
    block_spec = pl.BlockSpec((step, width), lambda i, place: (i, block))
    operands = [place, *sums, tfac, grams, *map(pinned, panels), x]
    in_specs = (
        [pl.BlockSpec(memory_space=pltpu.VMEM)] * 8
        + [panel_spec] * 3
        + [block_spec]
    )
    aliases = {}
    if out is not None:
        aliases = {len(operands): 0}
        operands.append(out)
        in_specs.append(IN_HBM)
    return pl.pallas_call(
        functools.partial(update_kernel, offset),
        grid_spec=pltpu.PrefetchScalarGridSpec(
            num_scalar_prefetch=1,
            grid=(rows // step,),
            in_specs=in_specs,
            out_specs=[block_spec, pl.BlockSpec((8, 128), lambda i, place: (0, 0))],
            scratch_shapes=[
                pltpu.VMEM((6 * half, width), F32),
                pltpu.VMEM((6 * half, width), F32),
                pltpu.VMEM((18 * half, width), BF16),
            ],
        ),
        out_shape=[jax.ShapeDtypeStruct(x.shape, F32), jax.ShapeDtypeStruct((8, 128), F32)],
        input_output_aliases=aliases,
        compiler_params=params(40),
        cost_estimate=cost(2 * 18 * half * rows * width, rows * width * 8 + rows * half * 24),
        name="update",
    )(*operands)


def pairs_of(count, step):
    return [(index, index ^ step) for index in range(count)]


def swap_cores(value):
    return lax.ppermute(value, "row", pairs_of(lax.axis_size("row"), 1))


def both_cores(chip_pairs):
    return [(2 * a + core, 2 * b + core) for a, b in chip_pairs for core in range(2)]


def sum_over_rows(keep, send):
    chips = lax.axis_size("row") // 2
    chip = lax.axis_index("row") // 2
    total = keep + swap_cores(send)
    for hop in range(chips // 2 - 1):
        pairs = [(hop, hop + 1), (chips - 1 - hop, chips - 2 - hop)]
        total = total + lax.ppermute(total, "row", both_cores(pairs))
    middle = [(chips // 2 - 1, chips // 2), (chips // 2, chips // 2 - 1)]
    total = total + lax.ppermute(total, "row", both_cores(middle))
    for hop in reversed(range(chips // 2 - 1)):
        pairs = [(hop + 1, hop), (chips - 2 - hop, chips - 1 - hop)]
        arrived = lax.ppermute(total, "row", both_cores(pairs))
        total = jnp.where((chip == hop) | (chip == chips - 1 - hop), arrived, total)
    return total, swap_cores(total)


def pick(index, *cases):
    return lax.select_n(index, *cases)


def fetch_square(slot, roots):
    half = slot.shape[1] // 2
    me = lax.axis_index("col")
    along = lambda value, step: lax.ppermute(value, "col", pairs_of(4, step))
    own = [slot[:, :half], slot[:, half:]]
    near, far = [], []
    for piece in own:
        near.append(along(piece, 1))
        far.append(along(piece, 2))
    cross = [along(far[0], 1), along(near[1], 2)]
    spare = (roots[0] + 3) % 4
    case = me ^ spare
    rounds = [
        ((*own, near[0], far[0]), jnp.array([[2, 3], [0, 1], [0, 1], [0, 1]], jnp.int32)[case]),
        ((*near, *far), jnp.array([[1, 3], [2, 3], [0, 1], [0, 2]], jnp.int32)[case]),
        ((*cross, near[1], far[1]), jnp.array([[0, 1], [0, 1], [0, 1], [2, 3]], jnp.int32)[case]),
    ]
    slots = jnp.array([[1, 2, 1, 2, 3, 3], [0, 0, 2, 2, 3, 3], [0, 0, 1, 1, 3, 3], [0, 0, 1, 2, 1, 2]], jnp.int32)
    halves = jnp.array([[0, 0, 1, 1, 0, 1], [0, 1, 0, 1, 0, 1], [0, 1, 0, 1, 0, 1], [0, 1, 0, 0, 1, 1]], jnp.int32)
    panel = ((slots[case] ^ me) - roots[0]) % 4
    places = panel * 2 + halves[case]
    later_of = jnp.array([[0, 1, 0, 0], [1, 0, 2, 2]], jnp.int32)[roots[0] - 2, me]
    earlier_of = jnp.array([[2, 2, 0, 1], [0, 0, 1, 0]], jnp.int32)[roots[0] - 2, me]
    both = jnp.arange(2, dtype=jnp.int32)
    later = ((*own, *near, *far), 2 * later_of + both)
    earlier = ((*own, *near, *far), 2 * earlier_of + both)
    holders = jnp.array([[3, 0, 1], [2, 3, 0]], jnp.int32)[roots[0] - 2]
    return rounds, places, later, earlier, holders


def fetch_any(slot, roots):
    half = slot.shape[1] // 2
    me = lax.axis_index("col")
    panels = [lax.psum(jnp.where(me == roots[index], slot, jnp.zeros_like(slot)), "col") for index in range(PANELS)]
    rounds = [(panel[:, :half], panel[:, half:]) for panel in panels]
    return rounds, jnp.arange(2 * PANELS, dtype=jnp.int32), panels


def gram(left, right):
    return lax.dot_general(
        left, right, (((0,), (0,)), ((), ())), precision=lax.Precision.HIGH, preferred_element_type=F32
    )


def exchange_kernel(names, pieces, ends_ref, *refs):
    use = dict(zip(names, refs))
    end = ends_ref[0] == 1
    if "acc" in use:
        start = 0
        for index in range(pieces):
            keep, swapped = use["keep", index], use["swapped", index]
            columns = slice(start, start + keep.shape[1])
            use["acc"][:, columns] = keep[...] + swapped[...]
            start = columns.stop
    if "part" in use:
        columns = use["part"].shape[1]
        use["part"][...] = use["acc_before"][...] + use["outer"][:, :columns]
    if "total" in use:
        use["total"][...] = use["part_before"][...] + use["inner"][...]
    if "final" in use:
        columns = use["final"].shape[1]
        use["final"][...] = jnp.where(end, use["outer"][:, :columns], use["total_before"][...])
    if "out" in use:
        sources = [use[name] for name in ("acc", "total") if name in use]
        if len(sources) == 1:
            use["out"][...] = sources[0][...]
        else:
            both = min(source.shape[1] for source in sources)
            use["out"][:, :both] = jnp.where(end, sources[0][:, :both], sources[1][:, :both])
            for source in sources:
                if source.shape[1] > both:
                    use["out"][:, both:] = source[:, both:]


def exchange(ends, operands, shapes, after):
    names = list(operands) + [None] * len(after) + list(shapes)
    pieces = sum(name[0] == "keep" for name in operands)
    in_vmem = pl.BlockSpec(memory_space=pltpu.VMEM)
    results = pl.pallas_call(
        functools.partial(exchange_kernel, names, pieces),
        in_specs=[pl.BlockSpec(memory_space=pltpu.SMEM)] + [in_vmem] * len(operands)
        + [ANYWHERE] * len(after),
        out_specs=[in_vmem] * len(shapes),
        out_shape=[jax.ShapeDtypeStruct(shape, F32) for shape in shapes.values()],
        compiler_params=params(14),
        cost_estimate=cost(0, 0),
        name="exchange",
    )(ends, *operands.values(), *after)
    return dict(zip(shapes, results))


def shards_square(eigvec, slot, roots, tfac):
    columns = eigvec.shape[1]
    width, half = columns // 2, slot.shape[1] // 2
    rounds, places, later, earlier, holders = fetch_square(slot, roots)
    chip, core = lax.axis_index("row") // 2, lax.axis_index("row") % 2
    ends = jnp.where((chip == 0) | (chip == 3), 1, 0).astype(jnp.int32).reshape(1)
    places = jnp.where(core == 0, places, places.reshape(PANELS, 2)[:, ::-1].reshape(-1))
    ordered = lambda pair: jnp.where(core == 0, pair, pair[::-1])
    x_both = split_array(eigvec, PIECE)
    chunks = [(0, 0), (0, 1), (1, 0), (2, 0), (1, 1), (2, 1)]
    count = len(chunks)
    gram_chunk = 2
    prepared, arrived, sizes, gram_sides = {}, {}, {}, []

    def start(number, after):
        index, block = chunks[number]
        pieces = []
        if index not in prepared:
            cases, which = rounds[index]
            prepared[index] = choose(cases, ordered(which), ("both", "flipped"), after)
        for part in range(width // PIECE):
            pieces.append(products(prepared[index][1], x_both, block * (width // PIECE) + part, after))
        if number == gram_chunk - 1:
            gram_sides.append(choose(later[0], ordered(later[1]), ("flipped",), after)[0])
            gram_sides.append(choose(*earlier, ("both",), after)[0])
        if number == gram_chunk:
            pieces.append(products(*gram_sides, 0, after))
        arrived[number] = [(mine, swap_cores(other)) for mine, other in pieces]
        sizes[number] = (half, sum(mine.shape[1] for mine, other in pieces))

    outer_pairs = both_cores([(0, 1), (1, 0), (2, 3), (3, 2)])
    inner_pairs = both_cores([(1, 2), (2, 1)])
    acc, part, total, outer, inner, sums = {}, {}, {}, {}, {}, {}
    grams, out = None, None
    start(0, ())
    for step in range(count + 3 * LAG):
        operands, shapes = {}, {}
        inward, middle, outward = step - LAG, step - 2 * LAG, step - 3 * LAG
        if step < count:
            for number, (mine, other) in enumerate(arrived[step]):
                operands["keep", number], operands["swapped", number] = mine, other
            shapes["acc"] = sizes[step]
        if step - LAG in outer:
            operands["outer"] = outer[step - LAG]
        if 0 <= inward < count:
            operands["acc_before"] = acc[inward]
            shapes["part"] = sizes[inward]
        if 0 <= middle < count:
            operands["part_before"], operands["inner"] = part[middle], inner[step - LAG]
            shapes["total"] = sizes[middle]
        if 0 <= outward < count:
            operands["total_before"] = total[outward]
            shapes["final"] = sizes[outward]
        sent = [shapes[name] for name in ("acc", "total") if name in shapes]
        if sent:
            shapes["out"] = max(sent, key=lambda shape: shape[1])
        ahead = [] if out is None else [finished]
        if step + 1 == chunks.index((PANELS - 1, 0)):
            ahead.extend(map(pinned, rounds[-1][0][:2]))
        if step == gram_chunk - 1:
            ahead.extend([gram_sides[0], pinned(gram_sides[1])])
        if 0 <= outward - 1 < count - 2:
            ahead.append(sums[chunks[outward - 1]][1])
        results = exchange(ends, operands, shapes, ahead)
        if "out" in results:
            outer[step] = lax.ppermute(results["out"], "row", outer_pairs)
        if "acc" in results:
            acc[step] = results["acc"]
        if "part" in results:
            part[inward] = results["part"]
            inner[step] = lax.ppermute(results["part"], "row", inner_pairs)
        if "total" in results:
            total[middle] = results["total"]
        if step + 1 < count:
            start(step + 1, [next(iter(results.values()))])
        if "final" in results:
            done = outward
            own, other = results["final"], swap_cores(results["final"])
            if done == gram_chunk:
                pair = own[:, width:], other[:, width:]
                block = jnp.where(core == 0, jnp.concatenate(pair, axis=0), jnp.concatenate(pair[::-1], axis=0))
                spread = [block] + [lax.ppermute(block, "col", pairs_of(4, shift)) for shift in range(1, 4)]
                places_of = holders ^ lax.axis_index("col")
                grams = jnp.stack([pick(places_of[number], *spread) for number in range(PANELS)])
            sums[chunks[done]] = (own, other)
            index, block = chunks[done]
            ready = block if index == PANELS - 1 else 0
            if step >= count:
                pieces = [piece for panel in range(PANELS) for piece in sums[panel, ready]]
                panels = [prepared[panel][0] for panel in range(PANELS)]
                if ready == 0:
                    place, size, offset = step - count, width // 2, (step - count) * (width // 2)
                else:
                    place, size, offset = 1, width, 0
                out, finished = update(places, pieces, tfac, grams, panels, eigvec, out, place, size, offset)
    return out


def shards(eigvec, slots, roots, tfac):
    if lax.axis_size("col") == 4 and lax.axis_size("row") == 8:
        return shards_square(eigvec, slots[0], roots, tfac)
    columns = eigvec.shape[1]
    width = min(columns, BLOCK)
    rounds, places, panels = fetch_any(slots[0], roots)
    core = lax.axis_index("row") % 2
    places = jnp.where(core == 0, places, places.reshape(PANELS, 2)[:, ::-1].reshape(-1))
    x_both = split_array(eigvec, width)
    prepared, sums = [], []
    for pair in rounds:
        which = jnp.where(core == 0, jnp.arange(2), jnp.arange(1, -1, -1)).astype(jnp.int32)
        prepared.append(choose(pair, which, ("both", "flipped")))
        sums.append([
            sum_over_rows(*products(prepared[-1][1], x_both, block)) for block in range(columns // width)
        ])
    grams = jnp.stack([gram(panels[1], panels[0]), gram(panels[2], panels[0]), gram(panels[2], panels[1])])
    grams = lax.psum(grams, "row")
    out = None
    for block in range(columns // width):
        pieces = [piece for index in range(PANELS) for piece in sums[index][block]]
        out, _ = update(places, pieces, tfac, grams, [both for both, _ in prepared], eigvec, out, block, width)
    return out


def solution(mesh):
    in_specs = (P("row", "col"), P("col", "row", None), P(), P())
    out_specs = P("row", "col")
    return jax.shard_map(shards, mesh=mesh, in_specs=in_specs, out_specs=out_specs, check_vma=False)
```

```python
import functools

import jax
import jax.numpy as jnp
from jax import lax
from jax.experimental import pallas as pl
from jax.experimental.pallas import tpu as pltpu
from jax.sharding import PartitionSpec as P

PANELS = 3
BLOCK = 512
LAG = 1
PIECE = 512
MIB = 1024 * 1024
F32 = jnp.float32
BF16 = jnp.bfloat16
ANYWHERE = pl.BlockSpec(memory_space=pl.ANY)
IN_HBM = pl.BlockSpec(memory_space=pltpu.HBM)


def split(value):
    high = value.astype(BF16)
    return high, (value - high.astype(F32)).astype(BF16)


def dot(left, right):
    return jnp.dot(left, right, preferred_element_type=F32)


def dot_three(left, right):
    left_high, left_low = split(left)
    right_high, right_low = split(right)
    return dot(
        jnp.concatenate([left_high, left_low, left_high], axis=1),
        jnp.concatenate([right_high, right_high, right_low], axis=0),
    )


def params(mib):
    return pltpu.CompilerParams(vmem_limit_bytes=mib * MIB)


def cost(flops, count):
    return pl.CostEstimate(flops=flops // 64, bytes_accessed=count // 64, transcendentals=0)


def pinned(value):
    return pltpu.with_memory_space_constraint(value, memory_space=pltpu.HBM)


def split_kernel(x_ref, both_ref):
    blocks, _, _, width = both_ref.shape
    for index in range(blocks):
        both_ref[index, 0], both_ref[index, 1] = split(x_ref[:, index * width : (index + 1) * width])


def split_array(x, width):
    rows, columns = x.shape
    step, blocks = min(rows, 256), columns // width
    return pl.pallas_call(
        split_kernel,
        grid=(rows // step,),
        in_specs=[pl.BlockSpec((step, columns), lambda i: (i, 0))],
        out_specs=pl.BlockSpec((blocks, 2, step, width), lambda i: (0, 0, i, 0)),
        out_shape=pltpu.HBM((blocks, 2, rows, width), BF16),
        compiler_params=params(63),
        cost_estimate=cost(rows * columns * 4, rows * columns * 8),
        name="split_x",
    )(x)


def choose_kernel(outputs, count, which_ref, *refs):
    cases, (panel_ref, split_ref, sem) = refs[:count], refs[-3:]
    use = dict(zip(outputs, refs[-3 - len(outputs) :]))
    half = cases[0].shape[1]
    for side in range(2):
        for index, case in enumerate(cases):

            @pl.when(which_ref[side] == index)
            def _(case=case, side=side):
                copy = pltpu.make_async_copy(case, panel_ref.at[:, side * half : (side + 1) * half], sem)
                copy.start()
                copy.wait()

    rows, width = panel_ref.shape
    step = min(rows, 256)
    for start in range(0, rows, step):
        here = slice(start, start + step)
        value = panel_ref[here, :]
        if "both" in use:
            split_ref[0, 0, here, :], split_ref[0, 1, here, :] = split(value)
        if "flipped" in use:
            high, low = split(value.T)
            use["flipped"][:width, here] = high
            use["flipped"][width:, here] = low
    if "both" in use:
        copy = pltpu.make_async_copy(split_ref, use["both"], sem)
        copy.start()
        copy.wait()


def choose(cases, which, outputs, after=()):
    rows, half = cases[0].shape
    shapes = {"both": (1, 2, rows, 2 * half), "flipped": (4 * half, rows)}
    spaces = {"both": pltpu.HBM, "flipped": pltpu.VMEM}
    return pl.pallas_call(
        functools.partial(choose_kernel, outputs, len(cases)),
        in_specs=[pl.BlockSpec(memory_space=pltpu.SMEM)] + [ANYWHERE] * (len(cases) + len(after)),
        out_specs=[pl.BlockSpec(memory_space=spaces[name]) for name in outputs],
        out_shape=[spaces[name](shapes[name], BF16) for name in outputs],
        scratch_shapes=[
            pltpu.VMEM((rows, 2 * half), F32),
            pltpu.VMEM(shapes["both"], BF16),
            pltpu.SemaphoreType.DMA,
        ],
        compiler_params=params(14),
        cost_estimate=cost(rows * half * 8, rows * half * 24),
        name="choose_panel",
    )(which, *cases, *after)


def products_kernel(block, flipped_ref, both_ref, *refs):
    keep_ref, send_ref, block_ref, sems = refs[-4:]
    half = keep_ref.shape[0]
    rows = block_ref.shape[1] // 2
    copies = []
    for index in range(2):
        here = slice(index * rows, (index + 1) * rows)
        for side in range(2):
            source, target = both_ref.at[block, side, here], block_ref.at[side, here]
            copies.append(pltpu.make_async_copy(source, target, sems.at[index, side]))
            copies[-1].start()
    total = None
    for index in range(2):
        here = slice(index * rows, (index + 1) * rows)
        copies[2 * index].wait()
        with_high = dot(flipped_ref[:, here], block_ref[0, here, :])
        copies[2 * index + 1].wait()
        with_low = dot(flipped_ref[: 2 * half, here], block_ref[1, here, :])
        part = with_high[: 2 * half] + (with_high[2 * half :] + with_low)
        total = part if total is None else total + part
    keep_ref[...] = total[:half]
    send_ref[...] = total[half:]


def products(flipped, both, block, after=()):
    rows, width = both.shape[2:]
    half = flipped.shape[0] // 4
    in_vmem = pl.BlockSpec(memory_space=pltpu.VMEM)
    return pl.pallas_call(
        functools.partial(products_kernel, block),
        in_specs=[in_vmem, IN_HBM] + [ANYWHERE] * len(after),
        out_specs=[in_vmem] * 2,
        out_shape=[jax.ShapeDtypeStruct((half, width), F32)] * 2,
        scratch_shapes=[pltpu.VMEM((2, rows, width), BF16), pltpu.SemaphoreType.DMA((2, 2))],
        compiler_params=params(16),
        cost_estimate=cost(2 * 6 * half * rows * width, rows * width * 4 + 8 * half * rows),
        name="products",
    )(flipped, pinned(both), *after)


def update_kernel(offset, place_ref, *refs):
    sums = refs[:6]
    tfac_ref, gram_ref = refs[6:8]
    panel_refs, x_ref = refs[8:11], refs[11]
    out_ref, done_ref, w_ref, y_ref, y_split_ref = refs[-5:]
    half = sums[0].shape[0]
    width = 2 * half

    @pl.when(pl.program_id(0) == 0)
    def _():
        for index, piece in enumerate(sums):
            start = pl.multiple_of(place_ref[index] * half, half)
            w_ref[pl.ds(start, half), :] = piece[:, offset : offset + w_ref.shape[1]]
        first = dot_three(tfac_ref[0], w_ref[:width, :])
        y_ref[:width, :] = first
        second = dot_three(tfac_ref[1], w_ref[width : 2 * width, :] - dot_three(gram_ref[0], first))
        y_ref[width : 2 * width, :] = second
        third = w_ref[2 * width :, :] - dot_three(gram_ref[1], first) - dot_three(gram_ref[2], second)
        y_ref[2 * width :, :] = dot_three(tfac_ref[2], third)
        for index in range(6):
            start = pl.multiple_of(place_ref[index] * half, half)
            high, low = split(y_ref[pl.ds(start, half), :])
            for number, value in enumerate((high, high, low)):
                y_split_ref[(6 * number + index) * half : (6 * number + index + 1) * half, :] = value

    sides = [ref[0, side] for side in (0, 1, 0) for ref in panel_refs]
    out_ref[...] = x_ref[...] - dot(jnp.concatenate(sides, axis=1), y_split_ref[...])
    done_ref[...] = jnp.zeros(done_ref.shape, F32)


def update(place, sums, tfac, grams, panels, x, out, block, width, offset=0):
    rows, columns = x.shape
    half = sums[0].shape[0]
    step = min(rows, 512)
    panel_spec = pl.BlockSpec((1, 2, step, 2 * half), lambda i, place: (0, 0, i, 0))
    block_spec = pl.BlockSpec((step, width), lambda i, place: (i, block))
    operands = [place, *sums, tfac, grams, *map(pinned, panels), x]
    in_specs = (
        [pl.BlockSpec(memory_space=pltpu.VMEM)] * 8
        + [panel_spec] * 3
        + [block_spec]
    )
    aliases = {}
    if out is not None:
        aliases = {len(operands): 0}
        operands.append(out)
        in_specs.append(IN_HBM)
    return pl.pallas_call(
        functools.partial(update_kernel, offset),
        grid_spec=pltpu.PrefetchScalarGridSpec(
            num_scalar_prefetch=1,
            grid=(rows // step,),
            in_specs=in_specs,
            out_specs=[block_spec, pl.BlockSpec((8, 128), lambda i, place: (0, 0))],
            scratch_shapes=[
                pltpu.VMEM((6 * half, width), F32),
                pltpu.VMEM((6 * half, width), F32),
                pltpu.VMEM((18 * half, width), BF16),
            ],
        ),
        out_shape=[jax.ShapeDtypeStruct(x.shape, F32), jax.ShapeDtypeStruct((8, 128), F32)],
        input_output_aliases=aliases,
        compiler_params=params(40),
        cost_estimate=cost(2 * 18 * half * rows * width, rows * width * 8 + rows * half * 24),
        name="update",
    )(*operands)


def pairs_of(count, step):
    return [(index, index ^ step) for index in range(count)]


def swap_cores(value):
    return lax.ppermute(value, "row", pairs_of(lax.axis_size("row"), 1))


def both_cores(chip_pairs):
    return [(2 * a + core, 2 * b + core) for a, b in chip_pairs for core in range(2)]


def sum_over_rows(keep, send):
    chips = lax.axis_size("row") // 2
    chip = lax.axis_index("row") // 2
    total = keep + swap_cores(send)
    for hop in range(chips // 2 - 1):
        pairs = [(hop, hop + 1), (chips - 1 - hop, chips - 2 - hop)]
        total = total + lax.ppermute(total, "row", both_cores(pairs))
    middle = [(chips // 2 - 1, chips // 2), (chips // 2, chips // 2 - 1)]
    total = total + lax.ppermute(total, "row", both_cores(middle))
    for hop in reversed(range(chips // 2 - 1)):
        pairs = [(hop + 1, hop), (chips - 2 - hop, chips - 1 - hop)]
        arrived = lax.ppermute(total, "row", both_cores(pairs))
        total = jnp.where((chip == hop) | (chip == chips - 1 - hop), arrived, total)
    return total, swap_cores(total)


def pick(index, *cases):
    return lax.select_n(index, *cases)


def fetch_square(slot, roots):
    half = slot.shape[1] // 2
    me = lax.axis_index("col")
    along = lambda value, step: lax.ppermute(value, "col", pairs_of(4, step))
    own = [slot[:, :half], slot[:, half:]]
    near, far = [], []
    for piece in own:
        near.append(along(piece, 1))
        far.append(along(piece, 2))
    cross = [along(far[0], 1), along(near[1], 2)]
    spare = (roots[0] + 3) % 4
    case = me ^ spare
    rounds = [
        ((*own, near[0], far[0]), jnp.array([[2, 3], [0, 1], [0, 1], [0, 1]], jnp.int32)[case]),
        ((*near, *far), jnp.array([[1, 3], [2, 3], [0, 1], [0, 2]], jnp.int32)[case]),
        ((*cross, near[1], far[1]), jnp.array([[0, 1], [0, 1], [0, 1], [2, 3]], jnp.int32)[case]),
    ]
    slots = jnp.array([[1, 2, 1, 2, 3, 3], [0, 0, 2, 2, 3, 3], [0, 0, 1, 1, 3, 3], [0, 0, 1, 2, 1, 2]], jnp.int32)
    halves = jnp.array([[0, 0, 1, 1, 0, 1], [0, 1, 0, 1, 0, 1], [0, 1, 0, 1, 0, 1], [0, 1, 0, 0, 1, 1]], jnp.int32)
    panel = ((slots[case] ^ me) - roots[0]) % 4
    places = panel * 2 + halves[case]
    later_of = jnp.array([[0, 1, 0, 0], [1, 0, 2, 2]], jnp.int32)[roots[0] - 2, me]
    earlier_of = jnp.array([[2, 2, 0, 1], [0, 0, 1, 0]], jnp.int32)[roots[0] - 2, me]
    both = jnp.arange(2, dtype=jnp.int32)
    later = ((*own, *near, *far), 2 * later_of + both)
    earlier = ((*own, *near, *far), 2 * earlier_of + both)
    holders = jnp.array([[3, 0, 1], [2, 3, 0]], jnp.int32)[roots[0] - 2]
    return rounds, places, later, earlier, holders


def fetch_any(slot, roots):
    half = slot.shape[1] // 2
    me = lax.axis_index("col")
    panels = [lax.psum(jnp.where(me == roots[index], slot, jnp.zeros_like(slot)), "col") for index in range(PANELS)]
    rounds = [(panel[:, :half], panel[:, half:]) for panel in panels]
    return rounds, jnp.arange(2 * PANELS, dtype=jnp.int32), panels


def gram(left, right):
    return lax.dot_general(
        left, right, (((0,), (0,)), ((), ())), precision=lax.Precision.HIGH, preferred_element_type=F32
    )


def exchange_kernel(names, pieces, ends_ref, *refs):
    use = dict(zip(names, refs))
    end = ends_ref[0] == 1
    if "acc" in use:
        start = 0
        for index in range(pieces):
            keep, swapped = use["keep", index], use["swapped", index]
            columns = slice(start, start + keep.shape[1])
            use["acc"][:, columns] = keep[...] + swapped[...]
            start = columns.stop
    if "part" in use:
        columns = use["part"].shape[1]
        use["part"][...] = use["acc_before"][...] + use["outer"][:, :columns]
    if "total" in use:
        use["total"][...] = use["part_before"][...] + use["inner"][...]
    if "final" in use:
        columns = use["final"].shape[1]
        use["final"][...] = jnp.where(end, use["outer"][:, :columns], use["total_before"][...])
    if "out" in use:
        sources = [use[name] for name in ("acc", "total") if name in use]
        if len(sources) == 1:
            use["out"][...] = sources[0][...]
        else:
            both = min(source.shape[1] for source in sources)
            use["out"][:, :both] = jnp.where(end, sources[0][:, :both], sources[1][:, :both])
            for source in sources:
                if source.shape[1] > both:
                    use["out"][:, both:] = source[:, both:]


def exchange(ends, operands, shapes, after):
    names = list(operands) + [None] * len(after) + list(shapes)
    pieces = sum(name[0] == "keep" for name in operands)
    in_vmem = pl.BlockSpec(memory_space=pltpu.VMEM)
    results = pl.pallas_call(
        functools.partial(exchange_kernel, names, pieces),
        in_specs=[pl.BlockSpec(memory_space=pltpu.SMEM)] + [in_vmem] * len(operands)
        + [ANYWHERE] * len(after),
        out_specs=[in_vmem] * len(shapes),
        out_shape=[jax.ShapeDtypeStruct(shape, F32) for shape in shapes.values()],
        compiler_params=params(14),
        cost_estimate=cost(0, 0),
        name="exchange",
    )(ends, *operands.values(), *after)
    return dict(zip(shapes, results))


def shards_square(eigvec, slot, roots, tfac):
    columns = eigvec.shape[1]
    width, half = columns // 2, slot.shape[1] // 2
    rounds, places, later, earlier, holders = fetch_square(slot, roots)
    chip, core = lax.axis_index("row") // 2, lax.axis_index("row") % 2
    ends = jnp.where((chip == 0) | (chip == 3), 1, 0).astype(jnp.int32).reshape(1)
    places = jnp.where(core == 0, places, places.reshape(PANELS, 2)[:, ::-1].reshape(-1))
    ordered = lambda pair: jnp.where(core == 0, pair, pair[::-1])
    x_both = split_array(eigvec, PIECE)
    chunks = [(0, 0), (0, 1), (1, 0), (2, 0), (1, 1), (2, 1)]
    count = len(chunks)
    gram_chunk = 2
    prepared, arrived, sizes, gram_sides = {}, {}, {}, []

    def start(number, after):
        index, block = chunks[number]
        pieces = []
        if index not in prepared:
            cases, which = rounds[index]
            prepared[index] = choose(cases, ordered(which), ("both", "flipped"), after)
        for part in range(width // PIECE):
            pieces.append(products(prepared[index][1], x_both, block * (width // PIECE) + part, after))
        if number == gram_chunk - 1:
            gram_sides.append(choose(later[0], ordered(later[1]), ("flipped",), after)[0])
            gram_sides.append(choose(*earlier, ("both",), after)[0])
        if number == gram_chunk:
            pieces.append(products(*gram_sides, 0, after))
        arrived[number] = [(mine, swap_cores(other)) for mine, other in pieces]
        sizes[number] = (half, sum(mine.shape[1] for mine, other in pieces))

    outer_pairs = both_cores([(0, 1), (1, 0), (2, 3), (3, 2)])
    inner_pairs = both_cores([(1, 2), (2, 1)])
    acc, part, total, outer, inner, sums = {}, {}, {}, {}, {}, {}
    grams, out = None, None
    start(0, ())
    for step in range(count + 3 * LAG):
        operands, shapes = {}, {}
        inward, middle, outward = step - LAG, step - 2 * LAG, step - 3 * LAG
        if step < count:
            for number, (mine, other) in enumerate(arrived[step]):
                operands["keep", number], operands["swapped", number] = mine, other
            shapes["acc"] = sizes[step]
        if step - LAG in outer:
            operands["outer"] = outer[step - LAG]
        if 0 <= inward < count:
            operands["acc_before"] = acc[inward]
            shapes["part"] = sizes[inward]
        if 0 <= middle < count:
            operands["part_before"], operands["inner"] = part[middle], inner[step - LAG]
            shapes["total"] = sizes[middle]
        if 0 <= outward < count:
            operands["total_before"] = total[outward]
            shapes["final"] = sizes[outward]
        sent = [shapes[name] for name in ("acc", "total") if name in shapes]
        if sent:
            shapes["out"] = max(sent, key=lambda shape: shape[1])
        ahead = [] if out is None else [finished]
        if step == gram_chunk - 1:
            ahead.extend([gram_sides[0], pinned(gram_sides[1])])
        if 0 <= outward - 1 < count - 2:
            ahead.append(sums[chunks[outward - 1]][1])
        results = exchange(ends, operands, shapes, ahead)
        if "out" in results:
            outer[step] = lax.ppermute(results["out"], "row", outer_pairs)
        if "acc" in results:
            acc[step] = results["acc"]
        if "part" in results:
            part[inward] = results["part"]
            inner[step] = lax.ppermute(results["part"], "row", inner_pairs)
        if "total" in results:
            total[middle] = results["total"]
        if step + 1 < count:
            start(step + 1, [next(iter(results.values()))])
        if "final" in results:
            done = outward
            own, other = results["final"], swap_cores(results["final"])
            if done == gram_chunk:
                pair = own[:, width:], other[:, width:]
                block = jnp.where(core == 0, jnp.concatenate(pair, axis=0), jnp.concatenate(pair[::-1], axis=0))
                spread = [block] + [lax.ppermute(block, "col", pairs_of(4, shift)) for shift in range(1, 4)]
                places_of = holders ^ lax.axis_index("col")
                grams = jnp.stack([pick(places_of[number], *spread) for number in range(PANELS)])
            sums[chunks[done]] = (own, other)
            index, block = chunks[done]
            ready = block if index == PANELS - 1 else 0
            if step >= count:
                pieces = [piece for panel in range(PANELS) for piece in sums[panel, ready]]
                panels = [prepared[panel][0] for panel in range(PANELS)]
                if ready == 0:
                    place, size, offset = step - count, width // 2, (step - count) * (width // 2)
                else:
                    place, size, offset = 1, width, 0
                out, finished = update(places, pieces, tfac, grams, panels, eigvec, out, place, size, offset)
    return out


def shards(eigvec, slots, roots, tfac):
    if lax.axis_size("col") == 4 and lax.axis_size("row") == 8:
        return shards_square(eigvec, slots[0], roots, tfac)
    columns = eigvec.shape[1]
    width = min(columns, BLOCK)
    rounds, places, panels = fetch_any(slots[0], roots)
    core = lax.axis_index("row") % 2
    places = jnp.where(core == 0, places, places.reshape(PANELS, 2)[:, ::-1].reshape(-1))
    x_both = split_array(eigvec, width)
    prepared, sums = [], []
    for pair in rounds:
        which = jnp.where(core == 0, jnp.arange(2), jnp.arange(1, -1, -1)).astype(jnp.int32)
        prepared.append(choose(pair, which, ("both", "flipped")))
        sums.append([
            sum_over_rows(*products(prepared[-1][1], x_both, block)) for block in range(columns // width)
        ])
    grams = jnp.stack([gram(panels[1], panels[0]), gram(panels[2], panels[0]), gram(panels[2], panels[1])])
    grams = lax.psum(grams, "row")
    out = None
    for block in range(columns // width):
        pieces = [piece for index in range(PANELS) for piece in sums[index][block]]
        out, _ = update(places, pieces, tfac, grams, [both for both, _ in prepared], eigvec, out, block, width)
    return out


def solution(mesh):
    in_specs = (P("row", "col"), P("col", "row", None), P(), P())
    out_specs = P("row", "col")
    return jax.shard_map(shards, mesh=mesh, in_specs=in_specs, out_specs=out_specs, check_vma=False)
```

```python
import functools

import jax
import jax.numpy as jnp
from jax import lax
from jax.experimental import pallas as pl
from jax.experimental.pallas import tpu as pltpu
from jax.sharding import PartitionSpec as P

PANELS = 3
BLOCK = 512
LAG = 1
PIECE = 512
MIB = 1024 * 1024
F32 = jnp.float32
BF16 = jnp.bfloat16
ANYWHERE = pl.BlockSpec(memory_space=pl.ANY)
IN_HBM = pl.BlockSpec(memory_space=pltpu.HBM)


def split(value):
    high = value.astype(BF16)
    return high, (value - high.astype(F32)).astype(BF16)


def dot(left, right):
    return jnp.dot(left, right, preferred_element_type=F32)


def dot_three(left, right):
    left_high, left_low = split(left)
    right_high, right_low = split(right)
    return dot(
        jnp.concatenate([left_high, left_low, left_high], axis=1),
        jnp.concatenate([right_high, right_high, right_low], axis=0),
    )


def params(mib):
    return pltpu.CompilerParams(vmem_limit_bytes=mib * MIB)


def cost(flops, count):
    return pl.CostEstimate(flops=flops // 64, bytes_accessed=count // 64, transcendentals=0)


def pinned(value):
    return pltpu.with_memory_space_constraint(value, memory_space=pltpu.HBM)


def split_kernel(x_ref, both_ref):
    blocks, _, _, width = both_ref.shape
    for index in range(blocks):
        both_ref[index, 0], both_ref[index, 1] = split(x_ref[:, index * width : (index + 1) * width])


def split_array(x, width):
    rows, columns = x.shape
    step, blocks = min(rows, 256), columns // width
    return pl.pallas_call(
        split_kernel,
        grid=(rows // step,),
        in_specs=[pl.BlockSpec((step, columns), lambda i: (i, 0))],
        out_specs=pl.BlockSpec((blocks, 2, step, width), lambda i: (0, 0, i, 0)),
        out_shape=pltpu.HBM((blocks, 2, rows, width), BF16),
        compiler_params=params(63),
        cost_estimate=cost(rows * columns * 4, rows * columns * 8),
        name="split_x",
    )(x)


def choose_kernel(outputs, count, which_ref, *refs):
    cases, (panel_ref, split_ref, sem) = refs[:count], refs[-3:]
    use = dict(zip(outputs, refs[-3 - len(outputs) :]))
    half = cases[0].shape[1]
    for side in range(2):
        for index, case in enumerate(cases):

            @pl.when(which_ref[side] == index)
            def _(case=case, side=side):
                copy = pltpu.make_async_copy(case, panel_ref.at[:, side * half : (side + 1) * half], sem)
                copy.start()
                copy.wait()

    rows, width = panel_ref.shape
    step = min(rows, 256)
    for start in range(0, rows, step):
        here = slice(start, start + step)
        value = panel_ref[here, :]
        if "both" in use:
            split_ref[0, 0, here, :], split_ref[0, 1, here, :] = split(value)
        if "flipped" in use:
            high, low = split(value.T)
            use["flipped"][:width, here] = high
            use["flipped"][width:, here] = low
    if "both" in use:
        copy = pltpu.make_async_copy(split_ref, use["both"], sem)
        copy.start()
        copy.wait()


def choose(cases, which, outputs, after=()):
    rows, half = cases[0].shape
    shapes = {"both": (1, 2, rows, 2 * half), "flipped": (4 * half, rows)}
    spaces = {"both": pltpu.HBM, "flipped": pltpu.VMEM}
    return pl.pallas_call(
        functools.partial(choose_kernel, outputs, len(cases)),
        in_specs=[pl.BlockSpec(memory_space=pltpu.SMEM)] + [ANYWHERE] * (len(cases) + len(after)),
        out_specs=[pl.BlockSpec(memory_space=spaces[name]) for name in outputs],
        out_shape=[spaces[name](shapes[name], BF16) for name in outputs],
        scratch_shapes=[
            pltpu.VMEM((rows, 2 * half), F32),
            pltpu.VMEM(shapes["both"], BF16),
            pltpu.SemaphoreType.DMA,
        ],
        compiler_params=params(14),
        cost_estimate=cost(rows * half * 8, rows * half * 24),
        name="choose_panel",
    )(which, *cases, *after)


def products_kernel(block, flipped_ref, both_ref, *refs):
    keep_ref, send_ref, block_ref, sems = refs[-4:]
    half = keep_ref.shape[0]
    rows = block_ref.shape[1] // 2
    copies = []
    for index in range(2):
        here = slice(index * rows, (index + 1) * rows)
        for side in range(2):
            source, target = both_ref.at[block, side, here], block_ref.at[side, here]
            copies.append(pltpu.make_async_copy(source, target, sems.at[index, side]))
            copies[-1].start()
    total = None
    for index in range(2):
        here = slice(index * rows, (index + 1) * rows)
        copies[2 * index].wait()
        with_high = dot(flipped_ref[:, here], block_ref[0, here, :])
        copies[2 * index + 1].wait()
        with_low = dot(flipped_ref[: 2 * half, here], block_ref[1, here, :])
        part = with_high[: 2 * half] + (with_high[2 * half :] + with_low)
        total = part if total is None else total + part
    keep_ref[...] = total[:half]
    send_ref[...] = total[half:]


def products(flipped, both, block, after=()):
    rows, width = both.shape[2:]
    half = flipped.shape[0] // 4
    in_vmem = pl.BlockSpec(memory_space=pltpu.VMEM)
    return pl.pallas_call(
        functools.partial(products_kernel, block),
        in_specs=[in_vmem, IN_HBM] + [ANYWHERE] * len(after),
        out_specs=[in_vmem] * 2,
        out_shape=[jax.ShapeDtypeStruct((half, width), F32)] * 2,
        scratch_shapes=[pltpu.VMEM((2, rows, width), BF16), pltpu.SemaphoreType.DMA((2, 2))],
        compiler_params=params(16),
        cost_estimate=cost(2 * 6 * half * rows * width, rows * width * 4 + 8 * half * rows),
        name="products",
    )(flipped, pinned(both), *after)


def update_kernel(offset, place_ref, *refs):
    sums = refs[:6]
    tfac_ref, gram_ref = refs[6:8]
    panel_refs, x_ref = refs[8:11], refs[11]
    out_ref, done_ref, w_ref, y_ref, y_split_ref = refs[-5:]
    half = sums[0].shape[0]
    width = 2 * half

    @pl.when(pl.program_id(0) == 0)
    def _():
        for index, piece in enumerate(sums):
            start = pl.multiple_of(place_ref[index] * half, half)
            w_ref[pl.ds(start, half), :] = piece[:, offset : offset + w_ref.shape[1]]
        first = dot_three(tfac_ref[0], w_ref[:width, :])
        y_ref[:width, :] = first
        second = dot_three(tfac_ref[1], w_ref[width : 2 * width, :] - dot_three(gram_ref[0], first))
        y_ref[width : 2 * width, :] = second
        third = w_ref[2 * width :, :] - dot_three(gram_ref[1], first) - dot_three(gram_ref[2], second)
        y_ref[2 * width :, :] = dot_three(tfac_ref[2], third)
        for index in range(6):
            start = pl.multiple_of(place_ref[index] * half, half)
            high, low = split(y_ref[pl.ds(start, half), :])
            for number, value in enumerate((high, high, low)):
                y_split_ref[(6 * number + index) * half : (6 * number + index + 1) * half, :] = value

    sides = [ref[0, side] for side in (0, 1, 0) for ref in panel_refs]
    out_ref[...] = x_ref[...] - dot(jnp.concatenate(sides, axis=1), y_split_ref[...])
    done_ref[...] = jnp.zeros(done_ref.shape, F32)


def update(place, sums, tfac, grams, panels, x, out, block, width, offset=0):
    rows, columns = x.shape
    half = sums[0].shape[0]
    step = min(rows, 512)
    panel_spec = pl.BlockSpec((1, 2, step, 2 * half), lambda i, place: (0, 0, i, 0))
    block_spec = pl.BlockSpec((step, width), lambda i, place: (i, block))
    operands = [place, *sums, tfac, grams, *map(pinned, panels), x]
    in_specs = (
        [pl.BlockSpec(memory_space=pltpu.VMEM)] * 8
        + [panel_spec] * 3
        + [block_spec]
    )
    aliases = {}
    if out is not None:
        aliases = {len(operands): 0}
        operands.append(out)
        in_specs.append(IN_HBM)
    return pl.pallas_call(
        functools.partial(update_kernel, offset),
        grid_spec=pltpu.PrefetchScalarGridSpec(
            num_scalar_prefetch=1,
            grid=(rows // step,),
            in_specs=in_specs,
            out_specs=[block_spec, pl.BlockSpec((8, 128), lambda i, place: (0, 0))],
            scratch_shapes=[
                pltpu.VMEM((6 * half, width), F32),
                pltpu.VMEM((6 * half, width), F32),
                pltpu.VMEM((18 * half, width), BF16),
            ],
        ),
        out_shape=[jax.ShapeDtypeStruct(x.shape, F32), jax.ShapeDtypeStruct((8, 128), F32)],
        input_output_aliases=aliases,
        compiler_params=params(40),
        cost_estimate=cost(2 * 18 * half * rows * width, rows * width * 8 + rows * half * 24),
        name="update",
    )(*operands)


def pairs_of(count, step):
    return [(index, index ^ step) for index in range(count)]


def swap_cores(value):
    return lax.ppermute(value, "row", pairs_of(lax.axis_size("row"), 1))


def both_cores(chip_pairs):
    return [(2 * a + core, 2 * b + core) for a, b in chip_pairs for core in range(2)]


def sum_over_rows(keep, send):
    chips = lax.axis_size("row") // 2
    chip = lax.axis_index("row") // 2
    total = keep + swap_cores(send)
    for hop in range(chips // 2 - 1):
        pairs = [(hop, hop + 1), (chips - 1 - hop, chips - 2 - hop)]
        total = total + lax.ppermute(total, "row", both_cores(pairs))
    middle = [(chips // 2 - 1, chips // 2), (chips // 2, chips // 2 - 1)]
    total = total + lax.ppermute(total, "row", both_cores(middle))
    for hop in reversed(range(chips // 2 - 1)):
        pairs = [(hop + 1, hop), (chips - 2 - hop, chips - 1 - hop)]
        arrived = lax.ppermute(total, "row", both_cores(pairs))
        total = jnp.where((chip == hop) | (chip == chips - 1 - hop), arrived, total)
    return total, swap_cores(total)


def pick(index, *cases):
    return lax.select_n(index, *cases)


def fetch_square(slot, roots):
    half = slot.shape[1] // 2
    me = lax.axis_index("col")
    along = lambda value, step: lax.ppermute(value, "col", pairs_of(4, step))
    own = [slot[:, :half], slot[:, half:]]
    near, far = [], []
    for piece in own:
        near.append(along(piece, 1))
        far.append(along(piece, 2))
    cross = [along(far[0], 1), along(near[1], 2)]
    spare = (roots[0] + 3) % 4
    case = me ^ spare
    rounds = [
        ((*own, near[0], far[0]), jnp.array([[2, 3], [0, 1], [0, 1], [0, 1]], jnp.int32)[case]),
        ((*near, *far), jnp.array([[1, 3], [2, 3], [0, 1], [0, 2]], jnp.int32)[case]),
        ((*cross, near[1], far[1]), jnp.array([[0, 1], [0, 1], [0, 1], [2, 3]], jnp.int32)[case]),
    ]
    slots = jnp.array([[1, 2, 1, 2, 3, 3], [0, 0, 2, 2, 3, 3], [0, 0, 1, 1, 3, 3], [0, 0, 1, 2, 1, 2]], jnp.int32)
    halves = jnp.array([[0, 0, 1, 1, 0, 1], [0, 1, 0, 1, 0, 1], [0, 1, 0, 1, 0, 1], [0, 1, 0, 0, 1, 1]], jnp.int32)
    panel = ((slots[case] ^ me) - roots[0]) % 4
    places = panel * 2 + halves[case]
    later_of = jnp.array([[0, 1, 0, 0], [1, 0, 2, 2]], jnp.int32)[roots[0] - 2, me]
    earlier_of = jnp.array([[2, 2, 0, 1], [0, 0, 1, 0]], jnp.int32)[roots[0] - 2, me]
    both = jnp.arange(2, dtype=jnp.int32)
    later = ((*own, *near, *far), 2 * later_of + both)
    earlier = ((*own, *near, *far), 2 * earlier_of + both)
    holders = jnp.array([[3, 0, 1], [2, 3, 0]], jnp.int32)[roots[0] - 2]
    return rounds, places, later, earlier, holders


def fetch_any(slot, roots):
    half = slot.shape[1] // 2
    me = lax.axis_index("col")
    panels = [lax.psum(jnp.where(me == roots[index], slot, jnp.zeros_like(slot)), "col") for index in range(PANELS)]
    rounds = [(panel[:, :half], panel[:, half:]) for panel in panels]
    return rounds, jnp.arange(2 * PANELS, dtype=jnp.int32), panels


def gram(left, right):
    return lax.dot_general(
        left, right, (((0,), (0,)), ((), ())), precision=lax.Precision.HIGH, preferred_element_type=F32
    )


def exchange_kernel(names, pieces, ends_ref, *refs):
    use = dict(zip(names, refs))
    end = ends_ref[0] == 1
    if "acc" in use:
        start = 0
        for index in range(pieces):
            keep, swapped = use["keep", index], use["swapped", index]
            columns = slice(start, start + keep.shape[1])
            use["acc"][:, columns] = keep[...] + swapped[...]
            start = columns.stop
    if "part" in use:
        columns = use["part"].shape[1]
        use["part"][...] = use["acc_before"][...] + use["outer"][:, :columns]
    if "total" in use:
        use["total"][...] = use["part_before"][...] + use["inner"][...]
    if "final" in use:
        columns = use["final"].shape[1]
        use["final"][...] = jnp.where(end, use["outer"][:, :columns], use["total_before"][...])
    if "out" in use:
        sources = [use[name] for name in ("acc", "total") if name in use]
        if len(sources) == 1:
            use["out"][...] = sources[0][...]
        else:
            both = min(source.shape[1] for source in sources)
            use["out"][:, :both] = jnp.where(end, sources[0][:, :both], sources[1][:, :both])
            for source in sources:
                if source.shape[1] > both:
                    use["out"][:, both:] = source[:, both:]


def exchange(ends, operands, shapes, after):
    names = list(operands) + [None] * len(after) + list(shapes)
    pieces = sum(name[0] == "keep" for name in operands)
    in_vmem = pl.BlockSpec(memory_space=pltpu.VMEM)
    results = pl.pallas_call(
        functools.partial(exchange_kernel, names, pieces),
        in_specs=[pl.BlockSpec(memory_space=pltpu.SMEM)] + [in_vmem] * len(operands)
        + [ANYWHERE] * len(after),
        out_specs=[in_vmem] * len(shapes),
        out_shape=[jax.ShapeDtypeStruct(shape, F32) for shape in shapes.values()],
        compiler_params=params(14),
        cost_estimate=cost(0, 0),
        name="exchange",
    )(ends, *operands.values(), *after)
    return dict(zip(shapes, results))


def shards_square(eigvec, slot, roots, tfac):
    columns = eigvec.shape[1]
    width, half = columns // 2, slot.shape[1] // 2
    rounds, places, later, earlier, holders = fetch_square(slot, roots)
    chip, core = lax.axis_index("row") // 2, lax.axis_index("row") % 2
    ends = jnp.where((chip == 0) | (chip == 3), 1, 0).astype(jnp.int32).reshape(1)
    places = jnp.where(core == 0, places, places.reshape(PANELS, 2)[:, ::-1].reshape(-1))
    ordered = lambda pair: jnp.where(core == 0, pair, pair[::-1])
    x_both = split_array(eigvec, PIECE)
    chunks = [(0, 0), (0, 1), (1, 0), (2, 0), (1, 1), (2, 1)]
    count = len(chunks)
    gram_chunk = 3
    prepared, arrived, sizes, gram_sides = {}, {}, {}, []

    def start(number, after):
        index, block = chunks[number]
        pieces = []
        if index not in prepared:
            cases, which = rounds[index]
            prepared[index] = choose(cases, ordered(which), ("both", "flipped"), after)
        for part in range(width // PIECE):
            pieces.append(products(prepared[index][1], x_both, block * (width // PIECE) + part, after))
        if number == gram_chunk - 1:
            gram_sides.append(choose(later[0], ordered(later[1]), ("flipped",), after)[0])
            gram_sides.append(choose(*earlier, ("both",), after)[0])
        if number == gram_chunk:
            pieces.append(products(*gram_sides, 0, after))
        arrived[number] = [(mine, swap_cores(other)) for mine, other in pieces]
        sizes[number] = (half, sum(mine.shape[1] for mine, other in pieces))

    outer_pairs = both_cores([(0, 1), (1, 0), (2, 3), (3, 2)])
    inner_pairs = both_cores([(1, 2), (2, 1)])
    acc, part, total, outer, inner, sums = {}, {}, {}, {}, {}, {}
    grams, out = None, None
    start(0, ())
    for step in range(count + 3 * LAG):
        operands, shapes = {}, {}
        inward, middle, outward = step - LAG, step - 2 * LAG, step - 3 * LAG
        if step < count:
            for number, (mine, other) in enumerate(arrived[step]):
                operands["keep", number], operands["swapped", number] = mine, other
            shapes["acc"] = sizes[step]
        if step - LAG in outer:
            operands["outer"] = outer[step - LAG]
        if 0 <= inward < count:
            operands["acc_before"] = acc[inward]
            shapes["part"] = sizes[inward]
        if 0 <= middle < count:
            operands["part_before"], operands["inner"] = part[middle], inner[step - LAG]
            shapes["total"] = sizes[middle]
        if 0 <= outward < count:
            operands["total_before"] = total[outward]
            shapes["final"] = sizes[outward]
        sent = [shapes[name] for name in ("acc", "total") if name in shapes]
        if sent:
            shapes["out"] = max(sent, key=lambda shape: shape[1])
        ahead = [] if out is None else [finished]
        if step == gram_chunk - 1:
            ahead.extend([gram_sides[0], pinned(gram_sides[1])])
        if 0 <= outward - 1 < count - 2:
            ahead.append(sums[chunks[outward - 1]][1])
        results = exchange(ends, operands, shapes, ahead)
        if "out" in results:
            outer[step] = lax.ppermute(results["out"], "row", outer_pairs)
        if "acc" in results:
            acc[step] = results["acc"]
        if "part" in results:
            part[inward] = results["part"]
            inner[step] = lax.ppermute(results["part"], "row", inner_pairs)
        if "total" in results:
            total[middle] = results["total"]
        if step + 1 < count:
            start(step + 1, [next(iter(results.values()))])
        if "final" in results:
            done = outward
            own, other = results["final"], swap_cores(results["final"])
            if done == gram_chunk:
                pair = own[:, width:], other[:, width:]
                block = jnp.where(core == 0, jnp.concatenate(pair, axis=0), jnp.concatenate(pair[::-1], axis=0))
                spread = [block] + [lax.ppermute(block, "col", pairs_of(4, shift)) for shift in range(1, 4)]
                places_of = holders ^ lax.axis_index("col")
                grams = jnp.stack([pick(places_of[number], *spread) for number in range(PANELS)])
            sums[chunks[done]] = (own, other)
            index, block = chunks[done]
            ready = block if index == PANELS - 1 else 0
            if step >= count:
                pieces = [piece for panel in range(PANELS) for piece in sums[panel, ready]]
                panels = [prepared[panel][0] for panel in range(PANELS)]
                if ready == 0:
                    place, size, offset = step - count, width // 2, (step - count) * (width // 2)
                else:
                    place, size, offset = 1, width, 0
                out, finished = update(places, pieces, tfac, grams, panels, eigvec, out, place, size, offset)
    return out


def shards(eigvec, slots, roots, tfac):
    if lax.axis_size("col") == 4 and lax.axis_size("row") == 8:
        return shards_square(eigvec, slots[0], roots, tfac)
    columns = eigvec.shape[1]
    width = min(columns, BLOCK)
    rounds, places, panels = fetch_any(slots[0], roots)
    core = lax.axis_index("row") % 2
    places = jnp.where(core == 0, places, places.reshape(PANELS, 2)[:, ::-1].reshape(-1))
    x_both = split_array(eigvec, width)
    prepared, sums = [], []
    for pair in rounds:
        which = jnp.where(core == 0, jnp.arange(2), jnp.arange(1, -1, -1)).astype(jnp.int32)
        prepared.append(choose(pair, which, ("both", "flipped")))
        sums.append([
            sum_over_rows(*products(prepared[-1][1], x_both, block)) for block in range(columns // width)
        ])
    grams = jnp.stack([gram(panels[1], panels[0]), gram(panels[2], panels[0]), gram(panels[2], panels[1])])
    grams = lax.psum(grams, "row")
    out = None
    for block in range(columns // width):
        pieces = [piece for index in range(PANELS) for piece in sums[index][block]]
        out, _ = update(places, pieces, tfac, grams, [both for both, _ in prepared], eigvec, out, block, width)
    return out


def solution(mesh):
    in_specs = (P("row", "col"), P("col", "row", None), P(), P())
    out_specs = P("row", "col")
    return jax.shard_map(shards, mesh=mesh, in_specs=in_specs, out_specs=out_specs, check_vma=False)
```

```python
import functools

import jax
import jax.numpy as jnp
from jax import lax
from jax.experimental import pallas as pl
from jax.experimental.pallas import tpu as pltpu
from jax.sharding import PartitionSpec as P

PANELS = 3
BLOCK = 512
LAG = 1
PIECE = 512
MIB = 1024 * 1024
F32 = jnp.float32
BF16 = jnp.bfloat16
ANYWHERE = pl.BlockSpec(memory_space=pl.ANY)
IN_HBM = pl.BlockSpec(memory_space=pltpu.HBM)


def split(value):
    high = value.astype(BF16)
    return high, (value - high.astype(F32)).astype(BF16)


def dot(left, right):
    return jnp.dot(left, right, preferred_element_type=F32)


def dot_three(left, right):
    left_high, left_low = split(left)
    right_high, right_low = split(right)
    return dot(
        jnp.concatenate([left_high, left_low, left_high], axis=1),
        jnp.concatenate([right_high, right_high, right_low], axis=0),
    )


def params(mib):
    return pltpu.CompilerParams(vmem_limit_bytes=mib * MIB)


def cost(flops, count):
    return pl.CostEstimate(flops=flops // 64, bytes_accessed=count // 64, transcendentals=0)


def pinned(value):
    return pltpu.with_memory_space_constraint(value, memory_space=pltpu.HBM)


def split_kernel(x_ref, both_ref):
    blocks, _, _, width = both_ref.shape
    for index in range(blocks):
        both_ref[index, 0], both_ref[index, 1] = split(x_ref[:, index * width : (index + 1) * width])


def split_array(x, width):
    rows, columns = x.shape
    step, blocks = min(rows, 256), columns // width
    return pl.pallas_call(
        split_kernel,
        grid=(rows // step,),
        in_specs=[pl.BlockSpec((step, columns), lambda i: (i, 0))],
        out_specs=pl.BlockSpec((blocks, 2, step, width), lambda i: (0, 0, i, 0)),
        out_shape=pltpu.HBM((blocks, 2, rows, width), BF16),
        compiler_params=params(63),
        cost_estimate=cost(rows * columns * 4, rows * columns * 8),
        name="split_x",
    )(x)


def choose_kernel(outputs, count, which_ref, *refs):
    cases, (panel_ref, split_ref, sem) = refs[:count], refs[-3:]
    use = dict(zip(outputs, refs[-3 - len(outputs) :]))
    half = cases[0].shape[1]
    for side in range(2):
        for index, case in enumerate(cases):

            @pl.when(which_ref[side] == index)
            def _(case=case, side=side):
                copy = pltpu.make_async_copy(case, panel_ref.at[:, side * half : (side + 1) * half], sem)
                copy.start()
                copy.wait()

    rows, width = panel_ref.shape
    step = min(rows, 256)
    for start in range(0, rows, step):
        here = slice(start, start + step)
        value = panel_ref[here, :]
        if "both" in use:
            split_ref[0, 0, here, :], split_ref[0, 1, here, :] = split(value)
        if "flipped" in use:
            high, low = split(value.T)
            use["flipped"][:width, here] = high
            use["flipped"][width:, here] = low
    if "both" in use:
        copy = pltpu.make_async_copy(split_ref, use["both"], sem)
        copy.start()
        copy.wait()


def choose(cases, which, outputs, after=()):
    rows, half = cases[0].shape
    shapes = {"both": (1, 2, rows, 2 * half), "flipped": (4 * half, rows)}
    spaces = {"both": pltpu.HBM, "flipped": pltpu.VMEM}
    return pl.pallas_call(
        functools.partial(choose_kernel, outputs, len(cases)),
        in_specs=[pl.BlockSpec(memory_space=pltpu.SMEM)] + [ANYWHERE] * (len(cases) + len(after)),
        out_specs=[pl.BlockSpec(memory_space=spaces[name]) for name in outputs],
        out_shape=[spaces[name](shapes[name], BF16) for name in outputs],
        scratch_shapes=[
            pltpu.VMEM((rows, 2 * half), F32),
            pltpu.VMEM(shapes["both"], BF16),
            pltpu.SemaphoreType.DMA,
        ],
        compiler_params=params(14),
        cost_estimate=cost(rows * half * 8, rows * half * 24),
        name="choose_panel",
    )(which, *cases, *after)


def products_kernel(block, flipped_ref, both_ref, *refs):
    keep_ref, send_ref, block_ref, sems = refs[-4:]
    half = keep_ref.shape[0]
    rows = block_ref.shape[1] // 2
    copies = []
    for index in range(2):
        here = slice(index * rows, (index + 1) * rows)
        for side in range(2):
            source, target = both_ref.at[block, side, here], block_ref.at[side, here]
            copies.append(pltpu.make_async_copy(source, target, sems.at[index, side]))
            copies[-1].start()
    total = None
    for index in range(2):
        here = slice(index * rows, (index + 1) * rows)
        copies[2 * index].wait()
        with_high = dot(flipped_ref[:, here], block_ref[0, here, :])
        copies[2 * index + 1].wait()
        with_low = dot(flipped_ref[: 2 * half, here], block_ref[1, here, :])
        part = with_high[: 2 * half] + (with_high[2 * half :] + with_low)
        total = part if total is None else total + part
    keep_ref[...] = total[:half]
    send_ref[...] = total[half:]


def products(flipped, both, block, after=()):
    rows, width = both.shape[2:]
    half = flipped.shape[0] // 4
    in_vmem = pl.BlockSpec(memory_space=pltpu.VMEM)
    return pl.pallas_call(
        functools.partial(products_kernel, block),
        in_specs=[in_vmem, IN_HBM] + [ANYWHERE] * len(after),
        out_specs=[in_vmem] * 2,
        out_shape=[jax.ShapeDtypeStruct((half, width), F32)] * 2,
        scratch_shapes=[pltpu.VMEM((2, rows, width), BF16), pltpu.SemaphoreType.DMA((2, 2))],
        compiler_params=params(16),
        cost_estimate=cost(2 * 6 * half * rows * width, rows * width * 4 + 8 * half * rows),
        name="products",
    )(flipped, pinned(both), *after)


def update_kernel(place_ref, *refs):
    sums = refs[:6]
    tfac_ref, gram_ref = refs[6:8]
    panel_refs, x_ref = refs[8:11], refs[11]
    out_ref, done_ref, w_ref, y_ref, y_split_ref = refs[-5:]
    half = sums[0].shape[0]
    width = 2 * half

    @pl.when(pl.program_id(0) == 0)
    def _():
        for index, piece in enumerate(sums):
            start = pl.multiple_of(place_ref[index] * half, half)
            w_ref[pl.ds(start, half), :] = piece[:, : w_ref.shape[1]]
        first = dot_three(tfac_ref[0], w_ref[:width, :])
        y_ref[:width, :] = first
        second = dot_three(tfac_ref[1], w_ref[width : 2 * width, :] - dot_three(gram_ref[0], first))
        y_ref[width : 2 * width, :] = second
        third = w_ref[2 * width :, :] - dot_three(gram_ref[1], first) - dot_three(gram_ref[2], second)
        y_ref[2 * width :, :] = dot_three(tfac_ref[2], third)
        for index in range(6):
            start = pl.multiple_of(place_ref[index] * half, half)
            high, low = split(y_ref[pl.ds(start, half), :])
            for number, value in enumerate((high, high, low)):
                y_split_ref[(6 * number + index) * half : (6 * number + index + 1) * half, :] = value

    sides = [ref[0, side] for side in (0, 1, 0) for ref in panel_refs]
    out_ref[...] = x_ref[...] - dot(jnp.concatenate(sides, axis=1), y_split_ref[...])
    done_ref[...] = jnp.zeros(done_ref.shape, F32)


def update(place, sums, tfac, grams, panels, x, out, block, width):
    rows, columns = x.shape
    half = sums[0].shape[0]
    step = min(rows, 512)
    panel_spec = pl.BlockSpec((1, 2, step, 2 * half), lambda i, place: (0, 0, i, 0))
    block_spec = pl.BlockSpec((step, width), lambda i, place: (i, block))
    operands = [place, *sums, tfac, grams, *map(pinned, panels), x]
    in_specs = (
        [pl.BlockSpec(memory_space=pltpu.VMEM)] * 8
        + [panel_spec] * 3
        + [block_spec]
    )
    aliases = {}
    if out is not None:
        aliases = {len(operands): 0}
        operands.append(out)
        in_specs.append(IN_HBM)
    return pl.pallas_call(
        update_kernel,
        grid_spec=pltpu.PrefetchScalarGridSpec(
            num_scalar_prefetch=1,
            grid=(rows // step,),
            in_specs=in_specs,
            out_specs=[block_spec, pl.BlockSpec((8, 128), lambda i, place: (0, 0))],
            scratch_shapes=[
                pltpu.VMEM((6 * half, width), F32),
                pltpu.VMEM((6 * half, width), F32),
                pltpu.VMEM((18 * half, width), BF16),
            ],
        ),
        out_shape=[jax.ShapeDtypeStruct(x.shape, F32), jax.ShapeDtypeStruct((8, 128), F32)],
        input_output_aliases=aliases,
        compiler_params=params(40),
        cost_estimate=cost(2 * 18 * half * rows * width, rows * width * 8 + rows * half * 24),
        name="update",
    )(*operands)


def pairs_of(count, step):
    return [(index, index ^ step) for index in range(count)]


def swap_cores(value):
    return lax.ppermute(value, "row", pairs_of(lax.axis_size("row"), 1))


def both_cores(chip_pairs):
    return [(2 * a + core, 2 * b + core) for a, b in chip_pairs for core in range(2)]


def sum_over_rows(keep, send):
    chips = lax.axis_size("row") // 2
    chip = lax.axis_index("row") // 2
    total = keep + swap_cores(send)
    for hop in range(chips // 2 - 1):
        pairs = [(hop, hop + 1), (chips - 1 - hop, chips - 2 - hop)]
        total = total + lax.ppermute(total, "row", both_cores(pairs))
    middle = [(chips // 2 - 1, chips // 2), (chips // 2, chips // 2 - 1)]
    total = total + lax.ppermute(total, "row", both_cores(middle))
    for hop in reversed(range(chips // 2 - 1)):
        pairs = [(hop + 1, hop), (chips - 2 - hop, chips - 1 - hop)]
        arrived = lax.ppermute(total, "row", both_cores(pairs))
        total = jnp.where((chip == hop) | (chip == chips - 1 - hop), arrived, total)
    return total, swap_cores(total)


def pick(index, *cases):
    return lax.select_n(index, *cases)


def fetch_square(slot, roots):
    half = slot.shape[1] // 2
    me = lax.axis_index("col")
    along = lambda value, step: lax.ppermute(value, "col", pairs_of(4, step))
    own = [slot[:, :half], slot[:, half:]]
    near, far = [], []
    for piece in own:
        near.append(along(piece, 1))
        far.append(along(piece, 2))
    cross = [along(far[0], 1), along(near[1], 2)]
    spare = (roots[0] + 3) % 4
    case = me ^ spare
    rounds = [
        ((*own, near[0], far[0]), jnp.array([[2, 3], [0, 1], [0, 1], [0, 1]], jnp.int32)[case]),
        ((*near, *far), jnp.array([[1, 3], [2, 3], [0, 1], [0, 2]], jnp.int32)[case]),
        ((*cross, near[1], far[1]), jnp.array([[0, 1], [0, 1], [0, 1], [2, 3]], jnp.int32)[case]),
    ]
    slots = jnp.array([[1, 2, 1, 2, 3, 3], [0, 0, 2, 2, 3, 3], [0, 0, 1, 1, 3, 3], [0, 0, 1, 2, 1, 2]], jnp.int32)
    halves = jnp.array([[0, 0, 1, 1, 0, 1], [0, 1, 0, 1, 0, 1], [0, 1, 0, 1, 0, 1], [0, 1, 0, 0, 1, 1]], jnp.int32)
    panel = ((slots[case] ^ me) - roots[0]) % 4
    places = panel * 2 + halves[case]
    later_of = jnp.array([[0, 1, 0, 0], [1, 0, 2, 2]], jnp.int32)[roots[0] - 2, me]
    earlier_of = jnp.array([[2, 2, 0, 1], [0, 0, 1, 0]], jnp.int32)[roots[0] - 2, me]
    both = jnp.arange(2, dtype=jnp.int32)
    later = ((*own, *near, *far), 2 * later_of + both)
    earlier = ((*own, *near, *far), 2 * earlier_of + both)
    holders = jnp.array([[3, 0, 1], [2, 3, 0]], jnp.int32)[roots[0] - 2]
    return rounds, places, later, earlier, holders


def fetch_any(slot, roots):
    half = slot.shape[1] // 2
    me = lax.axis_index("col")
    panels = [lax.psum(jnp.where(me == roots[index], slot, jnp.zeros_like(slot)), "col") for index in range(PANELS)]
    rounds = [(panel[:, :half], panel[:, half:]) for panel in panels]
    return rounds, jnp.arange(2 * PANELS, dtype=jnp.int32), panels


def gram(left, right):
    return lax.dot_general(
        left, right, (((0,), (0,)), ((), ())), precision=lax.Precision.HIGH, preferred_element_type=F32
    )


def exchange_kernel(names, pieces, ends_ref, *refs):
    use = dict(zip(names, refs))
    end = ends_ref[0] == 1
    if "acc" in use:
        start = 0
        for index in range(pieces):
            keep, swapped = use["keep", index], use["swapped", index]
            columns = slice(start, start + keep.shape[1])
            use["acc"][:, columns] = keep[...] + swapped[...]
            start = columns.stop
    if "part" in use:
        columns = use["part"].shape[1]
        use["part"][...] = use["acc_before"][...] + use["outer"][:, :columns]
    if "total" in use:
        use["total"][...] = use["part_before"][...] + use["inner"][...]
    if "final" in use:
        columns = use["final"].shape[1]
        use["final"][...] = jnp.where(end, use["outer"][:, :columns], use["total_before"][...])
    if "out" in use:
        sources = [use[name] for name in ("acc", "total") if name in use]
        if len(sources) == 1:
            use["out"][...] = sources[0][...]
        else:
            both = min(source.shape[1] for source in sources)
            use["out"][:, :both] = jnp.where(end, sources[0][:, :both], sources[1][:, :both])
            for source in sources:
                if source.shape[1] > both:
                    use["out"][:, both:] = source[:, both:]


def exchange(ends, operands, shapes, after):
    names = list(operands) + [None] * len(after) + list(shapes)
    pieces = sum(name[0] == "keep" for name in operands)
    in_vmem = pl.BlockSpec(memory_space=pltpu.VMEM)
    results = pl.pallas_call(
        functools.partial(exchange_kernel, names, pieces),
        in_specs=[pl.BlockSpec(memory_space=pltpu.SMEM)] + [in_vmem] * len(operands)
        + [ANYWHERE] * len(after),
        out_specs=[in_vmem] * len(shapes),
        out_shape=[jax.ShapeDtypeStruct(shape, F32) for shape in shapes.values()],
        compiler_params=params(14),
        cost_estimate=cost(0, 0),
        name="exchange",
    )(ends, *operands.values(), *after)
    return dict(zip(shapes, results))


def shards_square(eigvec, slot, roots, tfac):
    columns = eigvec.shape[1]
    width, half = columns // 2, slot.shape[1] // 2
    rounds, places, later, earlier, holders = fetch_square(slot, roots)
    chip, core = lax.axis_index("row") // 2, lax.axis_index("row") % 2
    ends = jnp.where((chip == 0) | (chip == 3), 1, 0).astype(jnp.int32).reshape(1)
    places = jnp.where(core == 0, places, places.reshape(PANELS, 2)[:, ::-1].reshape(-1))
    ordered = lambda pair: jnp.where(core == 0, pair, pair[::-1])
    x_both = split_array(eigvec, PIECE)
    chunks = [(index, block) for index in range(PANELS) for block in range(columns // width)]
    count = len(chunks)
    gram_chunk = 2
    prepared, arrived, sizes, gram_sides = {}, {}, {}, []

    def start(number, after):
        index, block = chunks[number]
        pieces = []
        if index not in prepared:
            cases, which = rounds[index]
            prepared[index] = choose(cases, ordered(which), ("both", "flipped"), after)
        for part in range(width // PIECE):
            pieces.append(products(prepared[index][1], x_both, block * (width // PIECE) + part, after))
        if number == gram_chunk - 1:
            gram_sides.append(choose(later[0], ordered(later[1]), ("flipped",), after)[0])
            gram_sides.append(choose(*earlier, ("both",), after)[0])
        if number == gram_chunk:
            pieces.append(products(*gram_sides, 0, after))
        arrived[number] = [(mine, swap_cores(other)) for mine, other in pieces]
        sizes[number] = (half, sum(mine.shape[1] for mine, other in pieces))

    outer_pairs = both_cores([(0, 1), (1, 0), (2, 3), (3, 2)])
    inner_pairs = both_cores([(1, 2), (2, 1)])
    acc, part, total, outer, inner, sums = {}, {}, {}, {}, {}, {}
    grams, out = None, None
    start(0, ())
    for step in range(count + 3 * LAG):
        operands, shapes = {}, {}
        inward, middle, outward = step - LAG, step - 2 * LAG, step - 3 * LAG
        if step < count:
            for number, (mine, other) in enumerate(arrived[step]):
                operands["keep", number], operands["swapped", number] = mine, other
            shapes["acc"] = sizes[step]
        if step - LAG in outer:
            operands["outer"] = outer[step - LAG]
        if 0 <= inward < count:
            operands["acc_before"] = acc[inward]
            shapes["part"] = sizes[inward]
        if 0 <= middle < count:
            operands["part_before"], operands["inner"] = part[middle], inner[step - LAG]
            shapes["total"] = sizes[middle]
        if 0 <= outward < count:
            operands["total_before"] = total[outward]
            shapes["final"] = sizes[outward]
        sent = [shapes[name] for name in ("acc", "total") if name in shapes]
        if sent:
            shapes["out"] = max(sent, key=lambda shape: shape[1])
        ahead = [] if out is None else [finished]
        if step + 1 == chunks.index((PANELS - 1, 0)):
            ahead.extend(rounds[-1][0][:2])
        if step == gram_chunk - 1:
            ahead.extend([gram_sides[0], pinned(gram_sides[1])])
        if step == count + 1:
            ahead.append(grams)
        if 0 <= outward - 1 < count - 2:
            ahead.append(sums[chunks[outward - 1]][1])
        results = exchange(ends, operands, shapes, ahead)
        if "out" in results:
            outer[step] = lax.ppermute(results["out"], "row", outer_pairs)
        if "acc" in results:
            acc[step] = results["acc"]
        if "part" in results:
            part[inward] = results["part"]
            inner[step] = lax.ppermute(results["part"], "row", inner_pairs)
        if "total" in results:
            total[middle] = results["total"]
        if step + 1 < count:
            start(step + 1, [next(iter(results.values()))])
        if "final" in results:
            done = outward
            own, other = results["final"], swap_cores(results["final"])
            if done == gram_chunk:
                pair = own[:, width:], other[:, width:]
                block = jnp.where(core == 0, jnp.concatenate(pair, axis=0), jnp.concatenate(pair[::-1], axis=0))
                spread = [block] + [lax.ppermute(block, "col", pairs_of(4, shift)) for shift in range(1, 4)]
                places_of = holders ^ lax.axis_index("col")
                grams = jnp.stack([pick(places_of[number], *spread) for number in range(PANELS)])
            sums[chunks[done]] = (own, other)
            index, block = chunks[done]
            if index == PANELS - 1:
                pieces = [piece for panel in range(PANELS) for piece in sums[panel, block]]
                panels = [prepared[panel][0] for panel in range(PANELS)]
                out, finished = update(places, pieces, tfac, grams, panels, eigvec, out, block, width)
    return out


def shards(eigvec, slots, roots, tfac):
    if lax.axis_size("col") == 4 and lax.axis_size("row") == 8:
        return shards_square(eigvec, slots[0], roots, tfac)
    columns = eigvec.shape[1]
    width = min(columns, BLOCK)
    rounds, places, panels = fetch_any(slots[0], roots)
    core = lax.axis_index("row") % 2
    places = jnp.where(core == 0, places, places.reshape(PANELS, 2)[:, ::-1].reshape(-1))
    x_both = split_array(eigvec, width)
    prepared, sums = [], []
    for pair in rounds:
        which = jnp.where(core == 0, jnp.arange(2), jnp.arange(1, -1, -1)).astype(jnp.int32)
        prepared.append(choose(pair, which, ("both", "flipped")))
        sums.append([
            sum_over_rows(*products(prepared[-1][1], x_both, block)) for block in range(columns // width)
        ])
    grams = jnp.stack([gram(panels[1], panels[0]), gram(panels[2], panels[0]), gram(panels[2], panels[1])])
    grams = lax.psum(grams, "row")
    out = None
    for block in range(columns // width):
        pieces = [piece for index in range(PANELS) for piece in sums[index][block]]
        out, _ = update(places, pieces, tfac, grams, [both for both, _ in prepared], eigvec, out, block, width)
    return out


def solution(mesh):
    in_specs = (P("row", "col"), P("col", "row", None), P(), P())
    out_specs = P("row", "col")
    return jax.shard_map(shards, mesh=mesh, in_specs=in_specs, out_specs=out_specs, check_vma=False)
```
